32 devices in a mesh: groups: 2 (over x), gx: 16 (over z, y, core).
Axes of the slice: x: 2, y: 2, z: 4, core: 2. Of those that a mesh axis runs over, the one named last changes fastest.
Arguments:
- u_prev: float32 [256, 256, 256], P(('groups', 'gx')), parts along dimension 0, may hold values from -7 to 7
- u_cur: float32 [256, 256, 256], P(('groups', 'gx')), parts along dimension 0, may hold values from -7 to 7
- courant_sq: float32 [256, 256, 256], P(('groups', 'gx')), parts along dimension 0, may hold values from 0.1 to 0.33
- patch_map: int32 [256, 4, 256], P(('groups', 'gx')), parts along dimension 0, may hold values from 0 to 159
- absorb: float32 [320], P('groups'), parts along dimension 0, may hold values from 0.05 to 1
- checkpoint: int32 [2], P('groups'), parts along dimension 0, may hold values from 0 to 60
- target_curve: float32 [128], P('groups'), parts along dimension 0, may hold values from 0 to 2.5
- tail_energy: float32 [2], P('groups'), parts along dimension 0, may hold values from 0.5 to 4
Outputs:
- grad_prev: float32 [256, 256, 256], P(('groups', 'gx')), parts along dimension 0
- grad_cur: float32 [256, 256, 256], P(('groups', 'gx')), parts along dimension 0
- grad_absorb: float32 [320], P(('groups', 'gx')), parts along dimension 0
The draws below stay inside these ranges and needn't reach their ends.
There are 2 independent parts, one for each index of `groups`. The reference program is written for one: setup_inputs(seed, part) draws one part's arguments, and reference() takes and returns one part's arrays. A program takes and returns all parts, laid end to end along the dimension named above; each array names one. Nothing has to cross between parts.
All inputs are finite; a program needn't handle non-finite values.
Results may differ from the reference program's by a relative error of at most 0.00002.
Values sent between devices are 32-bit elements; how exact they have to be, the bound alone decides.
No kernel may reach another device: no remote copies, remote signals or barrier semaphores. Data moves between devices by JAX's collectives and lax.ppermute only.
A program may use at most 128 MiB of HBM per device.

```python
import math
import jax
import jax.numpy as jnp
from jax import lax

CX = 8
SIDE = 256
STEPS = 4
HISTORY = 64
NX = 128
PATCHES = 160
PATCH_CELLS = 819
CELLS = 8388608


def brick_loudness(key):
    bricks = NX // CX
    phase = jax.random.randint(jax.random.fold_in(key, 5), (), 0, 2)
    strength = jax.random.uniform(jax.random.fold_in(key, 6), (bricks,), jnp.float32, 0.7, 1.0)
    parity = (jnp.arange(bricks, dtype=jnp.int32) + phase) % 2
    signed = 2.0 * parity.astype(jnp.float32) - 1.0
    loudness = jnp.exp(signed * strength)
    return jnp.repeat(loudness, CX, total_repeat_length=NX)[:, None, None]


def ramped_field(key, constant):
    subkey = jax.random.fold_in(key, constant)
    position = jnp.arange(NX, dtype=jnp.float32) / float(NX - 1)
    profile = (1.0 + 0.75 * position)[:, None, None]
    noise = jnp.clip(jax.random.normal(subkey, (NX, SIDE, SIDE), jnp.float32), -4.0, 4.0)
    return jnp.clip(noise * profile * brick_loudness(key), -7.0, 7.0)


def draw_u_prev(key, part):
    return ramped_field(key, 11)


def draw_u_cur(key, part):
    return ramped_field(key, 23)


def draw_courant_sq(key, part):
    subkey = jax.random.fold_in(key, 31)
    level = jax.random.randint(subkey, (NX, SIDE, SIDE), 0, 20)
    high = (level < 17).astype(jnp.float32)
    return 0.1 + 0.23 * high


def touch_ends(values, key, least, largest):
    dims = values.shape
    spot = [jax.random.randint(jax.random.fold_in(key, axis), (), 0, dims[axis]) for axis in range(len(dims))]
    values = values.at[tuple(spot)].set(least)
    longest = dims.index(max(dims))
    spot[longest] = (spot[longest] + 1) % dims[longest]
    return values.at[tuple(spot)].set(largest)


def setup_inputs(seed: int = 0, part: int = 0) -> dict:
    key_of = jax.random.split(jax.random.key(seed), 9)
    own_keys = jax.random.split(jax.random.fold_in(key_of[8], part), 9)
    return {
        "u_prev": draw_u_prev(jax.random.fold_in(jax.random.fold_in(key_of[8], part), 71), part),
        "u_cur": draw_u_cur(jax.random.fold_in(jax.random.fold_in(key_of[8], part), 71), part),
        "courant_sq": draw_courant_sq(jax.random.fold_in(jax.random.fold_in(key_of[8], part), 71), part),
        "patch_map": touch_ends(jax.random.randint(own_keys[3], (NX, 4, SIDE), 0, PATCHES), jax.random.fold_in(own_keys[3], 1), 0, PATCHES - 1).astype(jnp.int32),
        "absorb": jnp.clip(jnp.exp(jax.random.uniform(own_keys[4], (PATCHES,), jnp.float32, math.log(0.05), math.log(1.0))), 0.05, 1.0),
        "checkpoint": jax.random.randint(own_keys[5], (1,), 0, HISTORY - STEPS + 1).astype(jnp.int32),
        "target_curve": jnp.clip(jax.random.uniform(own_keys[6], (HISTORY,), jnp.float32, 0.0, 2.5), 0.0, 2.5),
        "tail_energy": jnp.clip(jax.random.uniform(own_keys[7], (1,), jnp.float32, 0.5, 4.0), 0.5, 4.0),
    }


def neighbours(field):
    full = jnp.pad(field, 1)
    total = full[2:, 1:-1, 1:-1] + full[:-2, 1:-1, 1:-1]
    total = total + full[1:-1, 2:, 1:-1] + full[1:-1, :-2, 1:-1]
    return total + full[1:-1, 1:-1, 2:] + full[1:-1, 1:-1, :-2]


def spread_faces(faces, side_cells):
    damping = jnp.zeros((faces.shape[0], side_cells, side_cells), jnp.float32)
    damping = damping.at[:, 0, :].add(faces[:, 0])
    damping = damping.at[:, -1, :].add(faces[:, 1])
    damping = damping.at[:, :, 0].add(faces[:, 2])
    return damping.at[:, :, -1].add(faces[:, 3])


def collect_faces(field):
    return jnp.stack([field[:, 0, :], field[:, -1, :], field[:, :, 0], field[:, :, -1]], axis=1)


def reference(u_prev, u_cur, courant_sq, patch_map, absorb, checkpoint, target_curve, tail_energy):
    damping = spread_faces(absorb[patch_map], SIDE)
    states = [u_prev, u_cur]
    for turn_index in range(STEPS):
        prior, now = states[-2], states[-1]
        states.append((2.0 * now - (1.0 - damping) * prior + courant_sq * (neighbours(now) - 6.0 * now)) / (1.0 + damping))
    energy = jnp.stack([jnp.sum(field * field) for field in states[2:]]) / float(CELLS)
    targets = lax.dynamic_slice_in_dim(target_curve, checkpoint[0], STEPS)
    schroeder = tail_energy[0] + jnp.cumsum(energy[::-1])[::-1]
    slopes = 2.0 * (jnp.log(schroeder) - targets) / schroeder
    weights = jnp.cumsum(slopes)
    inverse_gain = 1.0 / (1.0 + damping)
    retain = 1.0 - damping
    adjoint = 2.0 * weights[STEPS - 1] * states[STEPS + 1]
    w_later = jnp.zeros_like(u_cur)
    grad_damp = jnp.zeros_like(u_cur)
    for back_index in range(STEPS, 0, -1):
        weighted = inverse_gain * adjoint
        grad_damp = grad_damp + weighted * (states[back_index - 1] - states[back_index + 1])
        product = courant_sq * weighted
        fresh = 2.0 * weighted + neighbours(product) - 6.0 * product - retain * w_later
        if back_index > 1:
            fresh = fresh + 2.0 * weights[back_index - 2] * states[back_index]
        w_later = weighted
        adjoint = fresh
    grad_prev = -retain * w_later
    summed = jax.ops.segment_sum(collect_faces(grad_damp).reshape(-1), patch_map.reshape(-1), PATCHES)
    return grad_prev, adjoint, summed / float(PATCH_CELLS)
```

```python
import functools

import jax
import jax.numpy as jnp
from jax import lax
from jax.experimental import pallas as pl
from jax.experimental.pallas import tpu as pltpu
from jax.sharding import PartitionSpec as P

STEPS = 4
PATCH_CELLS = 819
CHUNK = 32
LANES = 128
F32 = jnp.float32
VMEM = pltpu.VMEM
in_vmem = pl.BlockSpec(memory_space=pltpu.VMEM)
in_smem = pl.BlockSpec(memory_space=pltpu.SMEM)
in_hbm = pl.BlockSpec(memory_space=pltpu.HBM)


def end_layer(parity, side, depth, cx):
    high = 1 - parity if side == 0 else parity
    return high * (cx - 1 - depth) + (1 - high) * depth


def layer(ref, x):
    return lambda row, count: ref[x, pl.ds(row, count), :]


def flat(ref, base):
    return lambda row, count: ref[pl.ds(base + row, count), :]


def chunks(side_cells):
    return [(row, CHUNK) for row in range(0, side_cells, CHUNK)]


def beside(field, row, count, side_cells):
    v = field(row, count)
    sub = lax.broadcasted_iota(jnp.int32, v.shape, 0)
    lane = lax.broadcasted_iota(jnp.int32, v.shape, 1)
    if row == 0:
        above = jnp.where(sub == 0, 0.0, pltpu.roll(v, 1, 0))
    else:
        above = field(row - 1, count)
    if row + count == side_cells:
        below = jnp.where(sub == count - 1, 0.0, pltpu.roll(v, count - 1, 0))
    else:
        below = field(row + 1, count)
    left = jnp.where(lane == 0, 0.0, pltpu.roll(v, 1, 1))
    right = jnp.where(lane == v.shape[1] - 1, 0.0, pltpu.roll(v, v.shape[1] - 1, 1))
    return v, (above + below) + (left + right)


def forward(now, prior, courant, inverse, sides, row, count, side_cells):
    v, total = beside(now, row, count, side_cells)
    for other in sides:
        total = total + other(row, count)
    p = prior(row, count)
    c, i = courant(row, count), inverse(row, count)
    return i * (2.0 * (v - p) + c * (total - 6.0 * v)) + p


def backward(product, w, later, inverse, source, sides, row, count, side_cells):
    q, total = beside(product, row, count, side_cells)
    for other in sides:
        total = total + other(row, count)
    fresh = total - 6.0 * q + source
    i = inverse(row, count)
    if later is None:
        return i * (2.0 * w + fresh)
    return i * (2.0 * (w - later) + fresh) + later


def sweep(low, high, body):
    def turn(x, carry):
        body(x)
        return carry

    lax.fori_loop(low, high, turn, 0)


def x_sides(ref, x, cx):
    return [layer(ref, k) for k in (x - 1, x + 1) if not isinstance(k, int) or 0 <= k < cx]


def fold(values):
    total = values[0:8]
    for row in range(8, values.shape[0], 8):
        total = total + values[row : row + 8]
    return total


def start_kernel(parity_ref, u_hbm, a_ref, b_ref, sems):
    cx = u_hbm.shape[0]
    copies = []
    for side, out in enumerate((a_ref, b_ref)):
        x = end_layer(parity_ref[0], side, 0, cx)
        copies.append(pltpu.make_async_copy(u_hbm.at[x], out, sems.at[side]))
    for copy in copies:
        copy.start()
    for copy in copies:
        copy.wait()


def lookup(maps, absorb_ref):
    def turn(p, got):
        return jnp.where(maps == p, absorb_ref[p], got)

    return lax.fori_loop(0, absorb_ref.shape[0], turn, jnp.zeros(maps.shape, F32))


def put_column(acc_ref, spot, tile, lane_from):
    side_cells = acc_ref.shape[0]
    for row, count in chunks(side_cells):
        values = pltpu.roll(tile(row, count), (spot - lane_from) % LANES, 1)
        lane = lax.broadcasted_iota(jnp.int32, values.shape, 1)
        acc_ref[pl.ds(row, count), :] = jnp.where(
            lane == spot, values, acc_ref[pl.ds(row, count), :]
        )


def low_tile(field):
    return lambda row, count: field(row, count)[:, :LANES]


def high_tile(field):
    return lambda row, count: field(row, count)[:, -LANES:]


def setup_kernel(
    parity_ref, absorb_ref, map_ref, u_hbm, up_hbm, c_hbm,
    u, up, c, s, inv, pay_a, pay_b,
    maps, found, turned, columns, sems,
):
    cx, side_cells = u.shape[0], u.shape[1]
    copies = [
        pltpu.make_async_copy(src, dst, sems.at[k])
        for k, (src, dst) in enumerate(((u_hbm, u), (up_hbm, up), (c_hbm, c)))
    ]
    for copy in copies:
        copy.start()
    for x in range(cx):
        maps[4 * x : 4 * x + 4, :] = map_ref[x]
    found[...] = lookup(maps[...], absorb_ref)
    turned[...] = jnp.zeros_like(turned)
    for x in range(cx):
        turned[x : x + 1, :] = found[4 * x + 2 : 4 * x + 3, :]
        turned[cx + x : cx + x + 1, :] = found[4 * x + 3 : 4 * x + 4, :]
    columns[...] = jnp.transpose(turned[...])

    def spread(x, carry):
        for row, count in chunks(side_cells):
            tile = columns[pl.ds(row, count), :]
            lane = lax.broadcasted_iota(jnp.int32, tile.shape, 1)
            near = jnp.where(lane == 0, pltpu.roll(tile, lax.rem(LANES - x, LANES), 1), 0.0)
            far = jnp.where(lane == LANES - 1, pltpu.roll(tile, LANES - 1 - cx - x, 1), 0.0)
            mid = [jnp.zeros_like(near)] * (side_cells // LANES - 2)
            field = jnp.concatenate([near, *mid, far], axis=1)
            sub = lax.broadcasted_iota(jnp.int32, field.shape, 0)
            if row == 0:
                field = field + jnp.where(sub == 0, found[pl.ds(4 * x, 1), :], 0.0)
            if row + count == side_cells:
                field = field + jnp.where(sub == count - 1, found[pl.ds(4 * x + 1, 1), :], 0.0)
            s[x, pl.ds(row, count), :] = field
            inv[x, pl.ds(row, count), :] = 1.0 / (1.0 + field)
        return carry

    lax.fori_loop(0, cx, spread, 0)
    for copy in copies:
        copy.wait()
    columns[...] = jnp.zeros_like(columns)
    for side, pay in enumerate((pay_a, pay_b)):
        x0 = end_layer(parity_ref[0], side, 0, cx)
        x1 = end_layer(parity_ref[0], side, 1, cx)
        for row, count in chunks(side_cells):
            pay[pl.ds(row, count), :] = forward(
                layer(u, x0), layer(up, x0), layer(c, x0), layer(inv, x0), [layer(u, x1)],
                row, count, side_cells,
            )
            pay[pl.ds(side_cells + row, count), :] = (
                c[x0, pl.ds(row, count), :] * inv[x0, pl.ds(row, count), :]
            )
        put_column(columns, 2 * side, low_tile(layer(up, x0)), 0)
        put_column(columns, 2 * side + 1, high_tile(layer(up, x0)), LANES - 1)
    rows = jnp.transpose(columns[...])
    for side, pay in enumerate((pay_a, pay_b)):
        x0 = end_layer(parity_ref[0], side, 0, cx)
        base = 2 * side_cells
        pay[base : base + 1, :] = up[x0, 0:1, :]
        pay[base + 1 : base + 2, :] = up[x0, side_cells - 1 : side_cells, :]
        pay[base + 2 : base + 4, :] = rows[2 * side : 2 * side + 2, :]
        pay[base + 4 : base + 8, :] = map_ref[x0].astype(F32)


def ahead_kernel(u, up, c, inv, u1, u2):
    cx, side_cells = u.shape[0], u.shape[1]

    def first(x):
        for row, count in chunks(side_cells):
            u1[x, pl.ds(row, count), :] = forward(
                layer(u, x), layer(up, x), layer(c, x), layer(inv, x), x_sides(u, x, cx),
                row, count, side_cells,
            )

    def second(x):
        for row, count in chunks(side_cells):
            u2[x, pl.ds(row, count), :] = forward(
                layer(u1, x), layer(u, x), layer(c, x), layer(inv, x), x_sides(u1, x, cx),
                row, count, side_cells,
            )

    first(0)
    sweep(1, cx - 1, first)
    first(cx - 1)
    sweep(2, cx - 2, second)


def finish_step(x0, now, fresh, c, inv, got_now, got_part, got_b, halo, side_cells):
    for row, count in chunks(side_cells):
        b = c[x0, pl.ds(row, count), :] * inv[x0, pl.ds(row, count), :]
        fresh[x0, pl.ds(row, count), :] += b * got_now(row, count)
        halo[pl.ds(row, count), :] = got_part(row, count) + got_b(row, count) * now[
            x0, pl.ds(row, count), :
        ]


def join_first_kernel(
    parity_ref, u, c, inv, near_a, near_b, got_a, got_b, u1_in, u2_in,
    u1, u2, halo_a, halo_b, pay_a, pay_b,
):
    cx, side_cells = u.shape[0], u.shape[1]
    for side, (near, got, halo, pay) in enumerate(
        ((near_a, got_a, halo_a, pay_a), (near_b, got_b, halo_b, pay_b))
    ):
        x0, x1, x2 = (end_layer(parity_ref[0], side, k, cx) for k in range(3))
        finish_step(
            x0, u, u1, c, inv, flat(near, 0), flat(got, 0), flat(got, side_cells), halo, side_cells
        )
        for row, count in chunks(side_cells):
            value = forward(
                layer(u1, x0), layer(u, x0), layer(c, x0), layer(inv, x0),
                [layer(u1, x1), flat(halo, 0)], row, count, side_cells,
            )
            u2[x0, pl.ds(row, count), :] = value
            pay[pl.ds(row, count), :] = value
            u2[x1, pl.ds(row, count), :] = forward(
                layer(u1, x1), layer(u, x1), layer(c, x1), layer(inv, x1),
                [layer(u1, x0), layer(u1, x2)], row, count, side_cells,
            )
        for row, count in chunks(side_cells):
            pay[pl.ds(side_cells + row, count), :] = forward(
                layer(u2, x0), layer(u1, x0), layer(c, x0), layer(inv, x0), [layer(u2, x1)],
                row, count, side_cells,
            )


def ahead_again_kernel(u1, u2, c, inv, u3, u4, energy):
    cx, side_cells = u1.shape[0], u1.shape[1]
    energy[...] = jnp.zeros_like(energy)

    def first(x, inner):
        for row, count in chunks(side_cells):
            value = forward(
                layer(u2, x), layer(u1, x), layer(c, x), layer(inv, x), x_sides(u2, x, cx),
                row, count, side_cells,
            )
            u3[x, pl.ds(row, count), :] = value
            energy[0] += fold(u1[x, pl.ds(row, count), :] ** 2)
            energy[1] += fold(u2[x, pl.ds(row, count), :] ** 2)
            if inner:
                energy[2] += fold(value * value)

    def second(x):
        for row, count in chunks(side_cells):
            value = forward(
                layer(u3, x), layer(u2, x), layer(c, x), layer(inv, x), x_sides(u3, x, cx),
                row, count, side_cells,
            )
            u4[x, pl.ds(row, count), :] = value
            energy[3] += fold(value * value)

    first(0, False)
    sweep(1, cx - 1, lambda x: first(x, True))
    first(cx - 1, False)
    sweep(2, cx - 2, second)


def join_second_kernel(
    parity_ref, u2, c, inv, energy_in, got_a, got_b, b_a, b_b, u3_in, u4_in,
    u3, u4, halo_a, halo_b, pay_a, pay_b, energy_rows, energy,
):
    cx, side_cells = u2.shape[0], u2.shape[1]
    energy[...] = energy_in[...]
    for side, (got, b, halo, pay) in enumerate(
        ((got_a, b_a, halo_a, pay_a), (got_b, b_b, halo_b, pay_b))
    ):
        x0, x1, x2 = (end_layer(parity_ref[0], side, k, cx) for k in range(3))
        finish_step(
            x0, u2, u3, c, inv, flat(got, 0), flat(got, side_cells), flat(b, side_cells), halo,
            side_cells,
        )
        for row, count in chunks(side_cells):
            energy[2] += fold(u3[x0, pl.ds(row, count), :] ** 2)
            value = forward(
                layer(u3, x0), layer(u2, x0), layer(c, x0), layer(inv, x0),
                [layer(u3, x1), flat(halo, 0)], row, count, side_cells,
            )
            u4[x0, pl.ds(row, count), :] = value
            pay[pl.ds(row, count), :] = (
                2.0 * c[x0, pl.ds(row, count), :] * inv[x0, pl.ds(row, count), :] * value
            )
            other = forward(
                layer(u3, x1), layer(u2, x1), layer(c, x1), layer(inv, x1),
                [layer(u3, x0), layer(u3, x2)], row, count, side_cells,
            )
            u4[x1, pl.ds(row, count), :] = other
            energy[3] += fold(value * value + other * other)

        def inner(row, count):
            at = pl.ds(row, count)
            return 2.0 * c[x1, at, :] * inv[x1, at, :] * u4[x1, at, :]

        for row, count in chunks(side_cells):
            at = pl.ds(row, count)
            w = 2.0 * inv[x0, at, :] * u4[x0, at, :]
            part = backward(
                flat(pay, 0), w, None, layer(inv, x0), 0.0, [inner], row, count, side_cells
            )
            pay[pl.ds(side_cells + row, count), :] = c[x0, at, :] * part
    lane = lax.broadcasted_iota(jnp.int32, energy_rows.shape, 1)
    rows = jnp.zeros(energy_rows.shape, F32)
    for n in range(STEPS):
        total = jnp.sum(jnp.sum(energy[n], axis=0, keepdims=True), axis=1, keepdims=True)
        rows = jnp.where(lane == n, total, rows)
    energy_rows[...] = rows


def adjoint_kernel(
    all_cells, checkpoint_ref, target_ref, tail_ref, sums, u2, u3, u4, c, inv,
    weights, w3, q3, w2, q2, q4,
):
    cx, side_cells = u2.shape[0], u2.shape[1]
    totals = jnp.sum(sums[...], axis=0, keepdims=True) / all_cells
    lane = lax.broadcasted_iota(jnp.int32, totals.shape, 1)
    start = jnp.clip(checkpoint_ref[0], 0, target_ref.shape[0] - STEPS)
    weight = jnp.zeros((1, 1), F32)
    g = []
    for n in range(STEPS):
        rest = jnp.where(jnp.logical_and(lane >= n, lane < STEPS), totals, 0.0)
        schroeder = tail_ref[0] + jnp.sum(rest, axis=1, keepdims=True)
        weight = weight + 2.0 * (jnp.log(schroeder) - target_ref[start + n]) / schroeder
        g.append(weight)
        weights[n : n + 1, :] = jnp.broadcast_to(weight, (1, LANES))
    twice = [2.0 * one for one in g]

    def zeroth(x):
        for row, count in chunks(side_cells):
            at = pl.ds(row, count)
            q4[x, at, :] = (twice[3] * c[x, at, :]) * (inv[x, at, :] * u4[x, at, :])

    def first(x):
        for row, count in chunks(side_cells):
            at = pl.ds(row, count)
            w = twice[3] * (inv[x, at, :] * u4[x, at, :])
            value = backward(
                layer(q4, x), w, None, layer(inv, x), twice[2] * u3[x, at, :],
                x_sides(q4, x, cx), row, count, side_cells,
            )
            w3[x, at, :] = value
            q3[x, at, :] = c[x, at, :] * value

    def second(x):
        for row, count in chunks(side_cells):
            at = pl.ds(row, count)
            later = twice[3] * (inv[x, at, :] * u4[x, at, :])
            value = backward(
                layer(q3, x), w3[x, at, :], later, layer(inv, x), twice[1] * u2[x, at, :],
                x_sides(q3, x, cx), row, count, side_cells,
            )
            w2[x, at, :] = value
            q2[x, at, :] = c[x, at, :] * value

    sweep(0, cx, zeroth)
    first(0)
    sweep(1, cx - 1, first)
    first(cx - 1)
    sweep(2, cx - 2, second)


def join_third_kernel(
    parity_ref, weights, u1, u2, u4, c, inv, u3h_a, u3h_b, got_a, got_b, b_a, b_b,
    w3_in, q3_in, w2_in, q2_in,
    w3, q3, w2, q2, pay_a, pay_b, halo,
):
    cx, side_cells = u2.shape[0], u2.shape[1]
    g = [weights[n : n + 1, 0:1] for n in range(STEPS)]
    for side, (u3h, got, b, pay) in enumerate(
        ((u3h_a, got_a, b_a, pay_a), (u3h_b, got_b, b_b, pay_b))
    ):
        x0, x1, x2 = (end_layer(parity_ref[0], side, k, cx) for k in range(3))
        for row, count in chunks(side_cells):
            at = pl.ds(row, count)
            i, cc = inv[x0, at, :], c[x0, at, :]
            value = w3[x0, at, :] + g[3] * (i * got[at, :])
            w3[x0, at, :] = value
            q3[x0, at, :] = cc * value
            own = 2.0 * cc * i * u4[x0, at, :]
            bh = b[pl.ds(side_cells + row, count), :]
            halo[at, :] = g[3] * (got[pl.ds(side_cells + row, count), :] + bh * own) + (
                2.0 * g[2]
            ) * (bh * u3h[at, :])
        for x, others in ((x0, [layer(q3, x1), flat(halo, 0)]), (x1, [layer(q3, x0), layer(q3, x2)])):
            for row, count in chunks(side_cells):
                at = pl.ds(row, count)
                later = (2.0 * g[3]) * (inv[x, at, :] * u4[x, at, :])
                value = backward(
                    layer(q3, x), w3[x, at, :], later, layer(inv, x),
                    (2.0 * g[1]) * u2[x, at, :], others, row, count, side_cells,
                )
                w2[x, at, :] = value
                q2[x, at, :] = c[x, at, :] * value
        for row, count in chunks(side_cells):
            at = pl.ds(row, count)
            pay[at, :] = q2[x0, at, :]
            pay[pl.ds(side_cells + row, count), :] = c[x0, at, :] * backward(
                layer(q2, x0), w2[x0, at, :], w3[x0, at, :], layer(inv, x0),
                (2.0 * g[0]) * u1[x0, at, :], [layer(q2, x1)], row, count, side_cells,
            )


def last_step(w1, q1, w2, s, x, at, sides, row, count, side_cells):
    q, total = beside(q1, row, count, side_cells)
    for other in sides:
        total = total + other(row, count)
    return 2.0 * w1(row, count) + total - 6.0 * q - (1.0 - s[x, at, :]) * w2[x, at, :]


def adjoint_end_kernel(weights, u1, w2, w3, q2, c, inv, s, w1, q1, cur_hbm, prev_hbm, cur, prev, sems):
    cx, side_cells = u1.shape[0], u1.shape[1]
    g0 = 2.0 * weights[0:1, 0:1]

    def first(x, inner):
        for row, count in chunks(side_cells):
            at = pl.ds(row, count)
            value = backward(
                layer(q2, x), w2[x, at, :], w3[x, at, :], layer(inv, x), g0 * u1[x, at, :],
                x_sides(q2, x, cx), row, count, side_cells,
            )
            w1[x, at, :] = value
            q1[x, at, :] = c[x, at, :] * value
            if inner:
                prev[x, at, :] = (s[x, at, :] - 1.0) * value

    def second(x):
        for row, count in chunks(side_cells):
            at = pl.ds(row, count)
            cur[x, at, :] = last_step(
                layer(w1, x), layer(q1, x), w2, s, x, at, x_sides(q1, x, cx), row, count, side_cells
            )

    first(0, False)
    sweep(1, cx - 1, lambda x: first(x, True))
    first(cx - 1, False)
    out_prev = pltpu.make_async_copy(
        prev.at[pl.ds(1, cx - 2)], prev_hbm.at[pl.ds(1, cx - 2)], sems.at[0]
    )
    out_prev.start()
    sweep(2, cx - 2, second)
    out_cur = pltpu.make_async_copy(
        cur.at[pl.ds(2, cx - 4)], cur_hbm.at[pl.ds(2, cx - 4)], sems.at[1]
    )
    out_cur.start()
    out_prev.wait()
    out_cur.wait()


def patch_kernel(
    own, absorb_ref, parity_ref, weights, map_ref, up, u, u1, u2, u3, u4, w3, w2, w1, q2, inv,
    u1h_a, u1h_b, got_a, got_b,
    sums, maps, values, columns,
):
    cx, side_cells = u.shape[0], u.shape[1]
    last = side_cells - 1
    g3 = 2.0 * weights[3:4, 0:1]
    columns[...] = jnp.zeros_like(columns)

    def field(x, at, lanes):
        k = (x, at, lanes)
        return (
            g3 * (inv[k] * u4[k]) * (u2[k] - u4[k])
            + w3[k] * (u1[k] - u3[k])
            + w2[k] * (u[k] - u2[k])
            + w1[k] * (up[k] - u1[k])
        )

    everything = pl.ds(0, side_cells)
    for x in range(cx):
        maps[4 * x : 4 * x + 4, :] = map_ref[x]
        values[4 * x : 4 * x + 1, :] = field(x, pl.ds(0, 8), everything)[0:1]
        values[4 * x + 1 : 4 * x + 2, :] = field(x, pl.ds(last - 7, 8), everything)[7:8]
        near = lambda row, count: field(x, pl.ds(row, count), pl.ds(0, LANES))
        far = lambda row, count: field(x, pl.ds(row, count), pl.ds(side_cells - LANES, LANES))
        put_column(columns, 2 * x, near, 0)
        put_column(columns, 2 * x + 1, far, LANES - 1)
    base = 2 * cx
    halves = ((u1h_a, got_a), (u1h_b, got_b))
    for side, (u1h, got) in enumerate(halves):
        x0 = end_layer(parity_ref[0], side, 0, cx)
        put_column(columns, base + 4 * side, low_tile(layer(q2, x0)), 0)
        put_column(columns, base + 4 * side + 1, high_tile(layer(q2, x0)), LANES - 1)
        put_column(columns, base + 4 * side + 2, low_tile(flat(u1h, 0)), 0)
        put_column(columns, base + 4 * side + 3, high_tile(flat(u1h, 0)), LANES - 1)
    rows = jnp.transpose(columns[...])
    for x in range(cx):
        values[4 * x + 2 : 4 * x + 4, :] = rows[2 * x : 2 * x + 2, :]
    for side, (u1h, got) in enumerate(halves):
        x0 = end_layer(parity_ref[0], side, 0, cx)
        extra = 2 * side_cells
        theirs = got[extra + 4 : extra + 8, :].astype(jnp.int32)
        damping = lookup(theirs, absorb_ref)
        lane = lax.broadcasted_iota(jnp.int32, (1, side_cells), 1)

        def corners(low, high):
            return jnp.where(lane == 0, low, 0.0) + jnp.where(lane == last, high, 0.0)

        d = [damping[f : f + 1] for f in range(4)]
        total = jnp.concatenate(
            [
                d[0] + corners(d[2][:, 0:1], d[3][:, 0:1]),
                d[1] + corners(d[2][:, last:], d[3][:, last:]),
                d[2] + corners(d[0][:, 0:1], d[1][:, 0:1]),
                d[3] + corners(d[0][:, last:], d[1][:, last:]),
            ],
            axis=0,
        )
        at = base + 4 * side
        mine = jnp.concatenate(
            [q2[x0, 0:1, :], q2[x0, last : last + 1, :], rows[at : at + 2, :]], axis=0
        )
        now = jnp.concatenate([u1h[0:1, :], u1h[last : last + 1, :], rows[at + 2 : at + 4, :]], axis=0)
        spot = 4 * cx + 4 * side
        values[spot : spot + 4, :] = mine * (got[extra : extra + 4, :] - now) / (1.0 + total)
        maps[spot : spot + 4, :] = theirs
    lane = lax.broadcasted_iota(jnp.int32, (1, LANES), 1)
    all_maps, all_values = maps[...], values[...]

    def owner(d, carry):
        row = jnp.zeros((1, LANES), F32)
        for j in range(own):
            picked = fold(jnp.where(all_maps == d * own + j, all_values, 0.0))
            half = picked[:, :LANES]
            for k in range(LANES, side_cells, LANES):
                half = half + picked[:, k : k + LANES]
            total = jnp.sum(jnp.sum(half, axis=0, keepdims=True), axis=1, keepdims=True)
            row = jnp.where(lane == j, total, row)
        sums[pl.ds(d, 1), :] = row
        return carry

    lax.fori_loop(0, sums.shape[0], owner, 0)


def join_last_kernel(
    parity_ref, w1, q1, w2, q2, c, inv, s, got_a, got_b, b_a, b_b, cur_in, prev_in,
    cur_hbm, prev_hbm, we, qe, halo, cur, prev, sems,
):
    cx, side_cells = w1.shape[0], w1.shape[1]
    copies = []
    for side, (got, b) in enumerate(((got_a, b_a), (got_b, b_b))):
        x0, x1, x2 = (end_layer(parity_ref[0], side, k, cx) for k in range(3))
        for row, count in chunks(side_cells):
            at = pl.ds(row, count)
            value = w1[x0, at, :] + inv[x0, at, :] * got[at, :]
            we[side, at, :] = value
            qe[side, at, :] = c[x0, at, :] * value
            prev[side, at, :] = (s[x0, at, :] - 1.0) * value
            below = pl.ds(side_cells + row, count)
            halo[at, :] = got[below, :] + b[below, :] * q2[x0, at, :]
        copies.append(pltpu.make_async_copy(prev.at[side], prev_hbm.at[x0], sems.at[3 * side]))
        copies[-1].start()
        for k, (x, w, q, others) in enumerate(
            (
                (x0, layer(we, side), layer(qe, side), [layer(q1, x1), flat(halo, 0)]),
                (x1, layer(w1, x1), layer(q1, x1), [layer(qe, side), layer(q1, x2)]),
            )
        ):
            for row, count in chunks(side_cells):
                at = pl.ds(row, count)
                cur[2 * side + k, at, :] = last_step(
                    w, q, w2, s, x, at, others, row, count, side_cells
                )
            copies.append(
                pltpu.make_async_copy(
                    cur.at[2 * side + k], cur_hbm.at[x], sems.at[3 * side + 1 + k]
                )
            )
            copies[-1].start()
    for copy in copies:
        copy.wait()


def call(kernel, ins, outs, scratch=(), aliases=None, name=None):
    kinds = {"v": in_vmem, "s": in_smem, "h": in_hbm}
    got = pl.pallas_call(
        kernel,
        out_shape=[
            pltpu.VMEM(shape, F32) if kind == "v" else jax.ShapeDtypeStruct(shape, F32)
            for kind, shape in outs
        ],
        in_specs=[kinds[kind] for kind, _ in ins],
        out_specs=[kinds[kind] for kind, _ in outs],
        scratch_shapes=list(scratch),
        input_output_aliases=aliases or {},
        compiler_params=pltpu.CompilerParams(vmem_limit_bytes=12 * 2**20),
        name=name,
    )(*[value for _, value in ins])
    return got


def on_device(u_prev, u_cur, courant_sq, patch_map, absorb, checkpoint, target_curve, tail_energy):
    cx, side = u_cur.shape[0], u_cur.shape[1]
    count = lax.axis_size("gx")
    patches = absorb.shape[0]
    own = patches // count
    all_cells = float(cx * count * side * side)
    field, plane = (cx, side, side), (side, side)
    double, triple = (2 * side, side), (2 * side + 8, side)
    parity = lax.rem(lax.axis_index("gx"), 2).astype(jnp.int32).reshape(1)
    within = [(i, i ^ 1) for i in range(count)]
    across = [(i, i + 1) for i in range(1, count - 1, 2)]
    across = across + [(j, i) for i, j in across]

    def swap(a, b):
        b = lax.ppermute(b, "gx", across)
        return lax.ppermute(a, "gx", within), b

    def deal(rows):
        return lax.all_to_all(rows, "gx", 0, 0, tiled=True)

    dma = pltpu.SemaphoreType.DMA
    sp, ab = ("s", parity), ("s", absorb)
    v = lambda *arrays: [("v", a) for a in arrays]
    near = call(
        start_kernel, [sp, ("h", u_cur)], [("v", plane)] * 2, [dma((2,))], name="edges"
    )
    near = swap(*near)
    u, up, c, s, inv, pay_a, pay_b = call(
        setup_kernel,
        [sp, ab, ("v", patch_map), ("h", u_cur), ("h", u_prev), ("h", courant_sq)],
        [("v", field)] * 5 + [("v", triple)] * 2,
        [
            VMEM((4 * cx, side), jnp.int32),
            VMEM((4 * cx, side), F32),
            VMEM((LANES, side), F32),
            VMEM((side, LANES), F32),
            dma((3,)),
        ],
        name="damping",
    )
    first = swap(pay_a, pay_b)
    u1, u2 = call(ahead_kernel, v(u, up, c, inv), [("v", field)] * 2, name="forward_1_2")
    u1, u2, u1h_a, u1h_b, pay_a, pay_b = call(
        join_first_kernel,
        [sp] + v(u, c, inv, *near, *first, u1, u2),
        [("v", field)] * 2 + [("v", plane)] * 2 + [("v", double)] * 2,
        aliases={8: 0, 9: 1},
        name="edges_1_2",
    )
    second = swap(pay_a, pay_b)
    u3, u4, energy = call(
        ahead_again_kernel,
        v(u1, u2, c, inv),
        [("v", field)] * 2 + [("v", (STEPS, 8, side))],
        name="forward_3_4",
    )
    u3, u4, u3h_a, u3h_b, pay_a, pay_b, energy_rows = call(
        join_second_kernel,
        [sp] + v(u2, c, inv, energy, *second, *first, u3, u4),
        [("v", field)] * 2 + [("v", plane)] * 2 + [("v", double)] * 2 + [("v", (count, LANES))],
        [VMEM((STEPS, 8, side), F32)],
        aliases={9: 0, 10: 1},
        name="edges_3_4",
    )
    third = swap(pay_a, pay_b)
    sums = deal(energy_rows)
    weights, w3, q3, w2, q2 = call(
        functools.partial(adjoint_kernel, all_cells),
        [("s", checkpoint), ("s", target_curve), ("s", tail_energy)] + v(sums, u2, u3, u4, c, inv),
        [("v", (8, LANES))] + [("v", field)] * 4,
        [VMEM(field, F32)],
        name="adjoint_3_2",
    )
    w3, q3, w2, q2, pay_a, pay_b = call(
        join_third_kernel,
        [sp] + v(weights, u1, u2, u4, c, inv, u3h_a, u3h_b, *third, *first, w3, q3, w2, q2),
        [("v", field)] * 4 + [("v", double)] * 2,
        [VMEM(plane, F32)],
        aliases={13: 0, 14: 1, 15: 2, 16: 3},
        name="edges_adjoint_3_2",
    )
    fourth = swap(pay_a, pay_b)
    w1, q1, cur, prev = call(
        adjoint_end_kernel,
        v(weights, u1, w2, w3, q2, c, inv, s),
        [("v", field)] * 2 + [("h", field)] * 2,
        [VMEM(field, F32), VMEM(field, F32), dma((2,))],
        name="adjoint_1_0",
    )
    (partial,) = call(
        functools.partial(patch_kernel, own),
        [ab, sp]
        + v(weights, patch_map, up, u, u1, u2, u3, u4, w3, w2, w1, q2, inv, u1h_a, u1h_b, *first),
        [("v", (count, LANES))],
        [
            VMEM((4 * cx + 8, side), jnp.int32),
            VMEM((4 * cx + 8, side), F32),
            VMEM((side, LANES), F32),
        ],
        name="patch_sums",
    )
    grad_absorb = jnp.sum(deal(partial), axis=0)[:own] / float(PATCH_CELLS)
    cur, prev = call(
        join_last_kernel,
        [sp] + v(w1, q1, w2, q2, c, inv, s, *fourth, *first) + [("h", cur), ("h", prev)],
        [("h", field)] * 2,
        [
            VMEM((2, side, side), F32),
            VMEM((2, side, side), F32),
            VMEM(plane, F32),
            VMEM((4, side, side), F32),
            VMEM((2, side, side), F32),
            dma((6,)),
        ],
        aliases={12: 0, 13: 1},
        name="edges_adjoint_1_0",
    )
    return prev, cur, grad_absorb


def solution(mesh):
    bricks = P(("groups", "gx"), None, None)
    return jax.shard_map(
        on_device,
        mesh=mesh,
        in_specs=(bricks, bricks, bricks, bricks, P("groups"), P("groups"), P("groups"), P("groups")),
        out_specs=(bricks, bricks, P(("groups", "gx"))),
        check_vma=False,
    )
```

```python
import functools

import jax
import jax.numpy as jnp
from jax import lax
from jax.experimental import pallas as pl
from jax.experimental.pallas import tpu as pltpu
from jax.sharding import PartitionSpec as P

STEPS = 4
PATCH_CELLS = 819
CHUNK = 16
LANES = 128
GROUP = 32
F32 = jnp.float32
VMEM = pltpu.VMEM
in_vmem = pl.BlockSpec(memory_space=pltpu.VMEM)
in_smem = pl.BlockSpec(memory_space=pltpu.SMEM)
in_hbm = pl.BlockSpec(memory_space=pltpu.HBM)


def end_layer(parity, side, depth, cx):
    high = 1 - parity if side == 0 else parity
    return high * (cx - 1 - depth) + (1 - high) * depth


def layer(ref, x):
    return lambda row, count: ref[x, pl.ds(row, count), :]


def flat(ref, base):
    return lambda row, count: ref[pl.ds(base + row, count), :]


def chunks(side_cells):
    return [(row, CHUNK) for row in range(0, side_cells, CHUNK)]


def beside(field, row, count, side_cells):
    v = field(row, count)
    tiles = [v[k : k + 8] for k in range(0, count, 8)]
    sub = lax.broadcasted_iota(jnp.int32, tiles[0].shape, 0)
    zero = jnp.zeros_like(tiles[0])
    before = pltpu.roll(field(row - 8, 8), 1, 0) if row else zero
    after = pltpu.roll(field(row + count, 8), 7, 0) if row + count < side_cells else zero
    down = [before] + [pltpu.roll(tile, 1, 0) for tile in tiles]
    up = [pltpu.roll(tile, 7, 0) for tile in tiles] + [after]
    total = jnp.concatenate(
        [
            jnp.where(sub == 0, down[k], down[k + 1]) + jnp.where(sub == 7, up[k + 1], up[k])
            for k in range(len(tiles))
        ],
        axis=0,
    )
    parts = [v[:, k : k + LANES] for k in range(0, side_cells, LANES)]
    lane = lax.broadcasted_iota(jnp.int32, parts[0].shape, 1)
    zero = jnp.zeros_like(parts[0])
    right = [zero] + [pltpu.roll(part, 1, 1) for part in parts]
    left = [pltpu.roll(part, LANES - 1, 1) for part in parts] + [zero]
    across = jnp.concatenate(
        [
            jnp.where(lane == 0, right[k], right[k + 1])
            + jnp.where(lane == LANES - 1, left[k + 1], left[k])
            for k in range(len(parts))
        ],
        axis=1,
    )
    return v, total + across


def forward(now, prior, courant, inverse, sides, row, count, side_cells):
    v, total = beside(now, row, count, side_cells)
    for other in sides:
        total = total + other(row, count)
    p = prior(row, count)
    c, i = courant(row, count), inverse(row, count)
    return i * (2.0 * (v - p) + c * (total - 6.0 * v)) + p


def backward(product, w, later, inverse, source, sides, row, count, side_cells):
    q, total = beside(product, row, count, side_cells)
    for other in sides:
        total = total + other(row, count)
    fresh = total - 6.0 * q + source
    i = inverse(row, count)
    if later is None:
        return i * (2.0 * w + fresh)
    return i * (2.0 * (w - later) + fresh) + later


def sweep(low, high, body):
    def turn(x, carry):
        body(x)
        return carry

    lax.fori_loop(low, high, turn, 0)


def x_sides(ref, x, cx):
    return [layer(ref, k) for k in (x - 1, x + 1) if not isinstance(k, int) or 0 <= k < cx]


def fold(values):
    total = values[0:8]
    for row in range(8, values.shape[0], 8):
        total = total + values[row : row + 8]
    return total


def spread_weight(weights, n, count):
    tile = weights[8 * n : 8 * n + 8, :]
    return jnp.concatenate([tile] * (count // 8), axis=0)


def start_kernel(parity_ref, u_hbm, a_ref, b_ref, sems):
    cx = u_hbm.shape[0]
    copies = []
    for side, out in enumerate((a_ref, b_ref)):
        x = end_layer(parity_ref[0], side, 0, cx)
        copies.append(pltpu.make_async_copy(u_hbm.at[x], out, sems.at[side]))
    for copy in copies:
        copy.start()
    for copy in copies:
        copy.wait()


def lookup(maps, absorb_ref):
    def turn(p, got):
        return jnp.where(maps == p, absorb_ref[p], got)

    return lax.fori_loop(0, absorb_ref.shape[0], turn, jnp.zeros(maps.shape, F32), unroll=8)


def to_lane(tile, spot, lane_from):
    return pltpu.roll(tile, (spot - lane_from) % LANES, 1)


def damping_at(x, cx, columns, found, row, count, side_cells):
    tile = columns[pl.ds(row, count), :]
    lane = lax.broadcasted_iota(jnp.int32, tile.shape, 1)
    near = jnp.where(lane == 0, pltpu.roll(tile, lax.rem(LANES - x, LANES), 1), 0.0)
    far = jnp.where(lane == LANES - 1, pltpu.roll(tile, LANES - 1 - cx - x, 1), 0.0)
    mid = [jnp.zeros_like(near)] * (side_cells // LANES - 2)
    field = jnp.concatenate([near, *mid, far], axis=1)
    sub = lax.broadcasted_iota(jnp.int32, field.shape, 0)
    if row == 0:
        field = field + jnp.where(sub == 0, found[pl.ds(4 * x, 1), :], 0.0)
    if row + count == side_cells:
        field = field + jnp.where(sub == count - 1, found[pl.ds(4 * x + 1, 1), :], 0.0)
    return field


def setup_kernel(
    parity_ref, absorb_ref, checkpoint_ref, target_ref, tail_ref, map_ref, e_a, e_b,
    u_hbm, up_hbm, c_hbm,
    pay_a, pay_b, columns, found, params,
    maps, turned, deep, prior, courant, inv, turned_back, sems,
):
    cx, side_cells = u_hbm.shape[0], u_hbm.shape[1]
    copies = []
    for side in range(2):
        x0 = end_layer(parity_ref[0], side, 0, cx)
        x1 = end_layer(parity_ref[0], side, 1, cx)
        for src, x, dst in ((up_hbm, x0, prior), (c_hbm, x0, courant), (u_hbm, x1, deep)):
            copies.append(
                pltpu.make_async_copy(src.at[x], dst.at[side], sems.at[len(copies)])
            )
            copies[-1].start()
    lane = lax.broadcasted_iota(jnp.int32, params.shape, 1)
    start = jnp.clip(checkpoint_ref[0], 0, target_ref.shape[0] - STEPS)
    row = jnp.where(lane == STEPS, tail_ref[0], 0.0)
    for n in range(STEPS):
        row = jnp.where(lane == n, target_ref[start + n], row)
    params[...] = row
    for x in range(cx):
        maps[4 * x : 4 * x + 4, :] = map_ref[x]
    found[...] = lookup(maps[...], absorb_ref)
    turned[...] = jnp.zeros_like(turned)
    for x in range(cx):
        turned[x : x + 1, :] = found[4 * x + 2 : 4 * x + 3, :]
        turned[cx + x : cx + x + 1, :] = found[4 * x + 3 : 4 * x + 4, :]
    columns[...] = jnp.transpose(turned[...])
    for side in range(2):
        x0 = end_layer(parity_ref[0], side, 0, cx)
        for row, count in chunks(side_cells):
            inv[side, pl.ds(row, count), :] = 1.0 / (
                1.0 + damping_at(x0, cx, columns, found, row, count, side_cells)
            )
    for copy in copies:
        copy.wait()
    for side, (edge, pay) in enumerate(((e_a, pay_a), (e_b, pay_b))):
        for row, count in chunks(side_cells):
            pay[pl.ds(row, count), :] = forward(
                flat(edge, 0), layer(prior, side), layer(courant, side), layer(inv, side),
                [layer(deep, side)], row, count, side_cells,
            )
            pay[pl.ds(side_cells + row, count), :] = (
                courant[side, pl.ds(row, count), :] * inv[side, pl.ds(row, count), :]
            )
    spot = lax.broadcasted_iota(jnp.int32, (CHUNK, LANES), 1)
    for row, count in chunks(side_cells):
        total = jnp.zeros((count, LANES), F32)
        for side in range(2):
            values = prior[side, pl.ds(row, count), :]
            total = jnp.where(spot == 2 * side, to_lane(values[:, :LANES], 2 * side, 0), total)
            total = jnp.where(
                spot == 2 * side + 1, to_lane(values[:, -LANES:], 2 * side + 1, LANES - 1), total
            )
        turned_back[pl.ds(row, count), :] = total
    rows = jnp.transpose(turned_back[...])
    base = 2 * side_cells
    for side, pay in enumerate((pay_a, pay_b)):
        x0 = end_layer(parity_ref[0], side, 0, cx)
        pay[base : base + 1, :] = prior[side, 0:1, :]
        pay[base + 1 : base + 2, :] = prior[side, side_cells - 1 : side_cells, :]
        pay[base + 2 : base + 4, :] = rows[2 * side : 2 * side + 2, :]
        pay[base + 4 : base + 8, :] = map_ref[x0].astype(F32)


def ahead_kernel(columns, found, u_hbm, up_hbm, c_hbm, u, up, c, s, inv, u1, u2, sems):
    cx, side_cells = u.shape[0], u.shape[1]
    copies = [
        pltpu.make_async_copy(src, dst, sems.at[k])
        for k, (src, dst) in enumerate(((u_hbm, u), (up_hbm, up), (c_hbm, c)))
    ]
    for copy in copies:
        copy.start()

    def spread(x):
        for row, count in chunks(side_cells):
            field = damping_at(x, cx, columns, found, row, count, side_cells)
            s[x, pl.ds(row, count), :] = field
            inv[x, pl.ds(row, count), :] = 1.0 / (1.0 + field)

    def first(x):
        for row, count in chunks(side_cells):
            u1[x, pl.ds(row, count), :] = forward(
                layer(u, x), layer(up, x), layer(c, x), layer(inv, x), x_sides(u, x, cx),
                row, count, side_cells,
            )

    def second(x):
        for row, count in chunks(side_cells):
            u2[x, pl.ds(row, count), :] = forward(
                layer(u1, x), layer(u, x), layer(c, x), layer(inv, x), x_sides(u1, x, cx),
                row, count, side_cells,
            )

    sweep(0, cx, spread)
    for copy in copies:
        copy.wait()
    for body in (first, second):
        body(0)
        sweep(1, cx - 1, body)
        body(cx - 1)


def join_forward(x0, x1, edge, mid, last, c, inv, got_now, got_part, got_b, b, halo, delta, side_cells):
    for row, count in chunks(side_cells):
        at = pl.ds(row, count)
        change = b(row, count) * got_now(row, count)
        delta[at, :] = change
        mid[x0, at, :] += change
        halo[at, :] = got_part(row, count) + got_b(row, count) * edge(row, count)
        last[x1, at, :] += (c[x1, at, :] * inv[x1, at, :]) * change
    for row, count in chunks(side_cells):
        at = pl.ds(row, count)
        v, total = beside(flat(delta, 0), row, count, side_cells)
        last[x0, at, :] += (2.0 * inv[x0, at, :]) * v + b(row, count) * (
            total - 6.0 * v + halo[at, :]
        )


def join_first_kernel(
    parity_ref, c, inv, e_a, e_b, near_a, near_b, own_a, own_b, got_a, got_b, u1_in, u2_in,
    u1, u2, halo_a, halo_b, pay_a, pay_b, delta,
):
    cx, side_cells = c.shape[0], c.shape[1]
    for side, (edge, near, own, got, halo, pay) in enumerate(
        ((e_a, near_a, own_a, got_a, halo_a, pay_a), (e_b, near_b, own_b, got_b, halo_b, pay_b))
    ):
        x0, x1 = (end_layer(parity_ref[0], side, k, cx) for k in range(2))
        join_forward(
            x0, x1, flat(edge, 0), u1, u2, c, inv, flat(near, 0), flat(got, 0),
            flat(got, side_cells), flat(own, side_cells), halo, delta, side_cells,
        )
        for row, count in chunks(side_cells):
            pay[pl.ds(row, count), :] = u2[x0, pl.ds(row, count), :]
            pay[pl.ds(side_cells + row, count), :] = forward(
                layer(u2, x0), layer(u1, x0), layer(c, x0), layer(inv, x0), [layer(u2, x1)],
                row, count, side_cells,
            )


def halo_walls(absorb_ref, map_ref, halves, maps, wall_gain, columns):
    cx, side_cells = map_ref.shape[0], columns.shape[0]
    last, extra = side_cells - 1, 2 * side_cells
    for x in range(cx):
        maps[4 * x : 4 * x + 4, :] = map_ref[x]
    for side, (_, got) in enumerate(halves):
        maps[4 * (cx + side) : 4 * (cx + side) + 4, :] = got[extra + 4 : extra + 8, :].astype(
            jnp.int32
        )
    damping = lookup(maps[4 * cx : 4 * cx + 8, :], absorb_ref)
    spot = lax.broadcasted_iota(jnp.int32, (CHUNK, LANES), 1)
    for row, count in chunks(side_cells):
        total = jnp.zeros((count, LANES), F32)
        for side, (u1h, _) in enumerate(halves):
            values = u1h[pl.ds(row, count), :]
            total = jnp.where(spot == 2 * side, to_lane(values[:, :LANES], 2 * side, 0), total)
            total = jnp.where(
                spot == 2 * side + 1, to_lane(values[:, -LANES:], 2 * side + 1, LANES - 1), total
            )
        columns[pl.ds(row, count), :] = total
    rows = jnp.transpose(columns[...])
    lane = lax.broadcasted_iota(jnp.int32, (1, side_cells), 1)

    def corners(one, two):
        return jnp.where(lane == 0, one, 0.0) + jnp.where(lane == last, two, 0.0)

    for side, (u1h, got) in enumerate(halves):
        d = [damping[4 * side + f : 4 * side + f + 1] for f in range(4)]
        total = jnp.concatenate(
            [
                d[0] + corners(d[2][:, 0:1], d[3][:, 0:1]),
                d[1] + corners(d[2][:, last:], d[3][:, last:]),
                d[2] + corners(d[0][:, 0:1], d[1][:, 0:1]),
                d[3] + corners(d[0][:, last:], d[1][:, last:]),
            ],
            axis=0,
        )
        now = jnp.concatenate(
            [u1h[0:1, :], u1h[last : last + 1, :], rows[2 * side : 2 * side + 2, :]], axis=0
        )
        wall_gain[4 * side : 4 * side + 4, :] = (got[extra : extra + 4, :] - now) / (1.0 + total)


def ahead_again_kernel(
    absorb_ref, map_ref, u1, u2, c, inv, u1h_a, u1h_b, got_a, got_b,
    u3, u4, energy, maps, wall_gain, columns,
):
    cx, side_cells = u1.shape[0], u1.shape[1]
    halo_walls(absorb_ref, map_ref, ((u1h_a, got_a), (u1h_b, got_b)), maps, wall_gain, columns)
    energy[...] = jnp.zeros_like(energy)

    def first(x, inner):
        sums = [jnp.zeros((8, side_cells), F32)] * 3
        for row, count in chunks(side_cells):
            value = forward(
                layer(u2, x), layer(u1, x), layer(c, x), layer(inv, x), x_sides(u2, x, cx),
                row, count, side_cells,
            )
            u3[x, pl.ds(row, count), :] = value
            sums[0] = sums[0] + fold(u1[x, pl.ds(row, count), :] ** 2)
            sums[1] = sums[1] + fold(u2[x, pl.ds(row, count), :] ** 2)
            sums[2] = sums[2] + fold(value * value)
        for k in range(3 if inner else 2):
            energy[k] += sums[k]

    def second(x, inner):
        total = jnp.zeros((8, side_cells), F32)
        for row, count in chunks(side_cells):
            value = forward(
                layer(u3, x), layer(u2, x), layer(c, x), layer(inv, x), x_sides(u3, x, cx),
                row, count, side_cells,
            )
            u4[x, pl.ds(row, count), :] = value
            total = total + fold(value * value)
        if inner:
            energy[3] += total

    first(0, False)
    sweep(1, cx - 1, lambda x: first(x, True))
    first(cx - 1, False)
    second(0, False)
    second(1, False)
    sweep(2, cx - 2, lambda x: second(x, True))
    second(cx - 2, False)
    second(cx - 1, False)


def join_second_kernel(
    parity_ref, c, inv, energy, edge_a, edge_b, own_a, own_b, got_a, got_b, b_a, b_b, u3_in, u4_in,
    u3, u4, halo_a, halo_b, pay_a, pay_b, energy_rows, delta,
):
    cx, side_cells = c.shape[0], c.shape[1]
    third = energy[2]
    fourth = energy[3]
    for side, (edge, own, got, gb, halo, pay) in enumerate(
        ((edge_a, own_a, got_a, b_a, halo_a, pay_a), (edge_b, own_b, got_b, b_b, halo_b, pay_b))
    ):
        x0, x1 = (end_layer(parity_ref[0], side, k, cx) for k in range(2))
        b = flat(own, side_cells)
        join_forward(
            x0, x1, flat(edge, 0), u3, u4, c, inv, flat(got, 0), flat(got, side_cells),
            flat(gb, side_cells), b, halo, delta, side_cells,
        )
        for row, count in chunks(side_cells):
            at = pl.ds(row, count)
            value, other = u4[x0, at, :], u4[x1, at, :]
            pay[at, :] = 2.0 * b(row, count) * value
            third = third + fold(u3[x0, at, :] ** 2)
            fourth = fourth + fold(value * value + other * other)
        for row, count in chunks(side_cells):
            at = pl.ds(row, count)
            q, total = beside(flat(pay, 0), row, count, side_cells)
            total = total + 2.0 * (c[x1, at, :] * inv[x1, at, :]) * u4[x1, at, :]
            pay[pl.ds(side_cells + row, count), :] = b(row, count) * (
                4.0 * (inv[x0, at, :] * u4[x0, at, :]) + total - 6.0 * q
            )
    lane = lax.broadcasted_iota(jnp.int32, energy_rows.shape, 1)
    rows = jnp.zeros(energy_rows.shape, F32)
    for n, part in enumerate((energy[0], energy[1], third, fourth)):
        total = jnp.sum(jnp.sum(part, axis=0, keepdims=True), axis=1, keepdims=True)
        rows = jnp.where(lane == n, total, rows)
    energy_rows[...] = rows


def adjoint_kernel(all_cells, params, sums, u2, u3, u4, c, inv, weights, w4, w3, w2, q2, q4, q3):
    cx, side_cells = u2.shape[0], u2.shape[1]
    totals = jnp.sum(sums[...], axis=0, keepdims=True) / all_cells
    lane = lax.broadcasted_iota(jnp.int32, totals.shape, 1)
    weight = jnp.zeros((1, 1), F32)
    for n in range(STEPS):
        rest = jnp.where(jnp.logical_and(lane >= n, lane < STEPS), totals, 0.0)
        schroeder = params[0:1, STEPS : STEPS + 1] + jnp.sum(rest, axis=1, keepdims=True)
        weight = weight + 2.0 * (jnp.log(schroeder) - params[0:1, n : n + 1]) / schroeder
        weights[8 * n : 8 * n + 8, :] = jnp.broadcast_to(2.0 * weight, (8, side_cells))

    def zeroth(x):
        for row, count in chunks(side_cells):
            at = pl.ds(row, count)
            value = spread_weight(weights, 3, count) * (inv[x, at, :] * u4[x, at, :])
            w4[x, at, :] = value
            q4[x, at, :] = c[x, at, :] * value

    def first(x):
        for row, count in chunks(side_cells):
            at = pl.ds(row, count)
            value = backward(
                layer(q4, x), w4[x, at, :], None, layer(inv, x),
                spread_weight(weights, 2, count) * u3[x, at, :],
                x_sides(q4, x, cx), row, count, side_cells,
            )
            w3[x, at, :] = value
            q3[x, at, :] = c[x, at, :] * value

    def second(x):
        for row, count in chunks(side_cells):
            at = pl.ds(row, count)
            value = backward(
                layer(q3, x), w3[x, at, :], w4[x, at, :], layer(inv, x),
                spread_weight(weights, 1, count) * u2[x, at, :],
                x_sides(q3, x, cx), row, count, side_cells,
            )
            w2[x, at, :] = value
            q2[x, at, :] = c[x, at, :] * value

    sweep(0, cx, zeroth)
    for body in (first, second):
        body(0)
        sweep(1, cx - 1, body)
        body(cx - 1)


def join_third_kernel(
    parity_ref, weights, u1, c, inv, u3h_a, u3h_b, own_a, own_b, got_a, got_b, b_a, b_b,
    w3_in, w2_in, q2_in,
    w3, w2, q2, pay_a, pay_b, halo, delta,
):
    cx, side_cells = c.shape[0], c.shape[1]
    g = [spread_weight(weights, n, CHUNK) for n in range(STEPS)]
    for side, (u3h, own, got, b, pay) in enumerate(
        ((u3h_a, own_a, got_a, b_a, pay_a), (u3h_b, own_b, got_b, b_b, pay_b))
    ):
        x0, x1 = (end_layer(parity_ref[0], side, k, cx) for k in range(2))
        for row, count in chunks(side_cells):
            at, below = pl.ds(row, count), pl.ds(side_cells + row, count)
            change = (0.5 * g[3]) * (inv[x0, at, :] * got[at, :])
            w3[x0, at, :] += change
            change = c[x0, at, :] * change
            delta[at, :] = change
            bh = b[below, :]
            halo[at, :] = (0.5 * g[3]) * (got[below, :] + bh * own[at, :]) + g[2] * (bh * u3h[at, :])
            value = w2[x1, at, :] + inv[x1, at, :] * change
            w2[x1, at, :] = value
            q2[x1, at, :] = c[x1, at, :] * value
        for row, count in chunks(side_cells):
            at = pl.ds(row, count)
            v, total = beside(flat(delta, 0), row, count, side_cells)
            i = inv[x0, at, :]
            value = w2[x0, at, :] + i * (
                g[3] * (i * got[at, :]) + total - 6.0 * v + halo[at, :]
            )
            w2[x0, at, :] = value
            value = c[x0, at, :] * value
            q2[x0, at, :] = value
            pay[at, :] = value
        for row, count in chunks(side_cells):
            at = pl.ds(row, count)
            pay[pl.ds(side_cells + row, count), :] = c[x0, at, :] * backward(
                flat(pay, 0), w2[x0, at, :], w3[x0, at, :], layer(inv, x0),
                g[0] * u1[x0, at, :], [layer(q2, x1)], row, count, side_cells,
            )


def adjoint_end_kernel(weights, u1, w2, w3, q2, c, inv, w1, q1):
    cx, side_cells = u1.shape[0], u1.shape[1]
    g0 = spread_weight(weights, 0, CHUNK)

    def first(x):
        for row, count in chunks(side_cells):
            at = pl.ds(row, count)
            value = backward(
                layer(q2, x), w2[x, at, :], w3[x, at, :], layer(inv, x), g0 * u1[x, at, :],
                x_sides(q2, x, cx), row, count, side_cells,
            )
            w1[x, at, :] = value
            q1[x, at, :] = c[x, at, :] * value

    first(0)
    sweep(1, cx - 1, first)
    first(cx - 1)


def result_kernel(w1, q1, w2, s, dealt, cur_hbm, prev_hbm, cur_ends, mine, cur, prev, sems):
    cx, side_cells = w1.shape[0], w1.shape[1]
    mine[...] = jnp.sum(dealt[...], axis=0, keepdims=True) / float(PATCH_CELLS)

    def send_cur(x):
        return pltpu.make_async_copy(cur.at[x], cur_hbm.at[x], sems.at[0, x])

    def send_prev(x):
        return pltpu.make_async_copy(prev.at[x], prev_hbm.at[x], sems.at[1, x])

    def turn(x, ends=None):
        for row, count in chunks(side_cells):
            at = pl.ds(row, count)
            q, total = beside(layer(q1, x), row, count, side_cells)
            for other in x_sides(q1, x, cx):
                total = total + other(row, count)
            w, keep = w1[x, at, :], s[x, at, :] - 1.0
            value = 2.0 * w + total - 6.0 * q + keep * w2[x, at, :]
            if ends is None:
                cur[x, at, :] = value
            else:
                cur_ends[ends, at, :] = value
            prev[x, at, :] = keep * w
        if ends is None:
            send_cur(x).start()
        if ends in (None, 1, 2):
            send_prev(x).start()

    turn(1, 1)
    turn(cx - 2, 2)
    sweep(2, cx - 2, turn)
    turn(0, 0)
    turn(cx - 1, 3)
    sweep(1, cx - 1, lambda x: send_prev(x).wait())
    sweep(2, cx - 2, lambda x: send_cur(x).wait())


def patch_kernel(
    own, parity_ref, maps, wall_gain, up, u, u1, u2, u3, u4, w4, w3, w2, w1, q2,
    sums, values, columns, totals,
):
    cx, side_cells = u.shape[0], u.shape[1]
    last = side_cells - 1
    ends = [end_layer(parity_ref[0], side, 0, cx) for side in range(2)]

    def field(x, at, lanes):
        k = (x, at, lanes)
        return (
            w4[k] * (u2[k] - u4[k])
            + w3[k] * (u1[k] - u3[k])
            + (w2[k] * (u[k] - u2[k]) + w1[k] * (up[k] - u1[k]))
        )

    everything = pl.ds(0, side_cells)
    low, high = pl.ds(0, LANES), pl.ds(side_cells - LANES, LANES)
    for x in range(cx):
        values[4 * x : 4 * x + 1, :] = field(x, pl.ds(0, 8), everything)[0:1]
        values[4 * x + 1 : 4 * x + 2, :] = field(x, pl.ds(last - 7, 8), everything)[7:8]
    base = 2 * cx
    spot = lax.broadcasted_iota(jnp.int32, (CHUNK, LANES), 1)

    def gather(k, carry):
        at = pl.ds(pl.multiple_of(k * CHUNK, CHUNK), CHUNK)
        total = jnp.zeros((CHUNK, LANES), F32)
        for x in range(cx):
            for j, (lanes, lane_from) in enumerate(((low, 0), (high, LANES - 1))):
                tile = to_lane(field(x, at, lanes), 2 * x + j, lane_from)
                total = jnp.where(spot == 2 * x + j, tile, total)
        for side in range(2):
            for j, (lanes, lane_from) in enumerate(((low, 0), (high, LANES - 1))):
                place = base + 2 * side + j
                total = jnp.where(
                    spot == place, to_lane(q2[ends[side], at, lanes], place, lane_from), total
                )
        columns[at, :] = total
        return carry

    lax.fori_loop(0, side_cells // CHUNK, gather, 0)
    rows = jnp.transpose(columns[...])
    for x in range(cx):
        values[4 * x + 2 : 4 * x + 4, :] = rows[2 * x : 2 * x + 2, :]
    for side in range(2):
        at, place = base + 2 * side, 4 * (cx + side)
        theirs = jnp.concatenate(
            [q2[ends[side], 0:1, :], q2[ends[side], last : last + 1, :], rows[at : at + 2, :]], axis=0
        )
        values[place : place + 4, :] = theirs * wall_gain[4 * side : 4 * side + 4, :]
    all_maps, all_values = maps[...], values[...]

    def patch(k, carry):
        for m in range(GROUP // 8):
            block = []
            for j in range(8):
                picked = fold(jnp.where(all_maps == GROUP * k + 8 * m + j, all_values, 0.0))
                half = picked[:, :LANES]
                for first in range(LANES, side_cells, LANES):
                    half = half + picked[:, first : first + LANES]
                block.append(jnp.sum(half, axis=0, keepdims=True))
            total = jnp.sum(jnp.concatenate(block, axis=0), axis=1, keepdims=True)
            totals[pl.ds(pl.multiple_of(GROUP * k + 8 * m, 8), 8), :] = jnp.broadcast_to(
                total, (8, LANES)
            )
        return carry

    lax.fori_loop(0, totals.shape[0] // GROUP, patch, 0)
    every = totals[...]
    ahead = lax.broadcasted_iota(jnp.int32, every.shape, 0) - lax.broadcasted_iota(
        jnp.int32, every.shape, 1
    )
    ahead = jnp.where(lax.broadcasted_iota(jnp.int32, every.shape, 1) < own, ahead, -1)

    def owner(d, carry):
        for k in range(4):
            mine = jnp.where(ahead == (4 * d + k) * own, every, 0.0)
            sums[pl.ds(4 * d + k, 1), :] = jnp.sum(mine, axis=0, keepdims=True)
        return carry

    lax.fori_loop(0, sums.shape[0] // 4, owner, 0)


def join_last_kernel(
    parity_ref, w1, q2, c, inv, s, got_a, got_b, b_a, b_b, cur_ends, cur_in, prev_in,
    cur_hbm, prev_hbm, delta, cur, prev, sems,
):
    cx, side_cells = w1.shape[0], w1.shape[1]
    copies = []

    def send(src, dst, x):
        copies.append(pltpu.make_async_copy(src, dst.at[x], sems.at[len(copies)]))
        copies[-1].start()

    for side, (got, b) in enumerate(((got_a, b_a), (got_b, b_b))):
        x0, x1 = (end_layer(parity_ref[0], side, k, cx) for k in range(2))
        e0, e1 = (end_layer(parity_ref[0], side, k, 4) for k in range(2))
        for row, count in chunks(side_cells):
            at = pl.ds(row, count)
            change = inv[x0, at, :] * got[at, :]
            prev[side, at, :] = (s[x0, at, :] - 1.0) * (w1[x0, at, :] + change)
            change = c[x0, at, :] * change
            delta[at, :] = change
            cur[2 * side + 1, at, :] = cur_ends[e1, at, :] + change
        send(prev.at[side], prev_hbm, x0)
        send(cur.at[2 * side + 1], cur_hbm, x1)
        for row, count in chunks(side_cells):
            at, below = pl.ds(row, count), pl.ds(side_cells + row, count)
            v, total = beside(flat(delta, 0), row, count, side_cells)
            cur[2 * side, at, :] = (
                cur_ends[e0, at, :]
                + 2.0 * (inv[x0, at, :] * got[at, :])
                + (total - 6.0 * v)
                + (got[below, :] + b[below, :] * q2[x0, at, :])
            )
        send(cur.at[2 * side], cur_hbm, x0)
    for copy in copies:
        copy.wait()


def call(kernel, ins, outs, scratch=(), aliases=None, name=None, us=2.0):
    kinds = {"v": in_vmem, "s": in_smem, "h": in_hbm}
    return pl.pallas_call(
        kernel,
        out_shape=[
            (pltpu.VMEM if kind == "v" else pltpu.HBM)(shape, *(dtype or [F32]))
            for kind, shape, *dtype in outs
        ],
        in_specs=[kinds[kind] for kind, _ in ins],
        out_specs=[kinds[kind] for kind, *_ in outs],
        scratch_shapes=list(scratch),
        input_output_aliases=aliases or {},
        compiler_params=pltpu.CompilerParams(vmem_limit_bytes=12 * 2**20),
        cost_estimate=pl.CostEstimate(flops=0, transcendentals=0, bytes_accessed=int(us * 3.0e6)),
        name=name,
    )(*[value for _, value in ins])


def on_device(u_prev, u_cur, courant_sq, patch_map, absorb, checkpoint, target_curve, tail_energy):
    cx, side = u_cur.shape[0], u_cur.shape[1]
    count = lax.axis_size("gx")
    patches = absorb.shape[0]
    own = patches // count
    all_cells = float(cx * count * side * side)
    field, plane = (cx, side, side), (side, side)
    double, triple = (2 * side, side), (2 * side + 8, side)
    parity = lax.rem(lax.axis_index("gx"), 2).astype(jnp.int32).reshape(1)
    within = [(i, i ^ 1) for i in range(count)]
    across = [(i, i + 1) for i in range(1, count - 1, 2)]
    across = across + [(j, i) for i, j in across]

    def swap(a, b):
        b = lax.ppermute(b, "gx", across)
        return lax.ppermute(a, "gx", within), b

    def deal(rows):
        return lax.all_to_all(rows, "gx", 0, 0, tiled=True)

    dma = pltpu.SemaphoreType.DMA
    sp, ab = ("s", parity), ("s", absorb)
    v = lambda *arrays: [("v", a) for a in arrays]
    raw = [
        ("h", pltpu.with_memory_space_constraint(a, pltpu.HBM))
        for a in (u_cur, u_prev, courant_sq)
    ]
    edge = call(start_kernel, [sp, raw[0]], [("v", plane)] * 2, [dma((2,))], name="edges", us=1.0)
    near = swap(*edge)
    *pays, columns, found, params = call(
        setup_kernel,
        [sp, ab, ("s", checkpoint), ("s", target_curve), ("s", tail_energy)]
        + v(patch_map, *edge)
        + raw,
        [("v", triple)] * 2
        + [("v", (side, LANES)), ("v", (4 * cx, side)), ("v", (8, LANES))],
        [
            VMEM((4 * cx, side), jnp.int32),
            VMEM((LANES, side), F32),
            VMEM((2, side, side), F32),
            VMEM((2, side, side), F32),
            VMEM((2, side, side), F32),
            VMEM((2, side, side), F32),
            VMEM((side, LANES), F32),
            dma((6,)),
        ],
        name="damping",
        us=2.6,
    )
    first = swap(*pays)
    u, up, c, s, inv, u1, u2 = call(
        ahead_kernel, v(columns, found) + raw, [("v", field)] * 7, [dma((3,))], name="forward_1_2", us=7.0
    )
    u1, u2, u1h_a, u1h_b, *edge_2 = call(
        join_first_kernel,
        [sp] + v(c, inv, *edge, *near, *pays, *first, u1, u2),
        [("v", field)] * 2 + [("v", plane)] * 2 + [("v", double)] * 2,
        [VMEM(plane, F32)],
        aliases={11: 0, 12: 1},
        name="edges_1_2",
    )
    second = swap(*edge_2)
    u3, u4, energy, maps, wall_gain = call(
        ahead_again_kernel,
        [ab] + v(patch_map, u1, u2, c, inv, u1h_a, u1h_b, *first),
        [("v", field)] * 2
        + [("v", (STEPS, 8, side)), ("v", (4 * cx + 8, side), jnp.int32), ("v", (8, side))],
        [VMEM((side, LANES), F32)],
        name="forward_3_4",
        us=5.5,
    )
    u3, u4, u3h_a, u3h_b, *edge_4, energy_rows = call(
        join_second_kernel,
        [sp] + v(c, inv, energy, *edge_2, *pays, *second, *first, u3, u4),
        [("v", field)] * 2 + [("v", plane)] * 2 + [("v", double)] * 2 + [("v", (count, LANES))],
        [VMEM(plane, F32)],
        aliases={12: 0, 13: 1},
        name="edges_3_4",
    )
    third = swap(*edge_4)
    sums = deal(energy_rows)
    weights, w4, w3, w2, q2 = call(
        functools.partial(adjoint_kernel, all_cells),
        v(params, sums, u2, u3, u4, c, inv),
        [("v", (8 * STEPS, side))] + [("v", field)] * 4,
        [VMEM(field, F32), VMEM(field, F32)],
        name="adjoint_3_2",
        us=5.0,
    )
    w3, w2, q2, *edge_2 = call(
        join_third_kernel,
        [sp] + v(weights, u1, c, inv, u3h_a, u3h_b, *edge_4, *third, *first, w3, w2, q2),
        [("v", field)] * 3 + [("v", double)] * 2,
        [VMEM(plane, F32), VMEM(plane, F32)],
        aliases={13: 0, 14: 1, 15: 2},
        name="edges_adjoint_3_2",
    )
    fourth = swap(*edge_2)
    w1, q1 = call(
        adjoint_end_kernel, v(weights, u1, w2, w3, q2, c, inv), [("v", field)] * 2, name="adjoint_1"
    )
    (partial,) = call(
        functools.partial(patch_kernel, own),
        [sp] + v(maps, wall_gain, up, u, u1, u2, u3, u4, w4, w3, w2, w1, q2),
        [("v", (count, LANES))],
        [
            VMEM((4 * cx + 8, side), F32),
            VMEM((side, LANES), F32),
            VMEM((-(-patches // GROUP) * GROUP, LANES), F32),
        ],
        name="patch_sums",
    )
    cur, prev, cur_ends, mine = call(
        result_kernel,
        v(w1, q1, w2, s, deal(partial)),
        [("h", field)] * 2 + [("v", (4, side, side)), ("v", (1, LANES))],
        [VMEM(field, F32), VMEM(field, F32), dma((2, cx))],
        name="adjoint_0",
    )
    grad_absorb = mine[0, :own]
    cur, prev = call(
        join_last_kernel,
        [sp] + v(w1, q2, c, inv, s, *fourth, *first, cur_ends) + [("h", cur), ("h", prev)],
        [("h", field)] * 2,
        [VMEM(plane, F32), VMEM((4, side, side), F32), VMEM((2, side, side), F32), dma((6,))],
        aliases={11: 0, 12: 1},
        name="edges_adjoint_1_0",
    )
    return prev, cur, grad_absorb


def solution(mesh):
    bricks = P(("groups", "gx"), None, None)
    return jax.shard_map(
        on_device,
        mesh=mesh,
        in_specs=(bricks, bricks, bricks, bricks, P("groups"), P("groups"), P("groups"), P("groups")),
        out_specs=(bricks, bricks, P(("groups", "gx"))),
        check_vma=False,
    )
```

```python
import functools

import jax
import jax.numpy as jnp
from jax import lax
from jax.experimental import pallas as pl
from jax.experimental.pallas import tpu as pltpu
from jax.sharding import PartitionSpec as P

STEPS = 4
PATCH_CELLS = 819
CHUNK = 16
LANES = 128
GROUP = 80
F32 = jnp.float32
VMEM = pltpu.VMEM
in_vmem = pl.BlockSpec(memory_space=pltpu.VMEM)
in_smem = pl.BlockSpec(memory_space=pltpu.SMEM)
in_hbm = pl.BlockSpec(memory_space=pltpu.HBM)


def end_layer(parity, side, depth, cx):
    high = 1 - parity if side == 0 else parity
    return high * (cx - 1 - depth) + (1 - high) * depth


def own_parity():
    return lax.rem(lax.axis_index("gx"), 2)


def layer(ref, x):
    return lambda row, count: ref[x, pl.ds(row, count), :]


def flat(ref, base):
    return lambda row, count: ref[pl.ds(base + row, count), :]


def chunks(side_cells):
    return [(row, CHUNK) for row in range(0, side_cells, CHUNK)]


def beside(field, row, count, side_cells):
    v = field(row, count)
    tiles = [v[k : k + 8] for k in range(0, count, 8)]
    sub = lax.broadcasted_iota(jnp.int32, tiles[0].shape, 0)
    zero = jnp.zeros_like(tiles[0])
    before = pltpu.roll(field(row - 8, 8), 1, 0) if row else zero
    after = pltpu.roll(field(row + count, 8), 7, 0) if row + count < side_cells else zero
    down = [before] + [pltpu.roll(tile, 1, 0) for tile in tiles]
    up = [pltpu.roll(tile, 7, 0) for tile in tiles] + [after]
    total = jnp.concatenate(
        [
            jnp.where(sub == 0, down[k], down[k + 1]) + jnp.where(sub == 7, up[k + 1], up[k])
            for k in range(len(tiles))
        ],
        axis=0,
    )
    parts = [v[:, k : k + LANES] for k in range(0, side_cells, LANES)]
    lane = lax.broadcasted_iota(jnp.int32, parts[0].shape, 1)
    zero = jnp.zeros_like(parts[0])
    right = [zero] + [pltpu.roll(part, 1, 1) for part in parts]
    left = [pltpu.roll(part, LANES - 1, 1) for part in parts] + [zero]
    across = jnp.concatenate(
        [
            jnp.where(lane == 0, right[k], right[k + 1])
            + jnp.where(lane == LANES - 1, left[k + 1], left[k])
            for k in range(len(parts))
        ],
        axis=1,
    )
    return v, total + across


def forward(now, prior, courant, inverse, sides, row, count, side_cells):
    v, total = beside(now, row, count, side_cells)
    for other in sides:
        total = total + other(row, count)
    p = prior(row, count)
    c, i = courant(row, count), inverse(row, count)
    return i * (2.0 * (v - p) + c * (total - 6.0 * v)) + p


def backward(product, w, later, inverse, source, sides, row, count, side_cells):
    q, total = beside(product, row, count, side_cells)
    for other in sides:
        total = total + other(row, count)
    fresh = total - 6.0 * q + source
    i = inverse(row, count)
    if later is None:
        return i * (2.0 * w + fresh)
    return i * (2.0 * (w - later) + fresh) + later


def sweep(low, high, body):
    def turn(x, carry):
        body(x)
        return carry

    lax.fori_loop(low, high, turn, 0)


def x_sides(ref, x, cx):
    return [layer(ref, k) for k in (x - 1, x + 1) if not isinstance(k, int) or 0 <= k < cx]


def fold(values):
    total = values[0:8]
    for row in range(8, values.shape[0], 8):
        total = total + values[row : row + 8]
    return total


def spread_weight(weights, n, count):
    tile = weights[8 * n : 8 * n + 8, :]
    return jnp.concatenate([tile] * (count // 8), axis=0)


def start_kernel(map_hbm, u_hbm, c_hbm, c_a, u_b, c_b, maps, sems):
    cx, side_cells = u_hbm.shape[0], u_hbm.shape[1]
    copies = []
    ends = [end_layer(own_parity(), side, 0, cx) for side in range(2)]
    u_a = c_a.at[pl.ds(side_cells + 8, side_cells)]
    for side, (u, c) in enumerate(((u_a, c_a), (u_b, c_b))):
        x0 = ends[side]
        for k, (src, dst) in enumerate(
            ((map_hbm, maps.at[side]), (u_hbm, u), (c_hbm, c.at[pl.ds(0, side_cells)]))
        ):
            copies.append(pltpu.make_async_copy(src.at[x0], dst, sems.at[k, side]))
    for copy in copies:
        copy.start()
    for side, c in enumerate((c_a, c_b)):
        copies[3 * side].wait()
        c[side_cells : side_cells + 4, :] = maps[side].astype(F32)
        c[side_cells + 4 : side_cells + 8, :] = jnp.zeros((4, side_cells), F32)
    for k, copy in enumerate(copies):
        if k % 3:
            copy.wait()


def lookup(maps, absorb_ref):
    def turn(p, got):
        return jnp.where(maps == p, absorb_ref[p], got)

    return lax.fori_loop(0, absorb_ref.shape[0], turn, jnp.zeros(maps.shape, F32), unroll=8)


def to_lane(tile, spot, lane_from):
    return pltpu.roll(tile, (spot - lane_from) % LANES, 1)


def wall_fields(columns, gains, low, high, top, bottom, row, count, side_cells):
    lane = lax.broadcasted_iota(jnp.int32, (count, LANES), 1)

    def place(ref, other):
        tile = ref[pl.ds(row, count), :]
        near = pltpu.roll(tile, lax.rem(LANES - low, LANES), 1)
        far = pltpu.roll(tile, LANES - 1 - high, 1)
        mid = [jnp.full((count, LANES), other, F32)] * (side_cells // LANES - 2)
        return jnp.concatenate(
            [
                jnp.where(lane == 0, near, other),
                *mid,
                jnp.where(lane == LANES - 1, far, other),
            ],
            axis=1,
        )

    field = place(columns, 0.0)
    if 0 < row and row + count < side_cells:
        return field, place(gains, 1.0)
    sub = lax.broadcasted_iota(jnp.int32, field.shape, 0)
    if row == 0:
        field = field + jnp.where(sub == 0, top, 0.0)
    if row + count == side_cells:
        field = field + jnp.where(sub == count - 1, bottom, 0.0)
    return field, 1.0 / (1.0 + field)


def ahead_one_kernel(
    absorb_ref, checkpoint, target, tail, map_hbm, u_hbm, up_hbm, c_hbm,
    u, up, c, s, inv, u1, params, map_ref,
    maps, found, turned, columns, gains, sems,
):
    cx, side_cells = u.shape[0], u.shape[1]
    copies = [
        pltpu.make_async_copy(src, dst, sems.at[k])
        for k, (src, dst) in enumerate(
            ((map_hbm, map_ref), (u_hbm, u), (up_hbm, up), (c_hbm, c))
        )
    ]
    for copy in copies:
        copy.start()
    copies[0].wait()
    for x in range(cx):
        maps[4 * x : 4 * x + 4, :] = map_ref[x]
    found[...] = lookup(maps[...], absorb_ref)
    turned[...] = jnp.zeros_like(turned)
    for x in range(cx):
        turned[x : x + 1, :] = found[4 * x + 2 : 4 * x + 3, :]
        turned[cx + x : cx + x + 1, :] = found[4 * x + 3 : 4 * x + 4, :]
    columns[...] = jnp.transpose(turned[...])
    gains[...] = 1.0 / (1.0 + columns[...])

    def spread(x):
        for row, count in chunks(side_cells):
            at = pl.ds(row, count)
            field, gain = wall_fields(
                columns, gains, x, cx + x, found[pl.ds(4 * x, 1), :], found[pl.ds(4 * x + 1, 1), :],
                row, count, side_cells,
            )
            s[x, at, :] = field
            inv[x, at, :] = gain

    def first(x):
        for row, count in chunks(side_cells):
            u1[x, pl.ds(row, count), :] = forward(
                layer(u, x), layer(up, x), layer(c, x), layer(inv, x), x_sides(u, x, cx),
                row, count, side_cells,
            )

    sweep(0, cx, spread)
    for copy in copies[1:]:
        copy.wait()
    history = target.shape[1]
    lane = lax.broadcasted_iota(jnp.int32, params.shape, 1)
    spot = lax.broadcasted_iota(jnp.int32, target.shape, 1)
    start = jnp.clip(checkpoint[...], 0, history - STEPS)
    row = jnp.where(lane == STEPS, tail[...], 0.0)
    for n in range(STEPS):
        value = jnp.sum(jnp.where(spot == start + n, target[...], 0.0), axis=1, keepdims=True)
        row = jnp.where(lane == n, value, row)
    params[...] = row
    first(0)
    sweep(1, cx - 1, first)
    first(cx - 1)


def join_one_kernel(c, inv, near_a, near_b, u1_in, u1, edge_a, edge_b):
    cx, side_cells = c.shape[0], c.shape[1]
    near_a = near_a.at[pl.ds(side_cells + 8, side_cells)]
    for side, (near, edge) in enumerate(((near_a, edge_a), (near_b, edge_b))):
        x0 = end_layer(own_parity(), side, 0, cx)
        for row, count in chunks(side_cells):
            at = pl.ds(row, count)
            value = u1[x0, at, :] + (c[x0, at, :] * inv[x0, at, :]) * near[at, :]
            u1[x0, at, :] = value
            edge[at, :] = value


def wall_rows(plane, columns, side_cells):
    last = side_cells - 1
    spot = lax.broadcasted_iota(jnp.int32, (CHUNK, LANES), 1)
    low, high = pl.ds(0, LANES), pl.ds(side_cells - LANES, LANES)
    for row, count in chunks(side_cells):
        at = pl.ds(row, count)
        far = to_lane(plane(at, high), 1, LANES - 1)
        columns[at, :] = jnp.where(spot == 0, plane(at, low), jnp.where(spot == 1, far, 0.0))
    rows = jnp.transpose(columns[...])
    every = pl.ds(0, side_cells)
    return jnp.concatenate([plane(pl.ds(0, 1), every), plane(pl.ds(last, 1), every), rows[0:2]], axis=0)


def ahead_two_kernel(
    absorb_ref, map_ref, u, up, c, inv, u1, got_a, got_b,
    u2, own_a, own_b, b_a, b_b, maps, wall_gain, wall_prior, columns, gains, turned,
):
    cx, side_cells = u.shape[0], u.shape[1]
    last = side_cells - 1
    ends = [end_layer(own_parity(), side, 0, cx) for side in range(2)]
    for x in range(cx):
        maps[4 * x : 4 * x + 4, :] = map_ref[x]
    for side, got in enumerate((got_a, got_b)):
        maps[4 * (cx + side) : 4 * (cx + side) + 4, :] = got[
            side_cells : side_cells + 4, :
        ].astype(jnp.int32)
    damping = lookup(maps[4 * cx : 4 * cx + 8, :], absorb_ref)
    turned[...] = jnp.zeros_like(turned)
    for side in range(2):
        turned[2 * side : 2 * side + 2, :] = damping[4 * side + 2 : 4 * side + 4]
    columns[...] = jnp.transpose(turned[...])
    gains[...] = 1.0 / (1.0 + columns[...])
    lane = lax.broadcasted_iota(jnp.int32, (1, side_cells), 1)

    def corners(one, two):
        return jnp.where(lane == 0, one, 0.0) + jnp.where(lane == last, two, 0.0)

    for side, (got, own, b) in enumerate(((got_a, own_a, b_a), (got_b, own_b, b_b))):
        d = [damping[4 * side + f : 4 * side + f + 1] for f in range(4)]
        for row, count in chunks(side_cells):
            at = pl.ds(row, count)
            own[at, :] = c[ends[side], at, :] * inv[ends[side], at, :]
            _, gain = wall_fields(
                columns, gains, 2 * side, 2 * side + 1, d[0], d[1], row, count, side_cells
            )
            b[at, :] = got[at, :] * gain
        total = jnp.concatenate(
            [
                d[0] + corners(d[2][:, 0:1], d[3][:, 0:1]),
                d[1] + corners(d[2][:, last:], d[3][:, last:]),
                d[2] + corners(d[0][:, 0:1], d[1][:, 0:1]),
                d[3] + corners(d[0][:, last:], d[1][:, last:]),
            ],
            axis=0,
        )
        wall_gain[4 * side : 4 * side + 4, :] = 1.0 / (1.0 + total)
    for side in range(2):
        wall_prior[4 * side : 4 * side + 4, :] = wall_rows(
            lambda at, lanes, x=ends[side]: up[x, at, lanes], columns, side_cells
        )

    def second(x):
        for row, count in chunks(side_cells):
            u2[x, pl.ds(row, count), :] = forward(
                layer(u1, x), layer(u, x), layer(c, x), layer(inv, x), x_sides(u1, x, cx),
                row, count, side_cells,
            )

    second(0)
    sweep(1, cx - 1, second)
    second(cx - 1)


def join_two_kernel(
    c, inv, own_a, own_b, near_a, near_b, wall_prior, u1, u2_in, u2, pay_a, pay_b
):
    cx, side_cells = c.shape[0], c.shape[1]
    for side, (own, near, pay) in enumerate(((own_a, near_a, pay_a), (own_b, near_b, pay_b))):
        x0, x1 = (end_layer(own_parity(), side, k, cx) for k in range(2))
        for row, count in chunks(side_cells):
            at = pl.ds(row, count)
            value = u2[x0, at, :] + own[at, :] * near[at, :]
            u2[x0, at, :] = value
            pay[at, :] = value
        pay[2 * side_cells : 2 * side_cells + 4, :] = wall_prior[4 * side : 4 * side + 4, :]
        pay[2 * side_cells + 4 : 2 * side_cells + 8, :] = jnp.zeros((4, side_cells), F32)
        for row, count in chunks(side_cells):
            pay[pl.ds(side_cells + row, count), :] = forward(
                flat(pay, 0), layer(u1, x0), layer(c, x0), layer(inv, x0), [layer(u2, x1)],
                row, count, side_cells,
            )


def join_forward(x0, x1, edge, mid, last, c, inv, got_now, got_part, got_b, b, halo, delta, side_cells):
    for row, count in chunks(side_cells):
        at = pl.ds(row, count)
        change = b(row, count) * got_now(row, count)
        delta[at, :] = change
        mid[x0, at, :] += change
        halo[at, :] = got_part(row, count) + got_b(row, count) * edge(row, count)
        last[x1, at, :] += (c[x1, at, :] * inv[x1, at, :]) * change
    for row, count in chunks(side_cells):
        at = pl.ds(row, count)
        v, total = beside(flat(delta, 0), row, count, side_cells)
        last[x0, at, :] += (2.0 * inv[x0, at, :]) * v + b(row, count) * (
            total - 6.0 * v + halo[at, :]
        )


def ahead_again_kernel(u1, u2, c, inv, u1h_a, u1h_b, u3, u4, energy, wall_now, columns):
    cx, side_cells = u1.shape[0], u1.shape[1]
    for side, u1h in enumerate((u1h_a, u1h_b)):
        wall_now[4 * side : 4 * side + 4, :] = wall_rows(
            lambda at, lanes, u1h=u1h: u1h[at, lanes], columns, side_cells
        )
    energy[...] = jnp.zeros_like(energy)

    def first(x, inner):
        sums = [jnp.zeros((8, side_cells), F32)] * 3
        for row, count in chunks(side_cells):
            value = forward(
                layer(u2, x), layer(u1, x), layer(c, x), layer(inv, x), x_sides(u2, x, cx),
                row, count, side_cells,
            )
            u3[x, pl.ds(row, count), :] = value
            sums[0] = sums[0] + fold(u1[x, pl.ds(row, count), :] ** 2)
            sums[1] = sums[1] + fold(u2[x, pl.ds(row, count), :] ** 2)
            sums[2] = sums[2] + fold(value * value)
        for k in range(3 if inner else 2):
            energy[k] += sums[k]

    def second(x, inner):
        total = jnp.zeros((8, side_cells), F32)
        for row, count in chunks(side_cells):
            value = forward(
                layer(u3, x), layer(u2, x), layer(c, x), layer(inv, x), x_sides(u3, x, cx),
                row, count, side_cells,
            )
            u4[x, pl.ds(row, count), :] = value
            total = total + fold(value * value)
        if inner:
            energy[3] += total

    first(0, False)
    sweep(1, cx - 1, lambda x: first(x, True))
    first(cx - 1, False)
    second(0, False)
    second(1, False)
    sweep(2, cx - 2, lambda x: second(x, True))
    second(cx - 2, False)
    second(cx - 1, False)


def join_second_kernel(
    c, inv, energy, edge_a, edge_b, own_a, own_b, got_a, got_b, b_a, b_b, u3_in, u4_in,
    u3, u4, halo_a, halo_b, pay_a, pay_b, energy_rows, delta,
):
    cx, side_cells = c.shape[0], c.shape[1]
    third = energy[2]
    fourth = energy[3]
    for side, (edge, own, got, gb, halo, pay) in enumerate(
        ((edge_a, own_a, got_a, b_a, halo_a, pay_a), (edge_b, own_b, got_b, b_b, halo_b, pay_b))
    ):
        x0, x1 = (end_layer(own_parity(), side, k, cx) for k in range(2))
        b = flat(own, 0)
        join_forward(
            x0, x1, flat(edge, 0), u3, u4, c, inv, flat(got, 0), flat(got, side_cells),
            flat(gb, 0), b, halo, delta, side_cells,
        )
        for row, count in chunks(side_cells):
            at = pl.ds(row, count)
            value, other = u4[x0, at, :], u4[x1, at, :]
            pay[at, :] = 2.0 * b(row, count) * value
            third = third + fold(u3[x0, at, :] ** 2)
            fourth = fourth + fold(value * value + other * other)
        for row, count in chunks(side_cells):
            at = pl.ds(row, count)
            q, total = beside(flat(pay, 0), row, count, side_cells)
            total = total + 2.0 * (c[x1, at, :] * inv[x1, at, :]) * u4[x1, at, :]
            pay[pl.ds(side_cells + row, count), :] = b(row, count) * (
                4.0 * (inv[x0, at, :] * u4[x0, at, :]) + total - 6.0 * q
            )
    lane = lax.broadcasted_iota(jnp.int32, energy_rows.shape, 1)
    rows = jnp.zeros(energy_rows.shape, F32)
    for n, part in enumerate((energy[0], energy[1], third, fourth)):
        total = jnp.sum(jnp.sum(part, axis=0, keepdims=True), axis=1, keepdims=True)
        rows = jnp.where(lane == n, total, rows)
    energy_rows[...] = rows


def adjoint_free_kernel(u4, c, inv, w4, w3, q4):
    cx, side_cells = u4.shape[0], u4.shape[1]

    def zeroth(x):
        for row, count in chunks(side_cells):
            at = pl.ds(row, count)
            value = 2.0 * (inv[x, at, :] * u4[x, at, :])
            w4[x, at, :] = value
            q4[x, at, :] = c[x, at, :] * value

    def first(x):
        for row, count in chunks(side_cells):
            at = pl.ds(row, count)
            w3[x, at, :] = backward(
                layer(q4, x), w4[x, at, :], None, layer(inv, x), 0.0,
                x_sides(q4, x, cx), row, count, side_cells,
            )

    sweep(0, cx, zeroth)
    first(0)
    sweep(1, cx - 1, first)
    first(cx - 1)


def adjoint_kernel(
    all_cells, params, sums, u2, u3, c, inv, w4_in, w3_in, weights, w4, w3, w2, q2, q3
):
    cx, side_cells = u2.shape[0], u2.shape[1]
    totals = jnp.sum(sums[...], axis=0, keepdims=True) / all_cells
    lane = lax.broadcasted_iota(jnp.int32, totals.shape, 1)
    weight = jnp.zeros((1, 1), F32)
    for n in range(STEPS):
        rest = jnp.where(jnp.logical_and(lane >= n, lane < STEPS), totals, 0.0)
        schroeder = params[0:1, STEPS : STEPS + 1] + jnp.sum(rest, axis=1, keepdims=True)
        weight = weight + 2.0 * (jnp.log(schroeder) - params[0:1, n : n + 1]) / schroeder
        weights[8 * n : 8 * n + 8, :] = jnp.broadcast_to(2.0 * weight, (8, side_cells))

    def first(x):
        for row, count in chunks(side_cells):
            at = pl.ds(row, count)
            g3 = 0.5 * spread_weight(weights, 3, count)
            w4[x, at, :] = g3 * w4[x, at, :]
            value = g3 * w3[x, at, :] + spread_weight(weights, 2, count) * (
                inv[x, at, :] * u3[x, at, :]
            )
            w3[x, at, :] = value
            q3[x, at, :] = c[x, at, :] * value

    def second(x):
        for row, count in chunks(side_cells):
            at = pl.ds(row, count)
            value = backward(
                layer(q3, x), w3[x, at, :], w4[x, at, :], layer(inv, x),
                spread_weight(weights, 1, count) * u2[x, at, :],
                x_sides(q3, x, cx), row, count, side_cells,
            )
            w2[x, at, :] = value
            q2[x, at, :] = c[x, at, :] * value

    sweep(0, cx, first)
    second(0)
    sweep(1, cx - 1, second)
    second(cx - 1)


def join_third_kernel(
    weights, u1, c, inv, u3h_a, u3h_b, own_a, own_b, got_a, got_b, b_a, b_b,
    w3_in, w2_in, q2_in,
    w3, w2, q2, pay_a, pay_b, halo, delta,
):
    cx, side_cells = c.shape[0], c.shape[1]
    g = [spread_weight(weights, n, CHUNK) for n in range(STEPS)]
    for side, (u3h, own, got, b, pay) in enumerate(
        ((u3h_a, own_a, got_a, b_a, pay_a), (u3h_b, own_b, got_b, b_b, pay_b))
    ):
        x0, x1 = (end_layer(own_parity(), side, k, cx) for k in range(2))
        for row, count in chunks(side_cells):
            at, below = pl.ds(row, count), pl.ds(side_cells + row, count)
            change = (0.5 * g[3]) * (inv[x0, at, :] * got[at, :])
            w3[x0, at, :] += change
            change = c[x0, at, :] * change
            delta[at, :] = change
            bh = b[at, :]
            halo[at, :] = (0.5 * g[3]) * (got[below, :] + bh * own[at, :]) + g[2] * (bh * u3h[at, :])
            value = w2[x1, at, :] + inv[x1, at, :] * change
            w2[x1, at, :] = value
            q2[x1, at, :] = c[x1, at, :] * value
        for row, count in chunks(side_cells):
            at = pl.ds(row, count)
            v, total = beside(flat(delta, 0), row, count, side_cells)
            i = inv[x0, at, :]
            value = w2[x0, at, :] + i * (
                g[3] * (i * got[at, :]) + total - 6.0 * v + halo[at, :]
            )
            w2[x0, at, :] = value
            value = c[x0, at, :] * value
            q2[x0, at, :] = value
            pay[at, :] = value
        for row, count in chunks(side_cells):
            at = pl.ds(row, count)
            pay[pl.ds(side_cells + row, count), :] = c[x0, at, :] * backward(
                flat(pay, 0), w2[x0, at, :], w3[x0, at, :], layer(inv, x0),
                g[0] * u1[x0, at, :], [layer(q2, x1)], row, count, side_cells,
            )


def result_kernel(w1, q1, w2, s, dealt, cur_hbm, prev_hbm, cur_ends, mine, cur, prev, sems):
    cx, side_cells = w1.shape[0], w1.shape[1]
    mine[...] = jnp.sum(dealt[...], axis=0, keepdims=True) / float(PATCH_CELLS)

    def send_cur(x):
        return pltpu.make_async_copy(cur.at[x], cur_hbm.at[x], sems.at[0, x])

    def send_prev(x):
        return pltpu.make_async_copy(prev.at[x], prev_hbm.at[x], sems.at[1, x])

    def turn(x, ends=None):
        for row, count in chunks(side_cells):
            at = pl.ds(row, count)
            q, total = beside(layer(q1, x), row, count, side_cells)
            for other in x_sides(q1, x, cx):
                total = total + other(row, count)
            w, keep = w1[x, at, :], s[x, at, :] - 1.0
            value = 2.0 * w + total - 6.0 * q + keep * w2[x, at, :]
            if ends is None:
                cur[x, at, :] = value
            else:
                cur_ends[ends, at, :] = value
            prev[x, at, :] = keep * w
        if ends is None:
            send_cur(x).start()
        if ends in (None, 1, 2):
            send_prev(x).start()

    turn(1, 1)
    turn(cx - 2, 2)
    sweep(2, cx - 2, turn)
    turn(0, 0)
    turn(cx - 1, 3)
    sweep(1, cx - 1, lambda x: send_prev(x).wait())
    sweep(2, cx - 2, lambda x: send_cur(x).wait())


def adjoint_end_kernel(weights, u1, w2, w3, q2, c, inv, w1, q1):
    cx, side_cells = u1.shape[0], u1.shape[1]
    g0 = spread_weight(weights, 0, CHUNK)

    def first(x):
        for row, count in chunks(side_cells):
            at = pl.ds(row, count)
            value = backward(
                layer(q2, x), w2[x, at, :], w3[x, at, :], layer(inv, x), g0 * u1[x, at, :],
                x_sides(q2, x, cx), row, count, side_cells,
            )
            w1[x, at, :] = value
            q1[x, at, :] = c[x, at, :] * value

    first(0)
    sweep(1, cx - 1, first)
    first(cx - 1)


def patch_kernel(
    own, maps, wall_gain, wall_now, got_a, got_b, up, u, u1, u2, u3, u4, w4, w3, w2, w1, q2,
    sums, values, columns, totals,
):
    cx, side_cells = u.shape[0], u.shape[1]
    last = side_cells - 1
    ends = [end_layer(own_parity(), side, 0, cx) for side in range(2)]

    def field(x, at, lanes):
        k = (x, at, lanes)
        return (
            w4[k] * (u2[k] - u4[k])
            + w3[k] * (u1[k] - u3[k])
            + (w2[k] * (u[k] - u2[k]) + w1[k] * (up[k] - u1[k]))
        )

    everything = pl.ds(0, side_cells)
    low, high = pl.ds(0, LANES), pl.ds(side_cells - LANES, LANES)
    for x in range(cx):
        values[4 * x : 4 * x + 1, :] = field(x, pl.ds(0, 8), everything)[0:1]
        values[4 * x + 1 : 4 * x + 2, :] = field(x, pl.ds(last - 7, 8), everything)[7:8]
    base = 2 * cx
    tall = 2 * CHUNK
    spot = lax.broadcasted_iota(jnp.int32, (tall, LANES), 1)

    def gather(k, carry):
        at = pl.ds(pl.multiple_of(k * tall, tall), tall)
        total = jnp.zeros((tall, LANES), F32)
        for x in range(cx):
            for j, (lanes, lane_from) in enumerate(((low, 0), (high, LANES - 1))):
                tile = to_lane(field(x, at, lanes), 2 * x + j, lane_from)
                total = jnp.where(spot == 2 * x + j, tile, total)
        for side in range(2):
            for j, (lanes, lane_from) in enumerate(((low, 0), (high, LANES - 1))):
                place = base + 2 * side + j
                total = jnp.where(
                    spot == place, to_lane(q2[ends[side], at, lanes], place, lane_from), total
                )
        columns[at, :] = total
        return carry

    lax.fori_loop(0, side_cells // tall, gather, 0)
    rows = jnp.transpose(columns[...])
    for x in range(cx):
        values[4 * x + 2 : 4 * x + 4, :] = rows[2 * x : 2 * x + 2, :]
    for side in range(2):
        at, place = base + 2 * side, 4 * (cx + side)
        theirs = jnp.concatenate(
            [q2[ends[side], 0:1, :], q2[ends[side], last : last + 1, :], rows[at : at + 2, :]], axis=0
        )
        faces = slice(4 * side, 4 * side + 4)
        prior = (got_a, got_b)[side][2 * side_cells : 2 * side_cells + 4, :]
        values[place : place + 4, :] = theirs * (wall_gain[faces, :] * (prior - wall_now[faces, :]))
    all_maps, all_values = maps[...], values[...]

    def patch(k, carry):
        for m in range(GROUP // 8):
            block = []
            for j in range(8):
                picked = fold(jnp.where(all_maps == GROUP * k + 8 * m + j, all_values, 0.0))
                half = picked[:, :LANES]
                for first in range(LANES, side_cells, LANES):
                    half = half + picked[:, first : first + LANES]
                block.append(jnp.sum(half, axis=0, keepdims=True))
            total = jnp.sum(jnp.concatenate(block, axis=0), axis=1, keepdims=True)
            totals[pl.ds(pl.multiple_of(GROUP * k + 8 * m, 8), 8), :] = jnp.broadcast_to(
                total, (8, LANES)
            )
        return carry

    totals[totals.shape[0] - LANES :, :] = jnp.zeros((LANES, LANES), F32)
    lax.fori_loop(0, (totals.shape[0] - LANES) // GROUP, patch, 0)
    tall = -(-own // 8) * 8
    sub = lax.broadcasted_iota(jnp.int32, (tall, LANES), 0)
    diagonal = sub == lax.broadcasted_iota(jnp.int32, (tall, LANES), 1)

    def owner(d, carry):
        mine = jnp.where(diagonal, totals[pl.ds(d * own, tall), :], 0.0)
        sums[pl.ds(d, 1), :] = jnp.sum(mine, axis=0, keepdims=True)
        return carry

    lax.fori_loop(0, sums.shape[0], owner, 0, unroll=8)


def join_last_kernel(
    w1, q2, c, inv, s, got_a, got_b, b_a, b_b, cur_ends, cur_in, prev_in,
    cur_hbm, prev_hbm, delta, cur, prev, sems,
):
    cx, side_cells = w1.shape[0], w1.shape[1]
    copies = []

    def send(src, dst, x):
        copies.append(pltpu.make_async_copy(src, dst.at[x], sems.at[len(copies)]))
        copies[-1].start()

    for side, (got, b) in enumerate(((got_a, b_a), (got_b, b_b))):
        x0, x1 = (end_layer(own_parity(), side, k, cx) for k in range(2))
        e0, e1 = (end_layer(own_parity(), side, k, 4) for k in range(2))
        for row, count in chunks(side_cells):
            at = pl.ds(row, count)
            change = inv[x0, at, :] * got[at, :]
            prev[side, at, :] = (s[x0, at, :] - 1.0) * (w1[x0, at, :] + change)
            change = c[x0, at, :] * change
            delta[at, :] = change
            cur[2 * side + 1, at, :] = cur_ends[e1, at, :] + change
        send(prev.at[side], prev_hbm, x0)
        send(cur.at[2 * side + 1], cur_hbm, x1)
        for row, count in chunks(side_cells):
            at, below = pl.ds(row, count), pl.ds(side_cells + row, count)
            v, total = beside(flat(delta, 0), row, count, side_cells)
            cur[2 * side, at, :] = (
                cur_ends[e0, at, :]
                + 2.0 * (inv[x0, at, :] * got[at, :])
                + (total - 6.0 * v)
                + (got[below, :] + b[at, :] * q2[x0, at, :])
            )
        send(cur.at[2 * side], cur_hbm, x0)
    for copy in copies:
        copy.wait()


def call(kernel, ins, outs, scratch=(), aliases=None, name=None, us=2.0):
    kinds = {"v": in_vmem, "s": in_smem, "h": in_hbm}
    return pl.pallas_call(
        kernel,
        out_shape=[
            (pltpu.VMEM if kind == "v" else pltpu.HBM)(shape, *(dtype or [F32]))
            for kind, shape, *dtype in outs
        ],
        in_specs=[kinds[kind] for kind, _ in ins],
        out_specs=[kinds[kind] for kind, *_ in outs],
        scratch_shapes=list(scratch),
        input_output_aliases=aliases or {},
        compiler_params=pltpu.CompilerParams(vmem_limit_bytes=12 * 2**20),
        cost_estimate=pl.CostEstimate(flops=0, transcendentals=0, bytes_accessed=int(us * 3.0e6)),
        name=name,
    )(*[value for _, value in ins])


def on_device(u_prev, u_cur, courant_sq, patch_map, absorb, checkpoint, target_curve, tail_energy):
    cx, side = u_cur.shape[0], u_cur.shape[1]
    count = lax.axis_size("gx")
    patches = absorb.shape[0]
    own = patches // count
    all_cells = float(cx * count * side * side)
    field, plane = (cx, side, side), (side, side)
    double, tall = (2 * side, side), (side + 8, side)
    within = [(i, i ^ 1) for i in range(count)]
    across = [(i, i + 1) for i in range(1, count - 1, 2)]
    across = across + [(j, i) for i, j in across]

    def swap(a, b):
        a = lax.ppermute(a, "gx", within)
        return a, lax.ppermute(b, "gx", across)

    def deal(rows):
        return lax.all_to_all(rows, "gx", 0, 0, tiled=True)

    dma = pltpu.SemaphoreType.DMA
    ab = ("s", absorb)
    v = lambda *arrays: [("v", a) for a in arrays]
    small = (checkpoint.reshape(1, 1), target_curve.reshape(1, -1), tail_energy.reshape(1, 1))
    raw = [
        ("h", pltpu.with_memory_space_constraint(a, pltpu.HBM))
        for a in (patch_map, u_cur, u_prev, courant_sq)
    ]
    c_a, u_b, c_b = call(
        start_kernel,
        [raw[0], raw[1], raw[3]],
        [("v", (2 * side + 8, side)), ("v", plane), ("v", tall)],
        [VMEM((2, 4, side), jnp.int32), dma((3, 2))],
        name="edges",
        us=1.0,
    )
    near_a = lax.ppermute(c_a, "gx", within)
    near = (near_a, lax.ppermute(u_b, "gx", across))
    got_c = (near_a, lax.ppermute(c_b, "gx", across))
    u, up, c, s, inv, u1, params, own_maps = call(
        ahead_one_kernel,
        [ab] + v(*small) + raw,
        [("v", field)] * 6 + [("v", (8, LANES)), ("v", (cx, 4, side), jnp.int32)],
        [
            VMEM((4 * cx, side), jnp.int32),
            VMEM((4 * cx, side), F32),
            VMEM((LANES, side), F32),
            VMEM((side, LANES), F32),
            VMEM((side, LANES), F32),
            dma((4,)),
        ],
        name="forward_1",
        us=6.0,
    )
    u1, *edge_1 = call(
        join_one_kernel,
        v(c, inv, *near, u1),
        [("v", field)] + [("v", plane)] * 2,
        aliases={4: 0},
        name="edges_1",
        us=0.5,
    )
    u1h_a, u1h_b = near = swap(*edge_1)
    u2, *own_b, b_a, b_b, maps, wall_gain, wall_prior = call(
        ahead_two_kernel,
        [ab] + v(own_maps, u, up, c, inv, u1, *got_c),
        [("v", field)]
        + [("v", plane)] * 4
        + [("v", (4 * cx + 8, side), jnp.int32), ("v", (8, side)), ("v", (8, side))],
        [VMEM((side, LANES), F32), VMEM((side, LANES), F32), VMEM((LANES, side), F32)],
        name="forward_2",
        us=3.5,
    )
    got_b = (b_a, b_b)
    u2, *edge_2 = call(
        join_two_kernel,
        v(c, inv, *own_b, *near, wall_prior, u1, u2),
        [("v", field)] + [("v", (2 * side + 8, side))] * 2,
        aliases={8: 0},
        name="edges_2",
        us=0.8,
    )
    second = swap(*edge_2)
    u3, u4, energy, wall_now = call(
        ahead_again_kernel,
        v(u1, u2, c, inv, u1h_a, u1h_b),
        [("v", field)] * 2 + [("v", (STEPS, 8, side)), ("v", (8, side))],
        [VMEM((side, LANES), F32)],
        name="forward_3_4",
        us=5.5,
    )
    u3, u4, u3h_a, u3h_b, *edge_4, energy_rows = call(
        join_second_kernel,
        v(c, inv, energy, *edge_2, *own_b, *second, *got_b, u3, u4),
        [("v", field)] * 2 + [("v", plane)] * 2 + [("v", double)] * 2 + [("v", (count, LANES))],
        [VMEM(plane, F32)],
        aliases={11: 0, 12: 1},
        name="edges_3_4",
    )
    third = swap(*edge_4)
    w4, w3 = call(
        adjoint_free_kernel,
        v(u4, c, inv),
        [("v", field)] * 2,
        [VMEM(field, F32)],
        name="adjoint_3",
        us=2.6,
    )
    energy_rows, w4, w3 = lax.optimization_barrier((energy_rows, w4, w3))
    sums = deal(energy_rows)
    weights, w4, w3, w2, q2 = call(
        functools.partial(adjoint_kernel, all_cells),
        v(params, sums, u2, u3, c, inv, w4, w3),
        [("v", (8 * STEPS, side))] + [("v", field)] * 4,
        [VMEM(field, F32)],
        aliases={6: 1, 7: 2},
        name="adjoint_2",
        us=3.0,
    )
    w3, w2, q2, *edge_2 = call(
        join_third_kernel,
        v(weights, u1, c, inv, u3h_a, u3h_b, *edge_4, *third, *got_b, w3, w2, q2),
        [("v", field)] * 3 + [("v", double)] * 2,
        [VMEM(plane, F32), VMEM(plane, F32)],
        aliases={12: 0, 13: 1, 14: 2},
        name="edges_adjoint_3_2",
    )
    fourth = swap(*edge_2)
    w1, q1 = call(
        adjoint_end_kernel, v(weights, u1, w2, w3, q2, c, inv), [("v", field)] * 2, name="adjoint_1"
    )
    (partial,) = call(
        functools.partial(patch_kernel, own),
        v(maps, wall_gain, wall_now, *second, up, u, u1, u2, u3, u4, w4, w3, w2, w1, q2),
        [("v", (count, LANES))],
        [
            VMEM((4 * cx + 8, side), F32),
            VMEM((side, LANES), F32),
            VMEM((-(-patches // GROUP) * GROUP + LANES, LANES), F32),
        ],
        name="patch_sums",
    )
    cur, prev, cur_ends, mine = call(
        result_kernel,
        v(w1, q1, w2, s, deal(partial)),
        [("h", field)] * 2 + [("v", (4, side, side)), ("v", (1, LANES))],
        [VMEM(field, F32), VMEM(field, F32), dma((2, cx))],
        name="adjoint_0",
    )
    grad_absorb = mine[0, :own]
    cur, prev = call(
        join_last_kernel,
        v(w1, q2, c, inv, s, *fourth, *got_b, cur_ends) + [("h", cur), ("h", prev)],
        [("h", field)] * 2,
        [VMEM(plane, F32), VMEM((4, side, side), F32), VMEM((2, side, side), F32), dma((6,))],
        aliases={10: 0, 11: 1},
        name="edges_adjoint_1_0",
    )
    return prev, cur, grad_absorb


def solution(mesh):
    bricks = P(("groups", "gx"), None, None)
    return jax.shard_map(
        on_device,
        mesh=mesh,
        in_specs=(bricks, bricks, bricks, bricks, P("groups"), P("groups"), P("groups"), P("groups")),
        out_specs=(bricks, bricks, P(("groups", "gx"))),
        check_vma=False,
    )
```

```python
import functools

import jax
import jax.numpy as jnp
from jax import lax
from jax.experimental import pallas as pl
from jax.experimental.pallas import tpu as pltpu
from jax.sharding import PartitionSpec as P

STEPS = 4
PATCH_CELLS = 819
CHUNK = 16
LANES = 128
GROUP = 160
F32 = jnp.float32
VMEM = pltpu.VMEM
in_vmem = pl.BlockSpec(memory_space=pltpu.VMEM)
in_smem = pl.BlockSpec(memory_space=pltpu.SMEM)
in_hbm = pl.BlockSpec(memory_space=pltpu.HBM)


def end_layer(parity, side, depth, cx):
    high = 1 - parity if side == 0 else parity
    return high * (cx - 1 - depth) + (1 - high) * depth


def own_parity():
    return lax.rem(lax.axis_index("gx"), 2)


def layer(ref, x):
    return lambda row, count: ref[x, pl.ds(row, count), :]


def flat(ref, base):
    return lambda row, count: ref[pl.ds(base + row, count), :]


def chunks(side_cells):
    return [(row, CHUNK) for row in range(0, side_cells, CHUNK)]


def beside(field, row, count, side_cells):
    v = field(row, count)
    tiles = [v[k : k + 8] for k in range(0, count, 8)]
    sub = lax.broadcasted_iota(jnp.int32, tiles[0].shape, 0)
    zero = jnp.zeros_like(tiles[0])
    before = pltpu.roll(field(row - 8, 8), 1, 0) if row else zero
    after = pltpu.roll(field(row + count, 8), 7, 0) if row + count < side_cells else zero
    down = [before] + [pltpu.roll(tile, 1, 0) for tile in tiles]
    up = [pltpu.roll(tile, 7, 0) for tile in tiles] + [after]
    total = jnp.concatenate(
        [
            jnp.where(sub == 0, down[k], down[k + 1]) + jnp.where(sub == 7, up[k + 1], up[k])
            for k in range(len(tiles))
        ],
        axis=0,
    )
    parts = [v[:, k : k + LANES] for k in range(0, side_cells, LANES)]
    lane = lax.broadcasted_iota(jnp.int32, parts[0].shape, 1)
    zero = jnp.zeros_like(parts[0])
    right = [zero] + [pltpu.roll(part, 1, 1) for part in parts]
    left = [pltpu.roll(part, LANES - 1, 1) for part in parts] + [zero]
    across = jnp.concatenate(
        [
            jnp.where(lane == 0, right[k], right[k + 1])
            + jnp.where(lane == LANES - 1, left[k + 1], left[k])
            for k in range(len(parts))
        ],
        axis=1,
    )
    return v, total + across


def forward(now, prior, courant, inverse, sides, row, count, side_cells):
    v, total = beside(now, row, count, side_cells)
    for other in sides:
        total = total + other(row, count)
    p = prior(row, count)
    c, i = courant(row, count), inverse(row, count)
    return i * (2.0 * (v - p) + c * (total - 6.0 * v)) + p


def backward(product, w, later, inverse, source, sides, row, count, side_cells):
    q, total = beside(product, row, count, side_cells)
    for other in sides:
        total = total + other(row, count)
    fresh = total - 6.0 * q + source
    i = inverse(row, count)
    if later is None:
        return i * (2.0 * w + fresh)
    return i * (2.0 * (w - later) + fresh) + later


def sweep(low, high, body):
    def turn(x, carry):
        body(x)
        return carry

    lax.fori_loop(low, high, turn, 0)


def x_sides(ref, x, cx):
    return [layer(ref, k) for k in (x - 1, x + 1) if not isinstance(k, int) or 0 <= k < cx]


def fold(values):
    total = values[0:8]
    for row in range(8, values.shape[0], 8):
        total = total + values[row : row + 8]
    return total


def spread_weight(weights, n, count):
    tile = weights[8 * n : 8 * n + 8, :]
    return jnp.concatenate([tile] * (count // 8), axis=0)


def start_kernel(map_hbm, u_hbm, c_hbm, c_a, u_b, c_b, maps, sems):
    cx, side_cells = u_hbm.shape[0], u_hbm.shape[1]
    copies = []
    ends = [end_layer(own_parity(), side, 0, cx) for side in range(2)]
    u_a = c_a.at[pl.ds(side_cells + 8, side_cells)]
    for side, (u, c) in enumerate(((u_a, c_a), (u_b, c_b))):
        x0 = ends[side]
        for k, (src, dst) in enumerate(
            ((map_hbm, maps.at[side]), (u_hbm, u), (c_hbm, c.at[pl.ds(0, side_cells)]))
        ):
            copies.append(pltpu.make_async_copy(src.at[x0], dst, sems.at[k, side]))
    for copy in copies:
        copy.start()
    for side, c in enumerate((c_a, c_b)):
        copies[3 * side].wait()
        c[side_cells : side_cells + 4, :] = maps[side].astype(F32)
        c[side_cells + 4 : side_cells + 8, :] = jnp.zeros((4, side_cells), F32)
    for k, copy in enumerate(copies):
        if k % 3:
            copy.wait()


def lookup(maps, absorb_ref):
    def turn(p, got):
        return jnp.where(maps == p, absorb_ref[p], got)

    return lax.fori_loop(0, absorb_ref.shape[0], turn, jnp.zeros(maps.shape, F32), unroll=8)


def to_lane(tile, spot, lane_from):
    return pltpu.roll(tile, (spot - lane_from) % LANES, 1)


def wall_fields(columns, gains, low, high, top, bottom, row, count, side_cells):
    lane = lax.broadcasted_iota(jnp.int32, (count, LANES), 1)

    def place(ref, other):
        tile = ref[pl.ds(row, count), :]
        near = pltpu.roll(tile, lax.rem(LANES - low, LANES), 1)
        far = pltpu.roll(tile, LANES - 1 - high, 1)
        mid = [jnp.full((count, LANES), other, F32)] * (side_cells // LANES - 2)
        return jnp.concatenate(
            [
                jnp.where(lane == 0, near, other),
                *mid,
                jnp.where(lane == LANES - 1, far, other),
            ],
            axis=1,
        )

    field = place(columns, 0.0)
    if 0 < row and row + count < side_cells:
        return field, place(gains, 1.0)
    sub = lax.broadcasted_iota(jnp.int32, field.shape, 0)
    if row == 0:
        field = field + jnp.where(sub == 0, top, 0.0)
    if row + count == side_cells:
        field = field + jnp.where(sub == count - 1, bottom, 0.0)
    return field, 1.0 / (1.0 + field)


def ahead_one_kernel(
    absorb_ref, checkpoint, target, tail, map_hbm, u_hbm, up_hbm, c_hbm,
    u, up, c, s, inv, u1, params, map_ref,
    maps, found, turned, columns, gains, sems,
):
    cx, side_cells = u.shape[0], u.shape[1]
    copies = [
        pltpu.make_async_copy(src, dst, sems.at[k])
        for k, (src, dst) in enumerate(
            ((map_hbm, map_ref), (u_hbm, u), (up_hbm, up), (c_hbm, c))
        )
    ]
    for copy in copies:
        copy.start()
    copies[0].wait()
    for x in range(cx):
        maps[4 * x : 4 * x + 4, :] = map_ref[x]
    found[...] = lookup(maps[...], absorb_ref)
    turned[...] = jnp.zeros_like(turned)
    for x in range(cx):
        turned[x : x + 1, :] = found[4 * x + 2 : 4 * x + 3, :]
        turned[cx + x : cx + x + 1, :] = found[4 * x + 3 : 4 * x + 4, :]
    columns[...] = jnp.transpose(turned[...])
    gains[...] = 1.0 / (1.0 + columns[...])

    def spread(x):
        for row, count in chunks(side_cells):
            at = pl.ds(row, count)
            field, gain = wall_fields(
                columns, gains, x, cx + x, found[pl.ds(4 * x, 1), :], found[pl.ds(4 * x + 1, 1), :],
                row, count, side_cells,
            )
            s[x, at, :] = field
            inv[x, at, :] = gain

    def first(x):
        for row, count in chunks(side_cells):
            u1[x, pl.ds(row, count), :] = forward(
                layer(u, x), layer(up, x), layer(c, x), layer(inv, x), x_sides(u, x, cx),
                row, count, side_cells,
            )

    sweep(0, cx, spread)
    for copy in copies[1:]:
        copy.wait()
    history = target.shape[1]
    lane = lax.broadcasted_iota(jnp.int32, params.shape, 1)
    spot = lax.broadcasted_iota(jnp.int32, target.shape, 1)
    start = jnp.clip(checkpoint[...], 0, history - STEPS)
    row = jnp.where(lane == STEPS, tail[...], 0.0)
    for n in range(STEPS):
        value = jnp.sum(jnp.where(spot == start + n, target[...], 0.0), axis=1, keepdims=True)
        row = jnp.where(lane == n, value, row)
    params[...] = row
    first(0)
    sweep(1, cx - 1, first)
    first(cx - 1)


def join_one_kernel(c, inv, near_a, near_b, u1_in, u1, edge_a, edge_b):
    cx, side_cells = c.shape[0], c.shape[1]
    near_a = near_a.at[pl.ds(side_cells + 8, side_cells)]
    for side, (near, edge) in enumerate(((near_a, edge_a), (near_b, edge_b))):
        x0 = end_layer(own_parity(), side, 0, cx)
        for row, count in chunks(side_cells):
            at = pl.ds(row, count)
            value = u1[x0, at, :] + (c[x0, at, :] * inv[x0, at, :]) * near[at, :]
            u1[x0, at, :] = value
            edge[at, :] = value


def wall_rows(plane, columns, side_cells):
    last = side_cells - 1
    spot = lax.broadcasted_iota(jnp.int32, (CHUNK, LANES), 1)
    low, high = pl.ds(0, LANES), pl.ds(side_cells - LANES, LANES)
    for row, count in chunks(side_cells):
        at = pl.ds(row, count)
        far = to_lane(plane(at, high), 1, LANES - 1)
        columns[at, :] = jnp.where(spot == 0, plane(at, low), jnp.where(spot == 1, far, 0.0))
    rows = jnp.transpose(columns[...])
    every = pl.ds(0, side_cells)
    return jnp.concatenate([plane(pl.ds(0, 1), every), plane(pl.ds(last, 1), every), rows[0:2]], axis=0)


def ahead_two_kernel(
    absorb_ref, map_ref, u, up, c, inv, u1, got_a, got_b,
    u2, own_a, own_b, b_a, b_b, maps, wall_gain, wall_prior, columns, gains, turned,
):
    cx, side_cells = u.shape[0], u.shape[1]
    last = side_cells - 1
    ends = [end_layer(own_parity(), side, 0, cx) for side in range(2)]
    for x in range(cx):
        maps[4 * x : 4 * x + 4, :] = map_ref[x]
    for side, got in enumerate((got_a, got_b)):
        maps[4 * (cx + side) : 4 * (cx + side) + 4, :] = got[
            side_cells : side_cells + 4, :
        ].astype(jnp.int32)
    damping = lookup(maps[4 * cx : 4 * cx + 8, :], absorb_ref)
    turned[...] = jnp.zeros_like(turned)
    for side in range(2):
        turned[2 * side : 2 * side + 2, :] = damping[4 * side + 2 : 4 * side + 4]
    columns[...] = jnp.transpose(turned[...])
    gains[...] = 1.0 / (1.0 + columns[...])
    lane = lax.broadcasted_iota(jnp.int32, (1, side_cells), 1)

    def corners(one, two):
        return jnp.where(lane == 0, one, 0.0) + jnp.where(lane == last, two, 0.0)

    for side, (got, own, b) in enumerate(((got_a, own_a, b_a), (got_b, own_b, b_b))):
        d = [damping[4 * side + f : 4 * side + f + 1] for f in range(4)]
        for row, count in chunks(side_cells):
            at = pl.ds(row, count)
            own[at, :] = c[ends[side], at, :] * inv[ends[side], at, :]
            _, gain = wall_fields(
                columns, gains, 2 * side, 2 * side + 1, d[0], d[1], row, count, side_cells
            )
            b[at, :] = got[at, :] * gain
        total = jnp.concatenate(
            [
                d[0] + corners(d[2][:, 0:1], d[3][:, 0:1]),
                d[1] + corners(d[2][:, last:], d[3][:, last:]),
                d[2] + corners(d[0][:, 0:1], d[1][:, 0:1]),
                d[3] + corners(d[0][:, last:], d[1][:, last:]),
            ],
            axis=0,
        )
        wall_gain[4 * side : 4 * side + 4, :] = 1.0 / (1.0 + total)
    for side in range(2):
        wall_prior[4 * side : 4 * side + 4, :] = wall_rows(
            lambda at, lanes, x=ends[side]: up[x, at, lanes], columns, side_cells
        )

    def second(x):
        for row, count in chunks(side_cells):
            u2[x, pl.ds(row, count), :] = forward(
                layer(u1, x), layer(u, x), layer(c, x), layer(inv, x), x_sides(u1, x, cx),
                row, count, side_cells,
            )

    second(0)
    sweep(1, cx - 1, second)
    second(cx - 1)


def join_two_kernel(side, c, inv, own, near, wall_prior, u1, u2_in, u2, pay):
    cx, side_cells = c.shape[0], c.shape[1]
    x0, x1 = (end_layer(own_parity(), side, k, cx) for k in range(2))
    for row, count in chunks(side_cells):
        at = pl.ds(row, count)
        value = u2[x0, at, :] + own[at, :] * near[at, :]
        u2[x0, at, :] = value
        pay[at, :] = value
    pay[2 * side_cells : 2 * side_cells + 4, :] = wall_prior[4 * side : 4 * side + 4, :]
    pay[2 * side_cells + 4 : 2 * side_cells + 8, :] = jnp.zeros((4, side_cells), F32)
    for row, count in chunks(side_cells):
        pay[pl.ds(side_cells + row, count), :] = forward(
            flat(pay, 0), layer(u1, x0), layer(c, x0), layer(inv, x0), [layer(u2, x1)],
            row, count, side_cells,
        )


def join_forward(x0, x1, edge, mid, last, c, inv, got_now, got_part, got_b, b, halo, delta, side_cells):
    for row, count in chunks(side_cells):
        at = pl.ds(row, count)
        change = b(row, count) * got_now(row, count)
        delta[at, :] = change
        mid[x0, at, :] += change
        halo[at, :] = got_part(row, count) + got_b(row, count) * edge(row, count)
        last[x1, at, :] += (c[x1, at, :] * inv[x1, at, :]) * change
    for row, count in chunks(side_cells):
        at = pl.ds(row, count)
        v, total = beside(flat(delta, 0), row, count, side_cells)
        last[x0, at, :] += (2.0 * inv[x0, at, :]) * v + b(row, count) * (
            total - 6.0 * v + halo[at, :]
        )


def ahead_again_kernel(u1, u2, c, inv, u1h_a, u1h_b, u3, u4, energy, wall_now, columns):
    cx, side_cells = u1.shape[0], u1.shape[1]
    for side, u1h in enumerate((u1h_a, u1h_b)):
        wall_now[4 * side : 4 * side + 4, :] = wall_rows(
            lambda at, lanes, u1h=u1h: u1h[at, lanes], columns, side_cells
        )
    energy[...] = jnp.zeros_like(energy)

    def first(x, inner):
        sums = [jnp.zeros((8, side_cells), F32)] * 3
        for row, count in chunks(side_cells):
            value = forward(
                layer(u2, x), layer(u1, x), layer(c, x), layer(inv, x), x_sides(u2, x, cx),
                row, count, side_cells,
            )
            u3[x, pl.ds(row, count), :] = value
            sums[0] = sums[0] + fold(u1[x, pl.ds(row, count), :] ** 2)
            sums[1] = sums[1] + fold(u2[x, pl.ds(row, count), :] ** 2)
            sums[2] = sums[2] + fold(value * value)
        for k in range(3 if inner else 2):
            energy[k] += sums[k]

    def second(x, inner):
        total = jnp.zeros((8, side_cells), F32)
        for row, count in chunks(side_cells):
            value = forward(
                layer(u3, x), layer(u2, x), layer(c, x), layer(inv, x), x_sides(u3, x, cx),
                row, count, side_cells,
            )
            u4[x, pl.ds(row, count), :] = value
            total = total + fold(value * value)
        if inner:
            energy[3] += total

    first(0, False)
    sweep(1, cx - 1, lambda x: first(x, True))
    first(cx - 1, False)
    second(0, False)
    second(1, False)
    sweep(2, cx - 2, lambda x: second(x, True))
    second(cx - 2, False)
    second(cx - 1, False)


def join_second_kernel(
    side, c, inv, energy_in, edge, own, got, gb, u3_in, u4_in, u3, u4, halo, pay, energy, delta
):
    cx, side_cells = c.shape[0], c.shape[1]
    third, fourth = energy_in[2], energy_in[3]
    x0, x1 = (end_layer(own_parity(), side, k, cx) for k in range(2))
    b = flat(own, 0)
    join_forward(
        x0, x1, flat(edge, 0), u3, u4, c, inv, flat(got, 0), flat(got, side_cells),
        flat(gb, 0), b, halo, delta, side_cells,
    )
    for row, count in chunks(side_cells):
        at = pl.ds(row, count)
        value, other = u4[x0, at, :], u4[x1, at, :]
        pay[at, :] = 2.0 * b(row, count) * value
        third = third + fold(u3[x0, at, :] ** 2)
        fourth = fourth + fold(value * value + other * other)
    for row, count in chunks(side_cells):
        at = pl.ds(row, count)
        q, total = beside(flat(pay, 0), row, count, side_cells)
        total = total + 2.0 * (c[x1, at, :] * inv[x1, at, :]) * u4[x1, at, :]
        pay[pl.ds(side_cells + row, count), :] = b(row, count) * (
            4.0 * (inv[x0, at, :] * u4[x0, at, :]) + total - 6.0 * q
        )
    parts = (energy_in[0], energy_in[1], third, fourth)
    if side == 0:
        for n, part in enumerate(parts):
            energy[n] = part
        return
    lane = lax.broadcasted_iota(jnp.int32, energy.shape, 1)
    rows = jnp.zeros(energy.shape, F32)
    for n, part in enumerate(parts):
        total = jnp.sum(jnp.sum(part, axis=0, keepdims=True), axis=1, keepdims=True)
        rows = jnp.where(lane == n, total, rows)
    energy[...] = rows


def adjoint_free_kernel(u4, c, inv, w4, w3, q4):
    cx, side_cells = u4.shape[0], u4.shape[1]

    def zeroth(x):
        for row, count in chunks(side_cells):
            at = pl.ds(row, count)
            value = 2.0 * (inv[x, at, :] * u4[x, at, :])
            w4[x, at, :] = value
            q4[x, at, :] = c[x, at, :] * value

    def first(x):
        for row, count in chunks(side_cells):
            at = pl.ds(row, count)
            w3[x, at, :] = backward(
                layer(q4, x), w4[x, at, :], None, layer(inv, x), 0.0,
                x_sides(q4, x, cx), row, count, side_cells,
            )

    sweep(0, cx, zeroth)
    first(0)
    sweep(1, cx - 1, first)
    first(cx - 1)


def adjoint_kernel(
    all_cells, params, sums, u2, u3, c, inv, w4_in, w3_in, weights, w4, w3, w2, q2, q3
):
    cx, side_cells = u2.shape[0], u2.shape[1]
    totals = jnp.sum(sums[...], axis=0, keepdims=True) / all_cells
    lane = lax.broadcasted_iota(jnp.int32, totals.shape, 1)
    weight = jnp.zeros((1, 1), F32)
    for n in range(STEPS):
        rest = jnp.where(jnp.logical_and(lane >= n, lane < STEPS), totals, 0.0)
        schroeder = params[0:1, STEPS : STEPS + 1] + jnp.sum(rest, axis=1, keepdims=True)
        weight = weight + 2.0 * (jnp.log(schroeder) - params[0:1, n : n + 1]) / schroeder
        weights[8 * n : 8 * n + 8, :] = jnp.broadcast_to(2.0 * weight, (8, side_cells))

    def first(x):
        for row, count in chunks(side_cells):
            at = pl.ds(row, count)
            g3 = 0.5 * spread_weight(weights, 3, count)
            w4[x, at, :] = g3 * w4[x, at, :]
            value = g3 * w3[x, at, :] + spread_weight(weights, 2, count) * (
                inv[x, at, :] * u3[x, at, :]
            )
            w3[x, at, :] = value
            q3[x, at, :] = c[x, at, :] * value

    def second(x):
        for row, count in chunks(side_cells):
            at = pl.ds(row, count)
            value = backward(
                layer(q3, x), w3[x, at, :], w4[x, at, :], layer(inv, x),
                spread_weight(weights, 1, count) * u2[x, at, :],
                x_sides(q3, x, cx), row, count, side_cells,
            )
            w2[x, at, :] = value
            q2[x, at, :] = c[x, at, :] * value

    sweep(0, cx, first)
    second(0)
    sweep(1, cx - 1, second)
    second(cx - 1)


def join_third_kernel(
    weights, u1, c, inv, u3h_a, u3h_b, own_a, own_b, got_a, got_b, b_a, b_b,
    w3_in, w2_in, q2_in,
    w3, w2, q2, pay_a, pay_b, halo, delta,
):
    cx, side_cells = c.shape[0], c.shape[1]
    g = [spread_weight(weights, n, CHUNK) for n in range(STEPS)]
    for side, (u3h, own, got, b, pay) in enumerate(
        ((u3h_a, own_a, got_a, b_a, pay_a), (u3h_b, own_b, got_b, b_b, pay_b))
    ):
        x0, x1 = (end_layer(own_parity(), side, k, cx) for k in range(2))
        for row, count in chunks(side_cells):
            at, below = pl.ds(row, count), pl.ds(side_cells + row, count)
            change = (0.5 * g[3]) * (inv[x0, at, :] * got[at, :])
            w3[x0, at, :] += change
            change = c[x0, at, :] * change
            delta[at, :] = change
            bh = b[at, :]
            halo[at, :] = (0.5 * g[3]) * (got[below, :] + bh * own[at, :]) + g[2] * (bh * u3h[at, :])
            value = w2[x1, at, :] + inv[x1, at, :] * change
            w2[x1, at, :] = value
            q2[x1, at, :] = c[x1, at, :] * value
        for row, count in chunks(side_cells):
            at = pl.ds(row, count)
            v, total = beside(flat(delta, 0), row, count, side_cells)
            i = inv[x0, at, :]
            value = w2[x0, at, :] + i * (
                g[3] * (i * got[at, :]) + total - 6.0 * v + halo[at, :]
            )
            w2[x0, at, :] = value
            value = c[x0, at, :] * value
            q2[x0, at, :] = value
            pay[at, :] = value
        for row, count in chunks(side_cells):
            at = pl.ds(row, count)
            pay[pl.ds(side_cells + row, count), :] = c[x0, at, :] * backward(
                flat(pay, 0), w2[x0, at, :], w3[x0, at, :], layer(inv, x0),
                g[0] * u1[x0, at, :], [layer(q2, x1)], row, count, side_cells,
            )


def result_kernel(w1, q1, w2, s, dealt, cur, mine):
    cx, side_cells = w1.shape[0], w1.shape[1]
    mine[...] = jnp.sum(dealt[...], axis=0, keepdims=True) / float(PATCH_CELLS)

    def turn(x):
        for row, count in chunks(side_cells):
            at = pl.ds(row, count)
            q, total = beside(layer(q1, x), row, count, side_cells)
            for other in x_sides(q1, x, cx):
                total = total + other(row, count)
            cur[x, at, :] = (
                2.0 * w1[x, at, :] + total - 6.0 * q + (s[x, at, :] - 1.0) * w2[x, at, :]
            )

    turn(0)
    sweep(1, cx - 1, turn)
    turn(cx - 1)


def adjoint_end_kernel(weights, u1, w2, w3, q2, c, inv, s, w1, q1, prev):
    cx, side_cells = u1.shape[0], u1.shape[1]
    g0 = spread_weight(weights, 0, CHUNK)

    def first(x):
        for row, count in chunks(side_cells):
            at = pl.ds(row, count)
            value = backward(
                layer(q2, x), w2[x, at, :], w3[x, at, :], layer(inv, x), g0 * u1[x, at, :],
                x_sides(q2, x, cx), row, count, side_cells,
            )
            w1[x, at, :] = value
            q1[x, at, :] = c[x, at, :] * value
            prev[x, at, :] = (s[x, at, :] - 1.0) * value

    first(0)
    sweep(1, cx - 1, first)
    first(cx - 1)


def patch_kernel(
    own, maps, wall_gain, wall_now, got_a, got_b, up, u, u1, u2, u3, u4, w4, w3, w2, w1, q2, prev,
    sums, prev_hbm, values, columns, totals, sem,
):
    cx, side_cells = u.shape[0], u.shape[1]
    last = side_cells - 1
    ends = [end_layer(own_parity(), side, 0, cx) for side in range(2)]
    inner = pl.ds(1, cx - 2)
    leave = pltpu.make_async_copy(prev.at[inner], prev_hbm.at[inner], sem)
    leave.start()

    def field(x, at, lanes):
        k = (x, at, lanes)
        return (
            w4[k] * (u2[k] - u4[k])
            + w3[k] * (u1[k] - u3[k])
            + (w2[k] * (u[k] - u2[k]) + w1[k] * (up[k] - u1[k]))
        )

    everything = pl.ds(0, side_cells)
    low, high = pl.ds(0, LANES), pl.ds(side_cells - LANES, LANES)
    for x in range(cx):
        values[4 * x : 4 * x + 1, :] = field(x, pl.ds(0, 8), everything)[0:1]
        values[4 * x + 1 : 4 * x + 2, :] = field(x, pl.ds(last - 7, 8), everything)[7:8]
    base = 2 * cx
    tall = 2 * CHUNK
    spot = lax.broadcasted_iota(jnp.int32, (tall, LANES), 1)

    def gather(k, carry):
        at = pl.ds(pl.multiple_of(k * tall, tall), tall)
        total = jnp.zeros((tall, LANES), F32)
        for x in range(cx):
            for j, (lanes, lane_from) in enumerate(((low, 0), (high, LANES - 1))):
                tile = to_lane(field(x, at, lanes), 2 * x + j, lane_from)
                total = jnp.where(spot == 2 * x + j, tile, total)
        for side in range(2):
            for j, (lanes, lane_from) in enumerate(((low, 0), (high, LANES - 1))):
                place = base + 2 * side + j
                total = jnp.where(
                    spot == place, to_lane(q2[ends[side], at, lanes], place, lane_from), total
                )
        columns[at, :] = total
        return carry

    lax.fori_loop(0, side_cells // tall, gather, 0)
    rows = jnp.transpose(columns[...])
    for x in range(cx):
        values[4 * x + 2 : 4 * x + 4, :] = rows[2 * x : 2 * x + 2, :]
    for side in range(2):
        at, place = base + 2 * side, 4 * (cx + side)
        theirs = jnp.concatenate(
            [q2[ends[side], 0:1, :], q2[ends[side], last : last + 1, :], rows[at : at + 2, :]], axis=0
        )
        faces = slice(4 * side, 4 * side + 4)
        prior = (got_a, got_b)[side][2 * side_cells : 2 * side_cells + 4, :]
        values[place : place + 4, :] = theirs * (wall_gain[faces, :] * (prior - wall_now[faces, :]))
    all_maps, all_values = maps[...], values[...]

    def patch(k, carry):
        for m in range(GROUP // 8):
            block = []
            for j in range(8):
                picked = fold(jnp.where(all_maps == GROUP * k + 8 * m + j, all_values, 0.0))
                half = picked[:, :LANES]
                for first in range(LANES, side_cells, LANES):
                    half = half + picked[:, first : first + LANES]
                block.append(jnp.sum(half, axis=0, keepdims=True))
            total = jnp.sum(jnp.concatenate(block, axis=0), axis=1, keepdims=True)
            totals[pl.ds(pl.multiple_of(GROUP * k + 8 * m, 8), 8), :] = jnp.broadcast_to(
                total, (8, LANES)
            )
        return carry

    totals[totals.shape[0] - LANES :, :] = jnp.zeros((LANES, LANES), F32)
    lax.fori_loop(0, (totals.shape[0] - LANES) // GROUP, patch, 0)
    tall = -(-own // 8) * 8
    sub = lax.broadcasted_iota(jnp.int32, (tall, LANES), 0)
    diagonal = sub == lax.broadcasted_iota(jnp.int32, (tall, LANES), 1)

    def owner(d, carry):
        mine = jnp.where(diagonal, totals[pl.ds(d * own, tall), :], 0.0)
        sums[pl.ds(d, 1), :] = jnp.sum(mine, axis=0, keepdims=True)
        return carry

    lax.fori_loop(0, sums.shape[0], owner, 0, unroll=8)
    leave.wait()


def join_last_kernel(
    w1, q2, c, inv, s, got_a, got_b, b_a, b_b, cur, prev_in, cur_hbm, prev_hbm, delta, prev, sems
):
    cx, side_cells = w1.shape[0], w1.shape[1]
    copies = []

    def send(src, dst):
        copies.append(pltpu.make_async_copy(src, dst, sems.at[len(copies)]))
        copies[-1].start()

    inner = pl.ds(2, cx - 4)
    send(cur.at[inner], cur_hbm.at[inner])
    for side, (got, b) in enumerate(((got_a, b_a), (got_b, b_b))):
        x0, x1 = (end_layer(own_parity(), side, k, cx) for k in range(2))
        for row, count in chunks(side_cells):
            at = pl.ds(row, count)
            change = inv[x0, at, :] * got[at, :]
            prev[side, at, :] = (s[x0, at, :] - 1.0) * (w1[x0, at, :] + change)
            change = c[x0, at, :] * change
            delta[at, :] = change
            cur[x1, at, :] += change
        send(prev.at[side], prev_hbm.at[x0])
        send(cur.at[x1], cur_hbm.at[x1])
        for row, count in chunks(side_cells):
            at, below = pl.ds(row, count), pl.ds(side_cells + row, count)
            v, total = beside(flat(delta, 0), row, count, side_cells)
            cur[x0, at, :] += (
                2.0 * (inv[x0, at, :] * got[at, :])
                + (total - 6.0 * v)
                + (got[below, :] + b[at, :] * q2[x0, at, :])
            )
        send(cur.at[x0], cur_hbm.at[x0])
    for copy in copies:
        copy.wait()


def call(kernel, ins, outs, scratch=(), aliases=None, name=None, us=2.0):
    kinds = {"v": in_vmem, "s": in_smem, "h": in_hbm}
    return pl.pallas_call(
        kernel,
        out_shape=[
            (pltpu.VMEM if kind == "v" else pltpu.HBM)(shape, *(dtype or [F32]))
            for kind, shape, *dtype in outs
        ],
        in_specs=[kinds[kind] for kind, _ in ins],
        out_specs=[kinds[kind] for kind, *_ in outs],
        scratch_shapes=list(scratch),
        input_output_aliases=aliases or {},
        compiler_params=pltpu.CompilerParams(vmem_limit_bytes=12 * 2**20),
        cost_estimate=pl.CostEstimate(flops=0, transcendentals=0, bytes_accessed=int(us * 3.0e6)),
        name=name,
    )(*[value for _, value in ins])


def on_device(u_prev, u_cur, courant_sq, patch_map, absorb, checkpoint, target_curve, tail_energy):
    cx, side = u_cur.shape[0], u_cur.shape[1]
    count = lax.axis_size("gx")
    patches = absorb.shape[0]
    own = patches // count
    all_cells = float(cx * count * side * side)
    field, plane = (cx, side, side), (side, side)
    double, tall = (2 * side, side), (side + 8, side)
    within = [(i, i ^ 1) for i in range(count)]
    across = [(i, i + 1) for i in range(1, count - 1, 2)]
    across = across + [(j, i) for i, j in across]

    def swap(a, b):
        a = lax.ppermute(a, "gx", within)
        return a, lax.ppermute(b, "gx", across)

    def deal(rows):
        return lax.all_to_all(rows, "gx", 0, 0, tiled=True)

    dma = pltpu.SemaphoreType.DMA
    ab = ("s", absorb)
    v = lambda *arrays: [("v", a) for a in arrays]
    small = (checkpoint.reshape(1, 1), target_curve.reshape(1, -1), tail_energy.reshape(1, 1))
    raw = [
        ("h", pltpu.with_memory_space_constraint(a, pltpu.HBM))
        for a in (patch_map, u_cur, u_prev, courant_sq)
    ]
    c_a, u_b, c_b = call(
        start_kernel,
        [raw[0], raw[1], raw[3]],
        [("v", (2 * side + 8, side)), ("v", plane), ("v", tall)],
        [VMEM((2, 4, side), jnp.int32), dma((3, 2))],
        name="edges",
        us=1.0,
    )
    near_a = lax.ppermute(c_a, "gx", within)
    near = (near_a, lax.ppermute(u_b, "gx", across))
    got_c = (near_a, lax.ppermute(c_b, "gx", across))
    u, up, c, s, inv, u1, params, own_maps = call(
        ahead_one_kernel,
        [ab] + v(*small) + raw,
        [("v", field)] * 6 + [("v", (8, LANES)), ("v", (cx, 4, side), jnp.int32)],
        [
            VMEM((4 * cx, side), jnp.int32),
            VMEM((4 * cx, side), F32),
            VMEM((LANES, side), F32),
            VMEM((side, LANES), F32),
            VMEM((side, LANES), F32),
            dma((4,)),
        ],
        name="forward_1",
        us=6.0,
    )
    u1, *edge_1 = call(
        join_one_kernel,
        v(c, inv, *near, u1),
        [("v", field)] + [("v", plane)] * 2,
        aliases={4: 0},
        name="edges_1",
        us=0.5,
    )
    u1h_a, u1h_b = near = swap(*edge_1)
    u2, *own_b, b_a, b_b, maps, wall_gain, wall_prior = call(
        ahead_two_kernel,
        [ab] + v(own_maps, u, up, c, inv, u1, *got_c),
        [("v", field)]
        + [("v", plane)] * 4
        + [("v", (4 * cx + 8, side), jnp.int32), ("v", (8, side)), ("v", (8, side))],
        [VMEM((side, LANES), F32), VMEM((side, LANES), F32), VMEM((LANES, side), F32)],
        name="forward_2",
        us=3.5,
    )
    got_b = (b_a, b_b)
    edge_2 = []
    for k in range(2):
        u2, pay = call(
            functools.partial(join_two_kernel, k),
            v(c, inv, own_b[k], near[k], wall_prior, u1, u2),
            [("v", field), ("v", (2 * side + 8, side))],
            aliases={6: 0},
            name="edges_2",
            us=0.4,
        )
        edge_2.append(pay)
    second = swap(*edge_2)
    u3, u4, energy, wall_now = call(
        ahead_again_kernel,
        v(u1, u2, c, inv, u1h_a, u1h_b),
        [("v", field)] * 2 + [("v", (STEPS, 8, side)), ("v", (8, side))],
        [VMEM((side, LANES), F32)],
        name="forward_3_4",
        us=5.5,
    )
    edge_4, u3h = [], []
    for k in range(2):
        u3, u4, halo, pay, energy = call(
            functools.partial(join_second_kernel, k),
            v(c, inv, energy, edge_2[k], own_b[k], second[k], got_b[k], u3, u4),
            [("v", field)] * 2
            + [("v", plane), ("v", double)]
            + [("v", (count, LANES) if k else (STEPS, 8, side))],
            [VMEM(plane, F32)],
            aliases={7: 0, 8: 1},
            name="edges_3_4",
            us=0.6,
        )
        edge_4.append(pay)
        u3h.append(halo)
    third = swap(*edge_4)
    w4, w3 = call(
        adjoint_free_kernel,
        v(u4, c, inv),
        [("v", field)] * 2,
        [VMEM(field, F32)],
        name="adjoint_3",
        us=2.6,
    )
    energy, w4, w3 = lax.optimization_barrier((energy, w4, w3))
    sums = deal(energy)
    weights, w4, w3, w2, q2 = call(
        functools.partial(adjoint_kernel, all_cells),
        v(params, sums, u2, u3, c, inv, w4, w3),
        [("v", (8 * STEPS, side))] + [("v", field)] * 4,
        [VMEM(field, F32)],
        aliases={6: 1, 7: 2},
        name="adjoint_2",
        us=3.0,
    )
    w3, w2, q2, *edge_2 = call(
        join_third_kernel,
        v(weights, u1, c, inv, *u3h, *edge_4, *third, *got_b, w3, w2, q2),
        [("v", field)] * 3 + [("v", double)] * 2,
        [VMEM(plane, F32), VMEM(plane, F32)],
        aliases={12: 0, 13: 1, 14: 2},
        name="edges_adjoint_3_2",
    )
    fourth = swap(*edge_2)
    w1, q1, prev = call(
        adjoint_end_kernel,
        v(weights, u1, w2, w3, q2, c, inv, s),
        [("v", field)] * 3,
        name="adjoint_1",
    )
    partial, prev = call(
        functools.partial(patch_kernel, own),
        v(maps, wall_gain, wall_now, *second, up, u, u1, u2, u3, u4, w4, w3, w2, w1, q2, prev),
        [("v", (count, LANES)), ("h", field)],
        [
            VMEM((4 * cx + 8, side), F32),
            VMEM((side, LANES), F32),
            VMEM((-(-patches // GROUP) * GROUP + LANES, LANES), F32),
            dma,
        ],
        name="patch_sums",
    )
    cur, mine = call(
        result_kernel,
        v(w1, q1, w2, s, deal(partial)),
        [("v", field), ("v", (1, LANES))],
        name="adjoint_0",
    )
    grad_absorb = mine[0, :own]
    cur, prev = call(
        join_last_kernel,
        v(w1, q2, c, inv, s, *fourth, *got_b, cur) + [("h", prev)],
        [("h", field)] * 2,
        [VMEM(plane, F32), VMEM((2, side, side), F32), dma((7,))],
        aliases={10: 1},
        name="edges_adjoint_1_0",
    )
    return prev, cur, grad_absorb


def solution(mesh):
    bricks = P(("groups", "gx"), None, None)
    return jax.shard_map(
        on_device,
        mesh=mesh,
        in_specs=(bricks, bricks, bricks, bricks, P("groups"), P("groups"), P("groups"), P("groups")),
        out_specs=(bricks, bricks, P(("groups", "gx"))),
        check_vma=False,
    )
```

```python
import functools

import jax
import jax.numpy as jnp
from jax import lax
from jax.experimental import pallas as pl
from jax.experimental.pallas import tpu as pltpu
from jax.sharding import PartitionSpec as P

STEPS = 4
PATCH_CELLS = 819
CHUNK = 16
LANES = 128
GROUP = 160
F32 = jnp.float32
VMEM = pltpu.VMEM
in_vmem = pl.BlockSpec(memory_space=pltpu.VMEM)
in_smem = pl.BlockSpec(memory_space=pltpu.SMEM)
in_hbm = pl.BlockSpec(memory_space=pltpu.HBM)


def end_layer(parity, side, depth, cx):
    high = 1 - parity if side == 0 else parity
    return high * (cx - 1 - depth) + (1 - high) * depth


def own_parity():
    return lax.rem(lax.axis_index("gx"), 2)


def layer(ref, x):
    return lambda row, count: ref[x, pl.ds(row, count), :]


def flat(ref, base):
    return lambda row, count: ref[pl.ds(base + row, count), :]


def chunks(side_cells):
    return [(row, CHUNK) for row in range(0, side_cells, CHUNK)]


def beside(field, row, count, side_cells):
    v = field(row, count)
    tiles = [v[k : k + 8] for k in range(0, count, 8)]
    sub = lax.broadcasted_iota(jnp.int32, tiles[0].shape, 0)
    zero = jnp.zeros_like(tiles[0])
    before = pltpu.roll(field(row - 8, 8), 1, 0) if row else zero
    after = pltpu.roll(field(row + count, 8), 7, 0) if row + count < side_cells else zero
    down = [before] + [pltpu.roll(tile, 1, 0) for tile in tiles]
    up = [pltpu.roll(tile, 7, 0) for tile in tiles] + [after]
    total = jnp.concatenate(
        [
            jnp.where(sub == 0, down[k], down[k + 1]) + jnp.where(sub == 7, up[k + 1], up[k])
            for k in range(len(tiles))
        ],
        axis=0,
    )
    parts = [v[:, k : k + LANES] for k in range(0, side_cells, LANES)]
    lane = lax.broadcasted_iota(jnp.int32, parts[0].shape, 1)
    zero = jnp.zeros_like(parts[0])
    right = [zero] + [pltpu.roll(part, 1, 1) for part in parts]
    left = [pltpu.roll(part, LANES - 1, 1) for part in parts] + [zero]
    across = jnp.concatenate(
        [
            jnp.where(lane == 0, right[k], right[k + 1])
            + jnp.where(lane == LANES - 1, left[k + 1], left[k])
            for k in range(len(parts))
        ],
        axis=1,
    )
    return v, total + across


def forward(now, prior, courant, inverse, sides, row, count, side_cells):
    v, total = beside(now, row, count, side_cells)
    for other in sides:
        total = total + other(row, count)
    p = prior(row, count)
    c, i = courant(row, count), inverse(row, count)
    return i * (2.0 * (v - p) + c * (total - 6.0 * v)) + p


def backward(product, w, later, inverse, source, sides, row, count, side_cells):
    q, total = beside(product, row, count, side_cells)
    for other in sides:
        total = total + other(row, count)
    fresh = total - 6.0 * q + source
    i = inverse(row, count)
    if later is None:
        return i * (2.0 * w + fresh)
    return i * (2.0 * (w - later) + fresh) + later


def sweep(low, high, body):
    def turn(x, carry):
        body(x)
        return carry

    lax.fori_loop(low, high, turn, 0)


def x_sides(ref, x, cx):
    return [layer(ref, k) for k in (x - 1, x + 1) if not isinstance(k, int) or 0 <= k < cx]


def fold(values):
    total = values[0:8]
    for row in range(8, values.shape[0], 8):
        total = total + values[row : row + 8]
    return total


def spread_weight(weights, n, count):
    tile = weights[8 * n : 8 * n + 8, :]
    return jnp.concatenate([tile] * (count // 8), axis=0)


def start_kernel(map_hbm, u_hbm, c_hbm, c_a, u_b, c_b, maps, sems):
    cx, side_cells = u_hbm.shape[0], u_hbm.shape[1]
    copies = []
    ends = [end_layer(own_parity(), side, 0, cx) for side in range(2)]
    u_a = c_a.at[pl.ds(side_cells + 8, side_cells)]
    for side, (u, c) in enumerate(((u_a, c_a), (u_b, c_b))):
        x0 = ends[side]
        for k, (src, dst) in enumerate(
            ((map_hbm, maps.at[side]), (u_hbm, u), (c_hbm, c.at[pl.ds(0, side_cells)]))
        ):
            copies.append(pltpu.make_async_copy(src.at[x0], dst, sems.at[k, side]))
    for copy in copies:
        copy.start()
    for side, c in enumerate((c_a, c_b)):
        copies[3 * side].wait()
        c[side_cells : side_cells + 4, :] = maps[side].astype(F32)
        c[side_cells + 4 : side_cells + 8, :] = jnp.zeros((4, side_cells), F32)
    for k, copy in enumerate(copies):
        if k % 3:
            copy.wait()


def lookup(maps, absorb_ref):
    def turn(p, got):
        return jnp.where(maps == p, absorb_ref[p], got)

    return lax.fori_loop(0, absorb_ref.shape[0], turn, jnp.zeros(maps.shape, F32), unroll=8)


def to_lane(tile, spot, lane_from):
    return pltpu.roll(tile, (spot - lane_from) % LANES, 1)


def wall_fields(columns, gains, low, high, top, bottom, row, count, side_cells):
    lane = lax.broadcasted_iota(jnp.int32, (count, LANES), 1)

    def place(ref, other):
        tile = ref[pl.ds(row, count), :]
        near = pltpu.roll(tile, lax.rem(LANES - low, LANES), 1)
        far = pltpu.roll(tile, LANES - 1 - high, 1)
        mid = [jnp.full((count, LANES), other, F32)] * (side_cells // LANES - 2)
        return jnp.concatenate(
            [
                jnp.where(lane == 0, near, other),
                *mid,
                jnp.where(lane == LANES - 1, far, other),
            ],
            axis=1,
        )

    field = place(columns, 0.0)
    if 0 < row and row + count < side_cells:
        return field, place(gains, 1.0)
    sub = lax.broadcasted_iota(jnp.int32, field.shape, 0)
    if row == 0:
        field = field + jnp.where(sub == 0, top, 0.0)
    if row + count == side_cells:
        field = field + jnp.where(sub == count - 1, bottom, 0.0)
    return field, 1.0 / (1.0 + field)


def ahead_one_kernel(
    absorb_ref, checkpoint, target, tail, map_hbm, u_hbm, up_hbm, c_hbm,
    u, up, c, s, inv, u1, params, map_ref,
    maps, found, turned, columns, gains, sems,
):
    cx, side_cells = u.shape[0], u.shape[1]
    copies = [
        pltpu.make_async_copy(src, dst, sems.at[k])
        for k, (src, dst) in enumerate(
            ((map_hbm, map_ref), (u_hbm, u), (up_hbm, up), (c_hbm, c))
        )
    ]
    for copy in copies:
        copy.start()
    copies[0].wait()
    for x in range(cx):
        maps[4 * x : 4 * x + 4, :] = map_ref[x]
    found[...] = lookup(maps[...], absorb_ref)
    turned[...] = jnp.zeros_like(turned)
    for x in range(cx):
        turned[x : x + 1, :] = found[4 * x + 2 : 4 * x + 3, :]
        turned[cx + x : cx + x + 1, :] = found[4 * x + 3 : 4 * x + 4, :]
    columns[...] = jnp.transpose(turned[...])
    gains[...] = 1.0 / (1.0 + columns[...])

    def spread(x):
        for row, count in chunks(side_cells):
            at = pl.ds(row, count)
            field, gain = wall_fields(
                columns, gains, x, cx + x, found[pl.ds(4 * x, 1), :], found[pl.ds(4 * x + 1, 1), :],
                row, count, side_cells,
            )
            s[x, at, :] = field
            inv[x, at, :] = gain

    def first(x):
        for row, count in chunks(side_cells):
            u1[x, pl.ds(row, count), :] = forward(
                layer(u, x), layer(up, x), layer(c, x), layer(inv, x), x_sides(u, x, cx),
                row, count, side_cells,
            )

    sweep(0, cx, spread)
    for copy in copies[1:]:
        copy.wait()
    history = target.shape[1]
    lane = lax.broadcasted_iota(jnp.int32, params.shape, 1)
    spot = lax.broadcasted_iota(jnp.int32, target.shape, 1)
    start = jnp.clip(checkpoint[...], 0, history - STEPS)
    row = jnp.where(lane == STEPS, tail[...], 0.0)
    for n in range(STEPS):
        value = jnp.sum(jnp.where(spot == start + n, target[...], 0.0), axis=1, keepdims=True)
        row = jnp.where(lane == n, value, row)
    params[...] = row
    first(0)
    sweep(1, cx - 1, first)
    first(cx - 1)


def join_one_kernel(side, c, inv, near, u1_in, u1, edge):
    cx, side_cells = c.shape[0], c.shape[1]
    x0 = end_layer(own_parity(), side, 0, cx)
    base = near.shape[0] - side_cells
    for row, count in chunks(side_cells):
        at = pl.ds(row, count)
        value = u1[x0, at, :] + (c[x0, at, :] * inv[x0, at, :]) * near[pl.ds(base + row, count), :]
        u1[x0, at, :] = value
        edge[at, :] = value


def wall_rows(plane, columns, side_cells):
    last = side_cells - 1
    spot = lax.broadcasted_iota(jnp.int32, (CHUNK, LANES), 1)
    low, high = pl.ds(0, LANES), pl.ds(side_cells - LANES, LANES)
    for row, count in chunks(side_cells):
        at = pl.ds(row, count)
        far = to_lane(plane(at, high), 1, LANES - 1)
        columns[at, :] = jnp.where(spot == 0, plane(at, low), jnp.where(spot == 1, far, 0.0))
    rows = jnp.transpose(columns[...])
    every = pl.ds(0, side_cells)
    return jnp.concatenate([plane(pl.ds(0, 1), every), plane(pl.ds(last, 1), every), rows[0:2]], axis=0)


def ahead_two_kernel(
    absorb_ref, map_ref, u, up, c, inv, u1, got_a, got_b,
    u2, own_a, own_b, b_a, b_b, maps, wall_gain, wall_prior, columns, gains, turned,
):
    cx, side_cells = u.shape[0], u.shape[1]
    last = side_cells - 1
    ends = [end_layer(own_parity(), side, 0, cx) for side in range(2)]
    for x in range(cx):
        maps[4 * x : 4 * x + 4, :] = map_ref[x]
    for side, got in enumerate((got_a, got_b)):
        maps[4 * (cx + side) : 4 * (cx + side) + 4, :] = got[
            side_cells : side_cells + 4, :
        ].astype(jnp.int32)
    damping = lookup(maps[4 * cx : 4 * cx + 8, :], absorb_ref)
    turned[...] = jnp.zeros_like(turned)
    for side in range(2):
        turned[2 * side : 2 * side + 2, :] = damping[4 * side + 2 : 4 * side + 4]
    columns[...] = jnp.transpose(turned[...])
    gains[...] = 1.0 / (1.0 + columns[...])
    lane = lax.broadcasted_iota(jnp.int32, (1, side_cells), 1)

    def corners(one, two):
        return jnp.where(lane == 0, one, 0.0) + jnp.where(lane == last, two, 0.0)

    for side, (got, own, b) in enumerate(((got_a, own_a, b_a), (got_b, own_b, b_b))):
        d = [damping[4 * side + f : 4 * side + f + 1] for f in range(4)]
        for row, count in chunks(side_cells):
            at = pl.ds(row, count)
            own[at, :] = c[ends[side], at, :] * inv[ends[side], at, :]
            _, gain = wall_fields(
                columns, gains, 2 * side, 2 * side + 1, d[0], d[1], row, count, side_cells
            )
            b[at, :] = got[at, :] * gain
        total = jnp.concatenate(
            [
                d[0] + corners(d[2][:, 0:1], d[3][:, 0:1]),
                d[1] + corners(d[2][:, last:], d[3][:, last:]),
                d[2] + corners(d[0][:, 0:1], d[1][:, 0:1]),
                d[3] + corners(d[0][:, last:], d[1][:, last:]),
            ],
            axis=0,
        )
        wall_gain[4 * side : 4 * side + 4, :] = 1.0 / (1.0 + total)
    for side in range(2):
        wall_prior[4 * side : 4 * side + 4, :] = wall_rows(
            lambda at, lanes, x=ends[side]: up[x, at, lanes], columns, side_cells
        )

    def second(x):
        for row, count in chunks(side_cells):
            u2[x, pl.ds(row, count), :] = forward(
                layer(u1, x), layer(u, x), layer(c, x), layer(inv, x), x_sides(u1, x, cx),
                row, count, side_cells,
            )

    second(0)
    sweep(1, cx - 1, second)
    second(cx - 1)


def join_two_kernel(side, c, inv, own, near, wall_prior, u1, u2_in, u2, pay):
    cx, side_cells = c.shape[0], c.shape[1]
    x0, x1 = (end_layer(own_parity(), side, k, cx) for k in range(2))
    for row, count in chunks(side_cells):
        at = pl.ds(row, count)
        value = u2[x0, at, :] + own[at, :] * near[at, :]
        u2[x0, at, :] = value
        pay[at, :] = value
    pay[2 * side_cells : 2 * side_cells + 4, :] = wall_prior[4 * side : 4 * side + 4, :]
    pay[2 * side_cells + 4 : 2 * side_cells + 8, :] = jnp.zeros((4, side_cells), F32)
    for row, count in chunks(side_cells):
        pay[pl.ds(side_cells + row, count), :] = forward(
            flat(pay, 0), layer(u1, x0), layer(c, x0), layer(inv, x0), [layer(u2, x1)],
            row, count, side_cells,
        )


def join_forward(x0, x1, edge, mid, last, c, inv, got_now, got_part, got_b, b, halo, delta, side_cells):
    for row, count in chunks(side_cells):
        at = pl.ds(row, count)
        change = b(row, count) * got_now(row, count)
        delta[at, :] = change
        mid[x0, at, :] += change
        halo[at, :] = got_part(row, count) + got_b(row, count) * edge(row, count)
        last[x1, at, :] += (c[x1, at, :] * inv[x1, at, :]) * change
    for row, count in chunks(side_cells):
        at = pl.ds(row, count)
        v, total = beside(flat(delta, 0), row, count, side_cells)
        last[x0, at, :] += (2.0 * inv[x0, at, :]) * v + b(row, count) * (
            total - 6.0 * v + halo[at, :]
        )


def ahead_again_kernel(u1, u2, c, inv, u1h_a, u1h_b, u3, u4, energy, wall_now, columns):
    cx, side_cells = u1.shape[0], u1.shape[1]
    for side, u1h in enumerate((u1h_a, u1h_b)):
        wall_now[4 * side : 4 * side + 4, :] = wall_rows(
            lambda at, lanes, u1h=u1h: u1h[at, lanes], columns, side_cells
        )
    energy[...] = jnp.zeros_like(energy)

    def first(x, inner):
        sums = [jnp.zeros((8, side_cells), F32)] * 3
        for row, count in chunks(side_cells):
            value = forward(
                layer(u2, x), layer(u1, x), layer(c, x), layer(inv, x), x_sides(u2, x, cx),
                row, count, side_cells,
            )
            u3[x, pl.ds(row, count), :] = value
            sums[0] = sums[0] + fold(u1[x, pl.ds(row, count), :] ** 2)
            sums[1] = sums[1] + fold(u2[x, pl.ds(row, count), :] ** 2)
            sums[2] = sums[2] + fold(value * value)
        for k in range(3 if inner else 2):
            energy[k] += sums[k]

    def second(x, inner):
        total = jnp.zeros((8, side_cells), F32)
        for row, count in chunks(side_cells):
            value = forward(
                layer(u3, x), layer(u2, x), layer(c, x), layer(inv, x), x_sides(u3, x, cx),
                row, count, side_cells,
            )
            u4[x, pl.ds(row, count), :] = value
            total = total + fold(value * value)
        if inner:
            energy[3] += total

    first(0, False)
    sweep(1, cx - 1, lambda x: first(x, True))
    first(cx - 1, False)
    second(0, False)
    second(1, False)
    sweep(2, cx - 2, lambda x: second(x, True))
    second(cx - 2, False)
    second(cx - 1, False)


def join_second_kernel(side, c, inv, energy_in, edge, own, got, gb, u3_in, u4_in, *refs):
    u3, u4, halo, pay, energy, delta = refs[-6:]
    cx, side_cells = c.shape[0], c.shape[1]
    third, fourth = energy_in[2], energy_in[3]
    x0, x1 = (end_layer(own_parity(), side, k, cx) for k in range(2))
    b = flat(own, 0)
    join_forward(
        x0, x1, flat(edge, 0), u3, u4, c, inv, flat(got, 0), flat(got, side_cells),
        flat(gb, 0), b, halo, delta, side_cells,
    )
    for row, count in chunks(side_cells):
        at = pl.ds(row, count)
        value, other = u4[x0, at, :], u4[x1, at, :]
        pay[at, :] = 2.0 * b(row, count) * value
        third = third + fold(u3[x0, at, :] ** 2)
        fourth = fourth + fold(value * value + other * other)
    for row, count in chunks(side_cells):
        at = pl.ds(row, count)
        q, total = beside(flat(pay, 0), row, count, side_cells)
        total = total + 2.0 * (c[x1, at, :] * inv[x1, at, :]) * u4[x1, at, :]
        pay[pl.ds(side_cells + row, count), :] = b(row, count) * (
            4.0 * (inv[x0, at, :] * u4[x0, at, :]) + total - 6.0 * q
        )
    parts = (energy_in[0], energy_in[1], third, fourth)
    if side == 0:
        for n, part in enumerate(parts):
            energy[n] = part
        return
    lane = lax.broadcasted_iota(jnp.int32, energy.shape, 1)
    rows = jnp.zeros(energy.shape, F32)
    for n, part in enumerate(parts):
        total = jnp.sum(jnp.sum(part, axis=0, keepdims=True), axis=1, keepdims=True)
        rows = jnp.where(lane == n, total, rows)
    energy[...] = rows


def adjoint_free_kernel(part, u4, c, inv, *refs):
    w4, w3, q4 = refs[-3:]
    cx, side_cells = u4.shape[0], u4.shape[1]

    def place(k):
        return end_layer(own_parity(), 0, k, cx)

    def zeroth(k):
        x = place(k)
        for row, count in chunks(side_cells):
            at = pl.ds(row, count)
            value = 2.0 * (inv[x, at, :] * u4[x, at, :])
            w4[x, at, :] = value
            q4[x, at, :] = c[x, at, :] * value

    def first(k):
        x = place(k)
        sides = [layer(q4, place(j)) for j in (k - 1, k + 1) if not isinstance(k, int) or 0 <= j < cx]
        for row, count in chunks(side_cells):
            at = pl.ds(row, count)
            w3[x, at, :] = backward(
                layer(q4, x), w4[x, at, :], None, layer(inv, x), 0.0, sides, row, count, side_cells
            )

    if part == 0:
        sweep(0, cx - 2, zeroth)
        first(0)
        sweep(1, cx - 3, first)
    else:
        sweep(cx - 2, cx, zeroth)
        sweep(cx - 3, cx - 1, first)
        first(cx - 1)


def adjoint_kernel(
    all_cells, params, sums, u2, u3, c, inv, w4_in, w3_in, weights, w4, w3, w2, q2, q3
):
    cx, side_cells = u2.shape[0], u2.shape[1]
    totals = jnp.sum(sums[...], axis=0, keepdims=True) / all_cells
    lane = lax.broadcasted_iota(jnp.int32, totals.shape, 1)
    weight = jnp.zeros((1, 1), F32)
    for n in range(STEPS):
        rest = jnp.where(jnp.logical_and(lane >= n, lane < STEPS), totals, 0.0)
        schroeder = params[0:1, STEPS : STEPS + 1] + jnp.sum(rest, axis=1, keepdims=True)
        weight = weight + 2.0 * (jnp.log(schroeder) - params[0:1, n : n + 1]) / schroeder
        weights[8 * n : 8 * n + 8, :] = jnp.broadcast_to(2.0 * weight, (8, side_cells))

    def first(x):
        for row, count in chunks(side_cells):
            at = pl.ds(row, count)
            g3 = 0.5 * spread_weight(weights, 3, count)
            w4[x, at, :] = g3 * w4[x, at, :]
            value = g3 * w3[x, at, :] + spread_weight(weights, 2, count) * (
                inv[x, at, :] * u3[x, at, :]
            )
            w3[x, at, :] = value
            q3[x, at, :] = c[x, at, :] * value

    def second(x):
        for row, count in chunks(side_cells):
            at = pl.ds(row, count)
            value = backward(
                layer(q3, x), w3[x, at, :], w4[x, at, :], layer(inv, x),
                spread_weight(weights, 1, count) * u2[x, at, :],
                x_sides(q3, x, cx), row, count, side_cells,
            )
            w2[x, at, :] = value
            q2[x, at, :] = c[x, at, :] * value

    sweep(0, cx, first)
    second(0)
    sweep(1, cx - 1, second)
    second(cx - 1)


def join_third_kernel(
    weights, u1, c, inv, u3h_a, u3h_b, own_a, own_b, got_a, got_b, b_a, b_b,
    w3_in, w2_in, q2_in,
    w3, w2, q2, pay_a, pay_b, halo, delta,
):
    cx, side_cells = c.shape[0], c.shape[1]
    g = [spread_weight(weights, n, CHUNK) for n in range(STEPS)]
    for side, (u3h, own, got, b, pay) in enumerate(
        ((u3h_a, own_a, got_a, b_a, pay_a), (u3h_b, own_b, got_b, b_b, pay_b))
    ):
        x0, x1 = (end_layer(own_parity(), side, k, cx) for k in range(2))
        for row, count in chunks(side_cells):
            at, below = pl.ds(row, count), pl.ds(side_cells + row, count)
            change = (0.5 * g[3]) * (inv[x0, at, :] * got[at, :])
            w3[x0, at, :] += change
            change = c[x0, at, :] * change
            delta[at, :] = change
            bh = b[at, :]
            halo[at, :] = (0.5 * g[3]) * (got[below, :] + bh * own[at, :]) + g[2] * (bh * u3h[at, :])
            value = w2[x1, at, :] + inv[x1, at, :] * change
            w2[x1, at, :] = value
            q2[x1, at, :] = c[x1, at, :] * value
        for row, count in chunks(side_cells):
            at = pl.ds(row, count)
            v, total = beside(flat(delta, 0), row, count, side_cells)
            i = inv[x0, at, :]
            value = w2[x0, at, :] + i * (
                g[3] * (i * got[at, :]) + total - 6.0 * v + halo[at, :]
            )
            w2[x0, at, :] = value
            value = c[x0, at, :] * value
            q2[x0, at, :] = value
            pay[at, :] = value
        for row, count in chunks(side_cells):
            at = pl.ds(row, count)
            pay[pl.ds(side_cells + row, count), :] = c[x0, at, :] * backward(
                flat(pay, 0), w2[x0, at, :], w3[x0, at, :], layer(inv, x0),
                g[0] * u1[x0, at, :], [layer(q2, x1)], row, count, side_cells,
            )


def result_kernel(w1, q1, w2, s, cur):
    cx, side_cells = w1.shape[0], w1.shape[1]

    def turn(x):
        for row, count in chunks(side_cells):
            at = pl.ds(row, count)
            q, total = beside(layer(q1, x), row, count, side_cells)
            for other in x_sides(q1, x, cx):
                total = total + other(row, count)
            cur[x, at, :] = (
                2.0 * w1[x, at, :] + total - 6.0 * q + (s[x, at, :] - 1.0) * w2[x, at, :]
            )

    turn(0)
    sweep(1, cx - 1, turn)
    turn(cx - 1)


def adjoint_end_kernel(weights, u1, w2, w3, q2, c, inv, s, w1, q1, prev):
    cx, side_cells = u1.shape[0], u1.shape[1]
    g0 = spread_weight(weights, 0, CHUNK)

    def first(x):
        for row, count in chunks(side_cells):
            at = pl.ds(row, count)
            value = backward(
                layer(q2, x), w2[x, at, :], w3[x, at, :], layer(inv, x), g0 * u1[x, at, :],
                x_sides(q2, x, cx), row, count, side_cells,
            )
            w1[x, at, :] = value
            q1[x, at, :] = c[x, at, :] * value
            prev[x, at, :] = (s[x, at, :] - 1.0) * value

    first(0)
    sweep(1, cx - 1, first)
    first(cx - 1)


def patch_kernel(
    own, maps, wall_gain, wall_now, got_a, got_b, up, u, u1, u2, u3, u4, w4, w3, w2, w1, q2,
    prev, prev_ends, cur, sums, prev_hbm, cur_hbm, values, columns, totals, sems,
):
    cx, side_cells = u.shape[0], u.shape[1]
    last = side_cells - 1
    ends = [end_layer(own_parity(), side, 0, cx) for side in range(2)]
    inner = pl.ds(1, cx - 2)
    leave = [
        pltpu.make_async_copy(prev.at[inner], prev_hbm.at[inner], sems.at[0]),
        pltpu.make_async_copy(prev_ends.at[0], prev_hbm.at[ends[0]], sems.at[1]),
    ]
    for k in range(cx - 2):
        x = end_layer(own_parity(), 0, k, cx)
        leave.append(pltpu.make_async_copy(cur.at[x], cur_hbm.at[x], sems.at[2 + k]))
    for copy in leave:
        copy.start()

    def field(x, at, lanes):
        k = (x, at, lanes)
        return (
            w4[k] * (u2[k] - u4[k])
            + w3[k] * (u1[k] - u3[k])
            + (w2[k] * (u[k] - u2[k]) + w1[k] * (up[k] - u1[k]))
        )

    everything = pl.ds(0, side_cells)
    low, high = pl.ds(0, LANES), pl.ds(side_cells - LANES, LANES)
    for x in range(cx):
        values[4 * x : 4 * x + 1, :] = field(x, pl.ds(0, 8), everything)[0:1]
        values[4 * x + 1 : 4 * x + 2, :] = field(x, pl.ds(last - 7, 8), everything)[7:8]
    base = 2 * cx
    tall = 2 * CHUNK
    spot = lax.broadcasted_iota(jnp.int32, (tall, LANES), 1)

    def gather(k, carry):
        at = pl.ds(pl.multiple_of(k * tall, tall), tall)
        total = jnp.zeros((tall, LANES), F32)
        for x in range(cx):
            for j, (lanes, lane_from) in enumerate(((low, 0), (high, LANES - 1))):
                tile = to_lane(field(x, at, lanes), 2 * x + j, lane_from)
                total = jnp.where(spot == 2 * x + j, tile, total)
        for side in range(2):
            for j, (lanes, lane_from) in enumerate(((low, 0), (high, LANES - 1))):
                place = base + 2 * side + j
                total = jnp.where(
                    spot == place, to_lane(q2[ends[side], at, lanes], place, lane_from), total
                )
        columns[at, :] = total
        return carry

    lax.fori_loop(0, side_cells // tall, gather, 0)
    rows = jnp.transpose(columns[...])
    for x in range(cx):
        values[4 * x + 2 : 4 * x + 4, :] = rows[2 * x : 2 * x + 2, :]
    for side in range(2):
        at, place = base + 2 * side, 4 * (cx + side)
        theirs = jnp.concatenate(
            [q2[ends[side], 0:1, :], q2[ends[side], last : last + 1, :], rows[at : at + 2, :]], axis=0
        )
        faces = slice(4 * side, 4 * side + 4)
        prior = (got_a, got_b)[side][2 * side_cells : 2 * side_cells + 4, :]
        values[place : place + 4, :] = theirs * (wall_gain[faces, :] * (prior - wall_now[faces, :]))
    all_maps, all_values = maps[...], values[...]

    def patch(k, carry):
        for m in range(GROUP // 8):
            block = []
            for j in range(8):
                picked = fold(jnp.where(all_maps == GROUP * k + 8 * m + j, all_values, 0.0))
                half = picked[:, :LANES]
                for first in range(LANES, side_cells, LANES):
                    half = half + picked[:, first : first + LANES]
                block.append(jnp.sum(half, axis=0, keepdims=True))
            total = jnp.sum(jnp.concatenate(block, axis=0), axis=1, keepdims=True)
            totals[pl.ds(pl.multiple_of(GROUP * k + 8 * m, 8), 8), :] = jnp.broadcast_to(
                total, (8, LANES)
            )
        return carry

    totals[totals.shape[0] - LANES :, :] = jnp.zeros((LANES, LANES), F32)
    lax.fori_loop(0, (totals.shape[0] - LANES) // GROUP, patch, 0)
    tall = -(-own // 8) * 8
    sub = lax.broadcasted_iota(jnp.int32, (tall, LANES), 0)
    diagonal = sub == lax.broadcasted_iota(jnp.int32, (tall, LANES), 1)

    def owner(d, carry):
        mine = jnp.where(diagonal, totals[pl.ds(d * own, tall), :], 0.0)
        sums[pl.ds(d, 1), :] = jnp.sum(mine, axis=0, keepdims=True)
        return carry

    lax.fori_loop(0, sums.shape[0], owner, 0, unroll=8)
    for copy in leave:
        copy.wait()


def join_last(side, w1, q2, c, inv, s, got, b, cur, prev, delta):
    cx, side_cells = w1.shape[0], w1.shape[1]
    x0, x1 = (end_layer(own_parity(), side, k, cx) for k in range(2))
    for row, count in chunks(side_cells):
        at = pl.ds(row, count)
        change = inv[x0, at, :] * got[at, :]
        prev[side, at, :] = (s[x0, at, :] - 1.0) * (w1[x0, at, :] + change)
        change = c[x0, at, :] * change
        delta[at, :] = change
        cur[x1, at, :] += change
    for row, count in chunks(side_cells):
        at, below = pl.ds(row, count), pl.ds(side_cells + row, count)
        v, total = beside(flat(delta, 0), row, count, side_cells)
        cur[x0, at, :] += (
            2.0 * (inv[x0, at, :] * got[at, :])
            + (total - 6.0 * v)
            + (got[below, :] + b[at, :] * q2[x0, at, :])
        )


def join_near_kernel(w1, q2, c, inv, s, got, b, cur_in, cur, prev, delta):
    join_last(0, w1, q2, c, inv, s, got, b, cur, prev, delta)


def share_kernel(own, dealt, cur_in, cur, mine):
    mine[...] = (jnp.sum(dealt[...], axis=0) / float(PATCH_CELLS))[:own]


def join_far_kernel(
    w1, q2, c, inv, s, got, b, mine, cur_in, ends_in, cur_hbm_in, prev_hbm_in,
    cur, prev, cur_hbm, prev_hbm, mine_hbm, delta, sems,
):
    cx = w1.shape[0]
    copies = []

    def send(src, dst):
        copies.append(pltpu.make_async_copy(src, dst, sems.at[len(copies)]))
        copies[-1].start()

    send(mine, mine_hbm)
    x0, x1 = (end_layer(own_parity(), 1, k, cx) for k in range(2))
    join_last(1, w1, q2, c, inv, s, got, b, cur, prev, delta)
    send(prev.at[1], prev_hbm.at[x0])
    send(cur.at[x1], cur_hbm.at[x1])
    send(cur.at[x0], cur_hbm.at[x0])
    for copy in copies:
        copy.wait()


def call(kernel, ins, outs, scratch=(), aliases=None, name=None, us=2.0):
    kinds = {"v": in_vmem, "s": in_smem, "h": in_hbm}
    return pl.pallas_call(
        kernel,
        out_shape=[
            (pltpu.VMEM if kind == "v" else pltpu.HBM)(shape, *(dtype or [F32]))
            for kind, shape, *dtype in outs
        ],
        in_specs=[kinds[kind] for kind, _ in ins],
        out_specs=[kinds[kind] for kind, *_ in outs],
        scratch_shapes=list(scratch),
        input_output_aliases=aliases or {},
        compiler_params=pltpu.CompilerParams(vmem_limit_bytes=12 * 2**20),
        cost_estimate=pl.CostEstimate(flops=0, transcendentals=0, bytes_accessed=int(us * 3.0e6)),
        name=name,
    )(*[value for _, value in ins])


def on_device(u_prev, u_cur, courant_sq, patch_map, absorb, checkpoint, target_curve, tail_energy):
    cx, side = u_cur.shape[0], u_cur.shape[1]
    count = lax.axis_size("gx")
    patches = absorb.shape[0]
    own = patches // count
    all_cells = float(cx * count * side * side)
    field, plane = (cx, side, side), (side, side)
    double, tall = (2 * side, side), (side + 8, side)
    within = [(i, i ^ 1) for i in range(count)]
    across = [(i, i + 1) for i in range(1, count - 1, 2)]
    across = across + [(j, i) for i, j in across]

    def swap(a, b):
        a = lax.ppermute(a, "gx", within)
        return a, lax.ppermute(b, "gx", across)

    def deal(rows):
        return lax.all_to_all(rows, "gx", 0, 0, tiled=True)

    dma = pltpu.SemaphoreType.DMA
    ab = ("s", absorb)
    v = lambda *arrays: [("v", a) for a in arrays]
    small = (checkpoint.reshape(1, 1), target_curve.reshape(1, -1), tail_energy.reshape(1, 1))
    raw = [
        ("h", pltpu.with_memory_space_constraint(a, pltpu.HBM))
        for a in (patch_map, u_cur, u_prev, courant_sq)
    ]
    c_a, u_b, c_b = call(
        start_kernel,
        [raw[0], raw[1], raw[3]],
        [("v", (2 * side + 8, side)), ("v", plane), ("v", tall)],
        [VMEM((2, 4, side), jnp.int32), dma((3, 2))],
        name="edges",
        us=1.0,
    )
    near_a = lax.ppermute(c_a, "gx", within)
    near = (near_a, lax.ppermute(u_b, "gx", across))
    got_c = (near_a, lax.ppermute(c_b, "gx", across))
    u, up, c, s, inv, u1, params, own_maps = call(
        ahead_one_kernel,
        [ab] + v(*small) + raw,
        [("v", field)] * 6 + [("v", (8, LANES)), ("v", (cx, 4, side), jnp.int32)],
        [
            VMEM((4 * cx, side), jnp.int32),
            VMEM((4 * cx, side), F32),
            VMEM((LANES, side), F32),
            VMEM((side, LANES), F32),
            VMEM((side, LANES), F32),
            dma((4,)),
        ],
        name="forward_1",
        us=6.0,
    )
    edge_1 = []
    for k in range(2):
        u1, plane_1 = call(
            functools.partial(join_one_kernel, k),
            v(c, inv, near[k], u1),
            [("v", field), ("v", plane)],
            aliases={3: 0},
            name="edges_1",
            us=0.1,
        )
        edge_1.append(plane_1)
    u1h_a, u1h_b = near = swap(*edge_1)
    u2, *own_b, b_a, b_b, maps, wall_gain, wall_prior = call(
        ahead_two_kernel,
        [ab] + v(own_maps, u, up, c, inv, u1, *got_c),
        [("v", field)]
        + [("v", plane)] * 4
        + [("v", (4 * cx + 8, side), jnp.int32), ("v", (8, side)), ("v", (8, side))],
        [VMEM((side, LANES), F32), VMEM((side, LANES), F32), VMEM((LANES, side), F32)],
        name="forward_2",
        us=3.5,
    )
    got_b = (b_a, b_b)
    edge_2 = []
    for k in range(2):
        u2, pay = call(
            functools.partial(join_two_kernel, k),
            v(c, inv, own_b[k], near[k], wall_prior, u1, u2),
            [("v", field), ("v", (2 * side + 8, side))],
            aliases={6: 0},
            name="edges_2",
            us=0.4,
        )
        edge_2.append(pay)
    second = swap(*edge_2)
    u3, u4, energy, wall_now = call(
        ahead_again_kernel,
        v(u1, u2, c, inv, u1h_a, u1h_b),
        [("v", field)] * 2 + [("v", (STEPS, 8, side)), ("v", (8, side))],
        [VMEM((side, LANES), F32)],
        name="forward_3_4",
        us=5.5,
    )
    edge_4, u3h, free = [], [], []
    for k in range(2):
        u3, u4, halo, pay, energy = call(
            functools.partial(join_second_kernel, k),
            v(c, inv, energy, edge_2[k], own_b[k], second[k], got_b[k], u3, u4, *free[:1]),
            [("v", field)] * 2
            + [("v", plane), ("v", double)]
            + [("v", (count, LANES) if k else (STEPS, 8, side))],
            [VMEM(plane, F32)],
            aliases={7: 0, 8: 1},
            name="edges_3_4",
            us=0.6,
        )
        edge_4.append(pay)
        u3h.append(halo)
        free = call(
            functools.partial(adjoint_free_kernel, k),
            v(u4, c, inv, *free),
            [("v", field)] * 3,
            aliases={3: 0, 4: 1, 5: 2} if k else None,
            name="adjoint_3",
            us=1.0,
        )
    third = swap(*edge_4)
    w4, w3, _ = free
    energy, w4, w3 = lax.optimization_barrier((energy, w4, w3))
    sums = deal(energy)
    weights, w4, w3, w2, q2 = call(
        functools.partial(adjoint_kernel, all_cells),
        v(params, sums, u2, u3, c, inv, w4, w3),
        [("v", (8 * STEPS, side))] + [("v", field)] * 4,
        [VMEM(field, F32)],
        aliases={6: 1, 7: 2},
        name="adjoint_2",
        us=3.0,
    )
    w3, w2, q2, *edge_2 = call(
        join_third_kernel,
        v(weights, u1, c, inv, *u3h, *edge_4, *third, *got_b, w3, w2, q2),
        [("v", field)] * 3 + [("v", double)] * 2,
        [VMEM(plane, F32), VMEM(plane, F32)],
        aliases={12: 0, 13: 1, 14: 2},
        name="edges_adjoint_3_2",
    )
    fourth = swap(*edge_2)
    w1, q1, prev = call(
        adjoint_end_kernel,
        v(weights, u1, w2, w3, q2, c, inv, s),
        [("v", field)] * 3,
        name="adjoint_1",
    )
    (cur,) = call(result_kernel, v(w1, q1, w2, s), [("v", field)], name="adjoint_0", us=1.8)
    cur, ends = call(
        join_near_kernel,
        v(w1, q2, c, inv, s, fourth[0], got_b[0], cur),
        [("v", field), ("v", (2, side, side))],
        [VMEM(plane, F32)],
        aliases={7: 0},
        name="near_edge_0",
        us=0.4,
    )
    partial, prev_out, cur_out = call(
        functools.partial(patch_kernel, own),
        v(maps, wall_gain, wall_now, second[0], second[1], up, u, u1, u2, u3, u4, w4, w3, w2, w1, q2)
        + v(prev, ends, cur),
        [("v", (count, LANES)), ("h", field), ("h", field)],
        [
            VMEM((4 * cx + 8, side), F32),
            VMEM((side, LANES), F32),
            VMEM((-(-patches // GROUP) * GROUP + LANES, LANES), F32),
            dma((cx,)),
        ],
        name="patch_sums",
        us=2.7,
    )
    cur, mine = call(
        functools.partial(share_kernel, own),
        v(deal(partial), cur),
        [("v", field), ("v", (own,))],
        aliases={1: 0},
        name="share",
        us=0.1,
    )
    _, _, cur, prev, mine = call(
        join_far_kernel,
        v(w1, q2, c, inv, s, fourth[1], got_b[1], mine, cur, ends)
        + [("h", cur_out), ("h", prev_out)],
        [("v", field), ("v", (2, side, side)), ("h", field), ("h", field), ("h", (own,))],
        [VMEM(plane, F32), dma((4,))],
        aliases={8: 0, 9: 1, 10: 2, 11: 3},
        name="far_edge_0",
        us=1.0,
    )
    return prev, cur, mine


def solution(mesh):
    bricks = P(("groups", "gx"), None, None)
    return jax.shard_map(
        on_device,
        mesh=mesh,
        in_specs=(bricks, bricks, bricks, bricks, P("groups"), P("groups"), P("groups"), P("groups")),
        out_specs=(bricks, bricks, P(("groups", "gx"))),
        check_vma=False,
    )
```

```python
import functools

import jax
import jax.numpy as jnp
from jax import lax
from jax.experimental import pallas as pl
from jax.experimental.pallas import tpu as pltpu
from jax.sharding import PartitionSpec as P

STEPS = 4
PATCH_CELLS = 819
CHUNK = 16
LANES = 128
GROUP = 160
F32 = jnp.float32
VMEM = pltpu.VMEM
in_vmem = pl.BlockSpec(memory_space=pltpu.VMEM)
in_smem = pl.BlockSpec(memory_space=pltpu.SMEM)
in_hbm = pl.BlockSpec(memory_space=pltpu.HBM)


def end_layer(parity, side, depth, cx):
    high = 1 - parity if side == 0 else parity
    return high * (cx - 1 - depth) + (1 - high) * depth


def own_parity():
    return lax.rem(lax.axis_index("gx"), 2)


def layer(ref, x):
    return lambda row, count: ref[x, pl.ds(row, count), :]


def flat(ref, base):
    return lambda row, count: ref[pl.ds(base + row, count), :]


def chunks(side_cells):
    return [(row, CHUNK) for row in range(0, side_cells, CHUNK)]


def beside(field, row, count, side_cells):
    v = field(row, count)
    tiles = [v[k : k + 8] for k in range(0, count, 8)]
    sub = lax.broadcasted_iota(jnp.int32, tiles[0].shape, 0)
    zero = jnp.zeros_like(tiles[0])
    before = pltpu.roll(field(row - 8, 8), 1, 0) if row else zero
    after = pltpu.roll(field(row + count, 8), 7, 0) if row + count < side_cells else zero
    down = [before] + [pltpu.roll(tile, 1, 0) for tile in tiles]
    up = [pltpu.roll(tile, 7, 0) for tile in tiles] + [after]
    total = jnp.concatenate(
        [
            jnp.where(sub == 0, down[k], down[k + 1]) + jnp.where(sub == 7, up[k + 1], up[k])
            for k in range(len(tiles))
        ],
        axis=0,
    )
    parts = [v[:, k : k + LANES] for k in range(0, side_cells, LANES)]
    lane = lax.broadcasted_iota(jnp.int32, parts[0].shape, 1)
    zero = jnp.zeros_like(parts[0])
    right = [zero] + [pltpu.roll(part, 1, 1) for part in parts]
    left = [pltpu.roll(part, LANES - 1, 1) for part in parts] + [zero]
    across = jnp.concatenate(
        [
            jnp.where(lane == 0, right[k], right[k + 1])
            + jnp.where(lane == LANES - 1, left[k + 1], left[k])
            for k in range(len(parts))
        ],
        axis=1,
    )
    return v, total + across


def forward(now, prior, courant, inverse, sides, row, count, side_cells):
    v, total = beside(now, row, count, side_cells)
    for other in sides:
        total = total + other(row, count)
    p = prior(row, count)
    c, i = courant(row, count), inverse(row, count)
    return i * (2.0 * (v - p) + c * (total - 6.0 * v)) + p


def backward(product, w, later, inverse, source, sides, row, count, side_cells):
    q, total = beside(product, row, count, side_cells)
    for other in sides:
        total = total + other(row, count)
    fresh = total - 6.0 * q + source
    i = inverse(row, count)
    if later is None:
        return i * (2.0 * w + fresh)
    return i * (2.0 * (w - later) + fresh) + later


def sweep(low, high, body):
    def turn(x, carry):
        body(x)
        return carry

    lax.fori_loop(low, high, turn, 0)


def x_sides(ref, x, cx):
    return [layer(ref, k) for k in (x - 1, x + 1) if not isinstance(k, int) or 0 <= k < cx]


def fold(values):
    total = values[0:8]
    for row in range(8, values.shape[0], 8):
        total = total + values[row : row + 8]
    return total


def spread_weight(weights, n, count):
    tile = weights[8 * n : 8 * n + 8, :]
    return jnp.concatenate([tile] * (count // 8), axis=0)


def start_kernel(map_hbm, u_hbm, c_hbm, c_a, u_b, c_b, maps, sems):
    cx, side_cells = u_hbm.shape[0], u_hbm.shape[1]
    ends = [end_layer(own_parity(), side, 0, cx) for side in range(2)]
    plane = pl.ds(0, side_cells)
    copies = [
        pltpu.make_async_copy(src, dst, sems.at[k])
        for k, (src, dst) in enumerate(
            (
                (map_hbm, maps),
                (u_hbm.at[ends[1]], u_b),
                (c_hbm.at[ends[1]], c_b.at[plane]),
                (c_hbm.at[ends[0]], c_a.at[plane]),
                (u_hbm.at[ends[0]], c_a.at[pl.ds(side_cells + 8, side_cells)]),
            )
        )
    ]
    for copy in copies:
        copy.start()
    copies[0].wait()
    for side, c in enumerate((c_a, c_b)):
        c[side_cells : side_cells + 4, :] = maps[ends[side]].astype(F32)
        c[side_cells + 4 : side_cells + 8, :] = jnp.zeros((4, side_cells), F32)
    for copy in copies[1:]:
        copy.wait()


def lookup(maps, absorb_ref):
    def turn(p, got):
        return jnp.where(maps == p, absorb_ref[p], got)

    return lax.fori_loop(0, absorb_ref.shape[0], turn, jnp.zeros(maps.shape, F32), unroll=8)


def to_lane(tile, spot, lane_from):
    return pltpu.roll(tile, (spot - lane_from) % LANES, 1)


def wall_fields(columns, gains, low, high, top, bottom, row, count, side_cells):
    lane = lax.broadcasted_iota(jnp.int32, (count, LANES), 1)

    def place(ref, other):
        tile = ref[pl.ds(row, count), :]
        near = pltpu.roll(tile, lax.rem(LANES - low, LANES), 1)
        far = pltpu.roll(tile, LANES - 1 - high, 1)
        mid = [jnp.full((count, LANES), other, F32)] * (side_cells // LANES - 2)
        return jnp.concatenate(
            [
                jnp.where(lane == 0, near, other),
                *mid,
                jnp.where(lane == LANES - 1, far, other),
            ],
            axis=1,
        )

    field = place(columns, 0.0)
    if 0 < row and row + count < side_cells:
        return field, place(gains, 1.0)
    sub = lax.broadcasted_iota(jnp.int32, field.shape, 0)
    if row == 0:
        field = field + jnp.where(sub == 0, top, 0.0)
    if row + count == side_cells:
        field = field + jnp.where(sub == count - 1, bottom, 0.0)
    return field, 1.0 / (1.0 + field)


def ahead_one_kernel(
    absorb_ref, checkpoint, target, tail, map_ref, u_hbm, up_hbm, c_hbm,
    u, up, c, s, inv, u1, params,
    maps, found, turned, columns, gains, sems,
):
    cx, side_cells = u.shape[0], u.shape[1]
    arrays = ((u_hbm, u), (up_hbm, up), (c_hbm, c))

    def load(k, x):
        src, dst = arrays[k]
        return pltpu.make_async_copy(src.at[x], dst.at[x], sems.at[k, x])

    for x in range(cx):
        for k in range(3):
            load(k, x).start()
    for x in range(cx):
        maps[4 * x : 4 * x + 4, :] = map_ref[x]
    found[...] = lookup(maps[...], absorb_ref)
    turned[...] = jnp.zeros_like(turned)
    for x in range(cx):
        turned[x : x + 1, :] = found[4 * x + 2 : 4 * x + 3, :]
        turned[cx + x : cx + x + 1, :] = found[4 * x + 3 : 4 * x + 4, :]
    columns[...] = jnp.transpose(turned[...])
    gains[...] = 1.0 / (1.0 + columns[...])

    def spread(x):
        for row, count in chunks(side_cells):
            at = pl.ds(row, count)
            field, gain = wall_fields(
                columns, gains, x, cx + x, found[pl.ds(4 * x, 1), :], found[pl.ds(4 * x + 1, 1), :],
                row, count, side_cells,
            )
            s[x, at, :] = field
            inv[x, at, :] = gain

    def first(x):
        for row, count in chunks(side_cells):
            u1[x, pl.ds(row, count), :] = forward(
                layer(u, x), layer(up, x), layer(c, x), layer(inv, x), x_sides(u, x, cx),
                row, count, side_cells,
            )

    sweep(0, cx, spread)
    history = target.shape[1]
    lane = lax.broadcasted_iota(jnp.int32, params.shape, 1)
    spot = lax.broadcasted_iota(jnp.int32, target.shape, 1)
    start = jnp.clip(checkpoint[...], 0, history - STEPS)
    row = jnp.where(lane == STEPS, tail[...], 0.0)
    for n in range(STEPS):
        value = jnp.sum(jnp.where(spot == start + n, target[...], 0.0), axis=1, keepdims=True)
        row = jnp.where(lane == n, value, row)
    params[...] = row
    for x in range(2):
        load(0, x).wait()
    for k in (1, 2):
        load(k, 0).wait()
    first(0)

    def turn(x):
        load(0, x + 1).wait()
        load(1, x).wait()
        load(2, x).wait()
        first(x)

    sweep(1, cx - 1, turn)
    for k in (1, 2):
        load(k, cx - 1).wait()
    first(cx - 1)


def join_one_kernel(side, c, inv, near, u1_in, u1, edge):
    cx, side_cells = c.shape[0], c.shape[1]
    x0 = end_layer(own_parity(), side, 0, cx)
    base = near.shape[0] - side_cells
    for row, count in chunks(side_cells):
        at = pl.ds(row, count)
        value = u1[x0, at, :] + (c[x0, at, :] * inv[x0, at, :]) * near[pl.ds(base + row, count), :]
        u1[x0, at, :] = value
        edge[at, :] = value


def wall_rows(plane, columns, side_cells):
    last = side_cells - 1
    spot = lax.broadcasted_iota(jnp.int32, (CHUNK, LANES), 1)
    low, high = pl.ds(0, LANES), pl.ds(side_cells - LANES, LANES)
    for row, count in chunks(side_cells):
        at = pl.ds(row, count)
        far = to_lane(plane(at, high), 1, LANES - 1)
        columns[at, :] = jnp.where(spot == 0, plane(at, low), jnp.where(spot == 1, far, 0.0))
    rows = jnp.transpose(columns[...])
    every = pl.ds(0, side_cells)
    return jnp.concatenate([plane(pl.ds(0, 1), every), plane(pl.ds(last, 1), every), rows[0:2]], axis=0)


def ahead_two_kernel(
    absorb_ref, map_ref, u, up, c, inv, u1, got_a, got_b,
    u2, own_a, own_b, b_a, b_b, maps, wall_gain, wall_prior, columns, gains, turned,
):
    cx, side_cells = u.shape[0], u.shape[1]
    last = side_cells - 1
    ends = [end_layer(own_parity(), side, 0, cx) for side in range(2)]
    for x in range(cx):
        maps[4 * x : 4 * x + 4, :] = map_ref[x]
    for side, got in enumerate((got_a, got_b)):
        maps[4 * (cx + side) : 4 * (cx + side) + 4, :] = got[
            side_cells : side_cells + 4, :
        ].astype(jnp.int32)
    damping = lookup(maps[4 * cx : 4 * cx + 8, :], absorb_ref)
    turned[...] = jnp.zeros_like(turned)
    for side in range(2):
        turned[2 * side : 2 * side + 2, :] = damping[4 * side + 2 : 4 * side + 4]
    columns[...] = jnp.transpose(turned[...])
    gains[...] = 1.0 / (1.0 + columns[...])
    lane = lax.broadcasted_iota(jnp.int32, (1, side_cells), 1)

    def corners(one, two):
        return jnp.where(lane == 0, one, 0.0) + jnp.where(lane == last, two, 0.0)

    for side, (got, own, b) in enumerate(((got_a, own_a, b_a), (got_b, own_b, b_b))):
        d = [damping[4 * side + f : 4 * side + f + 1] for f in range(4)]
        for row, count in chunks(side_cells):
            at = pl.ds(row, count)
            own[at, :] = c[ends[side], at, :] * inv[ends[side], at, :]
            _, gain = wall_fields(
                columns, gains, 2 * side, 2 * side + 1, d[0], d[1], row, count, side_cells
            )
            b[at, :] = got[at, :] * gain
        total = jnp.concatenate(
            [
                d[0] + corners(d[2][:, 0:1], d[3][:, 0:1]),
                d[1] + corners(d[2][:, last:], d[3][:, last:]),
                d[2] + corners(d[0][:, 0:1], d[1][:, 0:1]),
                d[3] + corners(d[0][:, last:], d[1][:, last:]),
            ],
            axis=0,
        )
        wall_gain[4 * side : 4 * side + 4, :] = 1.0 / (1.0 + total)
    for side in range(2):
        wall_prior[4 * side : 4 * side + 4, :] = wall_rows(
            lambda at, lanes, x=ends[side]: up[x, at, lanes], columns, side_cells
        )

    def second(x):
        for row, count in chunks(side_cells):
            u2[x, pl.ds(row, count), :] = forward(
                layer(u1, x), layer(u, x), layer(c, x), layer(inv, x), x_sides(u1, x, cx),
                row, count, side_cells,
            )

    second(0)
    sweep(1, cx - 1, second)
    second(cx - 1)


def join_two_kernel(side, c, inv, own, near, wall_prior, u1, u2_in, u2, pay):
    cx, side_cells = c.shape[0], c.shape[1]
    x0, x1 = (end_layer(own_parity(), side, k, cx) for k in range(2))
    for row, count in chunks(side_cells):
        at = pl.ds(row, count)
        value = u2[x0, at, :] + own[at, :] * near[at, :]
        u2[x0, at, :] = value
        pay[at, :] = value
    pay[2 * side_cells : 2 * side_cells + 4, :] = wall_prior[4 * side : 4 * side + 4, :]
    pay[2 * side_cells + 4 : 2 * side_cells + 8, :] = jnp.zeros((4, side_cells), F32)
    for row, count in chunks(side_cells):
        pay[pl.ds(side_cells + row, count), :] = forward(
            flat(pay, 0), layer(u1, x0), layer(c, x0), layer(inv, x0), [layer(u2, x1)],
            row, count, side_cells,
        )


def join_forward(x0, x1, edge, mid, last, c, inv, got_now, got_part, got_b, b, halo, delta, side_cells):
    for row, count in chunks(side_cells):
        at = pl.ds(row, count)
        change = b(row, count) * got_now(row, count)
        delta[at, :] = change
        mid[x0, at, :] += change
        halo[at, :] = got_part(row, count) + got_b(row, count) * edge(row, count)
        last[x1, at, :] += (c[x1, at, :] * inv[x1, at, :]) * change
    for row, count in chunks(side_cells):
        at = pl.ds(row, count)
        v, total = beside(flat(delta, 0), row, count, side_cells)
        last[x0, at, :] += (2.0 * inv[x0, at, :]) * v + b(row, count) * (
            total - 6.0 * v + halo[at, :]
        )


def ahead_again_kernel(u1, u2, c, inv, u1h_a, u1h_b, u3, u4, energy, wall_now, columns):
    cx, side_cells = u1.shape[0], u1.shape[1]
    for side, u1h in enumerate((u1h_a, u1h_b)):
        wall_now[4 * side : 4 * side + 4, :] = wall_rows(
            lambda at, lanes, u1h=u1h: u1h[at, lanes], columns, side_cells
        )
    energy[...] = jnp.zeros_like(energy)

    def first(x, inner):
        sums = [jnp.zeros((8, side_cells), F32)] * 3
        for row, count in chunks(side_cells):
            value = forward(
                layer(u2, x), layer(u1, x), layer(c, x), layer(inv, x), x_sides(u2, x, cx),
                row, count, side_cells,
            )
            u3[x, pl.ds(row, count), :] = value
            sums[0] = sums[0] + fold(u1[x, pl.ds(row, count), :] ** 2)
            sums[1] = sums[1] + fold(u2[x, pl.ds(row, count), :] ** 2)
            sums[2] = sums[2] + fold(value * value)
        for k in range(3 if inner else 2):
            energy[k] += sums[k]

    def second(x, inner):
        total = jnp.zeros((8, side_cells), F32)
        for row, count in chunks(side_cells):
            value = forward(
                layer(u3, x), layer(u2, x), layer(c, x), layer(inv, x), x_sides(u3, x, cx),
                row, count, side_cells,
            )
            u4[x, pl.ds(row, count), :] = value
            total = total + fold(value * value)
        if inner:
            energy[3] += total

    first(0, False)
    sweep(1, cx - 1, lambda x: first(x, True))
    first(cx - 1, False)
    second(0, False)
    second(1, False)
    sweep(2, cx - 2, lambda x: second(x, True))
    second(cx - 2, False)
    second(cx - 1, False)


def join_second_kernel(side, c, inv, energy_in, edge, own, got, gb, u3_in, u4_in, *refs):
    u3, u4, halo, pay, energy, delta = refs[-6:]
    cx, side_cells = c.shape[0], c.shape[1]
    third, fourth = energy_in[2], energy_in[3]
    x0, x1 = (end_layer(own_parity(), side, k, cx) for k in range(2))
    b = flat(own, 0)
    join_forward(
        x0, x1, flat(edge, 0), u3, u4, c, inv, flat(got, 0), flat(got, side_cells),
        flat(gb, 0), b, halo, delta, side_cells,
    )
    for row, count in chunks(side_cells):
        at = pl.ds(row, count)
        value, other = u4[x0, at, :], u4[x1, at, :]
        pay[at, :] = 2.0 * b(row, count) * value
        third = third + fold(u3[x0, at, :] ** 2)
        fourth = fourth + fold(value * value + other * other)
    for row, count in chunks(side_cells):
        at = pl.ds(row, count)
        q, total = beside(flat(pay, 0), row, count, side_cells)
        total = total + 2.0 * (c[x1, at, :] * inv[x1, at, :]) * u4[x1, at, :]
        pay[pl.ds(side_cells + row, count), :] = b(row, count) * (
            4.0 * (inv[x0, at, :] * u4[x0, at, :]) + total - 6.0 * q
        )
    parts = (energy_in[0], energy_in[1], third, fourth)
    if side == 0:
        for n, part in enumerate(parts):
            energy[n] = part
        return
    lane = lax.broadcasted_iota(jnp.int32, energy.shape, 1)
    rows = jnp.zeros(energy.shape, F32)
    for n, part in enumerate(parts):
        total = jnp.sum(jnp.sum(part, axis=0, keepdims=True), axis=1, keepdims=True)
        rows = jnp.where(lane == n, total, rows)
    energy[...] = rows


def adjoint_free_kernel(part, u4, c, inv, *refs):
    w4, w3, q4 = refs[-3:]
    cx, side_cells = u4.shape[0], u4.shape[1]

    def place(k):
        return end_layer(own_parity(), 0, k, cx)

    def zeroth(k):
        x = place(k)
        for row, count in chunks(side_cells):
            at = pl.ds(row, count)
            value = 2.0 * (inv[x, at, :] * u4[x, at, :])
            w4[x, at, :] = value
            q4[x, at, :] = c[x, at, :] * value

    def first(k):
        x = place(k)
        sides = [layer(q4, place(j)) for j in (k - 1, k + 1) if not isinstance(k, int) or 0 <= j < cx]
        for row, count in chunks(side_cells):
            at = pl.ds(row, count)
            w3[x, at, :] = backward(
                layer(q4, x), w4[x, at, :], None, layer(inv, x), 0.0, sides, row, count, side_cells
            )

    if part == 0:
        sweep(0, cx - 2, zeroth)
        first(0)
        sweep(1, cx - 3, first)
    else:
        sweep(cx - 2, cx, zeroth)
        sweep(cx - 3, cx - 1, first)
        first(cx - 1)


def adjoint_kernel(
    all_cells, params, sums, u2, u3, c, inv, w4_in, w3_in, weights, w4, w3, w2, q2, q3
):
    cx, side_cells = u2.shape[0], u2.shape[1]
    totals = jnp.sum(sums[...], axis=0, keepdims=True) / all_cells
    lane = lax.broadcasted_iota(jnp.int32, totals.shape, 1)
    weight = jnp.zeros((1, 1), F32)
    for n in range(STEPS):
        rest = jnp.where(jnp.logical_and(lane >= n, lane < STEPS), totals, 0.0)
        schroeder = params[0:1, STEPS : STEPS + 1] + jnp.sum(rest, axis=1, keepdims=True)
        weight = weight + 2.0 * (jnp.log(schroeder) - params[0:1, n : n + 1]) / schroeder
        weights[8 * n : 8 * n + 8, :] = jnp.broadcast_to(2.0 * weight, (8, side_cells))

    def first(x):
        for row, count in chunks(side_cells):
            at = pl.ds(row, count)
            g3 = 0.5 * spread_weight(weights, 3, count)
            w4[x, at, :] = g3 * w4[x, at, :]
            value = g3 * w3[x, at, :] + spread_weight(weights, 2, count) * (
                inv[x, at, :] * u3[x, at, :]
            )
            w3[x, at, :] = value
            q3[x, at, :] = c[x, at, :] * value

    def second(x):
        for row, count in chunks(side_cells):
            at = pl.ds(row, count)
            value = backward(
                layer(q3, x), w3[x, at, :], w4[x, at, :], layer(inv, x),
                spread_weight(weights, 1, count) * u2[x, at, :],
                x_sides(q3, x, cx), row, count, side_cells,
            )
            w2[x, at, :] = value
            q2[x, at, :] = c[x, at, :] * value

    sweep(0, cx, first)
    second(0)
    sweep(1, cx - 1, second)
    second(cx - 1)


def join_third_kernel(
    weights, u1, c, inv, u3h_a, u3h_b, own_a, own_b, got_a, got_b, b_a, b_b,
    w3_in, w2_in, q2_in,
    w3, w2, q2, pay_a, pay_b, halo, delta,
):
    cx, side_cells = c.shape[0], c.shape[1]
    g = [spread_weight(weights, n, CHUNK) for n in range(STEPS)]
    for side, (u3h, own, got, b, pay) in enumerate(
        ((u3h_a, own_a, got_a, b_a, pay_a), (u3h_b, own_b, got_b, b_b, pay_b))
    ):
        x0, x1 = (end_layer(own_parity(), side, k, cx) for k in range(2))
        for row, count in chunks(side_cells):
            at, below = pl.ds(row, count), pl.ds(side_cells + row, count)
            change = (0.5 * g[3]) * (inv[x0, at, :] * got[at, :])
            w3[x0, at, :] += change
            change = c[x0, at, :] * change
            delta[at, :] = change
            bh = b[at, :]
            halo[at, :] = (0.5 * g[3]) * (got[below, :] + bh * own[at, :]) + g[2] * (bh * u3h[at, :])
            value = w2[x1, at, :] + inv[x1, at, :] * change
            w2[x1, at, :] = value
            q2[x1, at, :] = c[x1, at, :] * value
        for row, count in chunks(side_cells):
            at = pl.ds(row, count)
            v, total = beside(flat(delta, 0), row, count, side_cells)
            i = inv[x0, at, :]
            value = w2[x0, at, :] + i * (
                g[3] * (i * got[at, :]) + total - 6.0 * v + halo[at, :]
            )
            w2[x0, at, :] = value
            value = c[x0, at, :] * value
            q2[x0, at, :] = value
            pay[at, :] = value
        for row, count in chunks(side_cells):
            at = pl.ds(row, count)
            pay[pl.ds(side_cells + row, count), :] = c[x0, at, :] * backward(
                flat(pay, 0), w2[x0, at, :], w3[x0, at, :], layer(inv, x0),
                g[0] * u1[x0, at, :], [layer(q2, x1)], row, count, side_cells,
            )


def result_kernel(w1, q1, w2, s, cur):
    cx, side_cells = w1.shape[0], w1.shape[1]

    def turn(x):
        for row, count in chunks(side_cells):
            at = pl.ds(row, count)
            q, total = beside(layer(q1, x), row, count, side_cells)
            for other in x_sides(q1, x, cx):
                total = total + other(row, count)
            cur[x, at, :] = (
                2.0 * w1[x, at, :] + total - 6.0 * q + (s[x, at, :] - 1.0) * w2[x, at, :]
            )

    turn(0)
    sweep(1, cx - 1, turn)
    turn(cx - 1)


def adjoint_end_kernel(weights, u1, w2, w3, q2, c, inv, s, w1, q1, prev):
    cx, side_cells = u1.shape[0], u1.shape[1]
    g0 = spread_weight(weights, 0, CHUNK)

    def first(x):
        for row, count in chunks(side_cells):
            at = pl.ds(row, count)
            value = backward(
                layer(q2, x), w2[x, at, :], w3[x, at, :], layer(inv, x), g0 * u1[x, at, :],
                x_sides(q2, x, cx), row, count, side_cells,
            )
            w1[x, at, :] = value
            q1[x, at, :] = c[x, at, :] * value
            prev[x, at, :] = (s[x, at, :] - 1.0) * value

    first(0)
    sweep(1, cx - 1, first)
    first(cx - 1)


def patch_kernel(
    own, maps, wall_gain, wall_now, got_a, got_b, up, u, u1, u2, u3, u4, w4, w3, w2, w1, q2,
    prev, prev_ends, cur, sums, prev_hbm, cur_hbm, values, columns, totals, sems,
):
    cx, side_cells = u.shape[0], u.shape[1]
    last = side_cells - 1
    ends = [end_layer(own_parity(), side, 0, cx) for side in range(2)]
    inner = pl.ds(1, cx - 2)
    leave = [
        pltpu.make_async_copy(prev.at[inner], prev_hbm.at[inner], sems.at[0]),
        pltpu.make_async_copy(prev_ends.at[0], prev_hbm.at[ends[0]], sems.at[1]),
    ]
    for k in range(cx - 2):
        x = end_layer(own_parity(), 0, k, cx)
        leave.append(pltpu.make_async_copy(cur.at[x], cur_hbm.at[x], sems.at[2 + k]))
    for copy in leave:
        copy.start()

    def field(x, at, lanes):
        k = (x, at, lanes)
        return (
            w4[k] * (u2[k] - u4[k])
            + w3[k] * (u1[k] - u3[k])
            + (w2[k] * (u[k] - u2[k]) + w1[k] * (up[k] - u1[k]))
        )

    everything = pl.ds(0, side_cells)
    low, high = pl.ds(0, LANES), pl.ds(side_cells - LANES, LANES)
    for x in range(cx):
        values[4 * x : 4 * x + 1, :] = field(x, pl.ds(0, 8), everything)[0:1]
        values[4 * x + 1 : 4 * x + 2, :] = field(x, pl.ds(last - 7, 8), everything)[7:8]
    base = 2 * cx
    tall = 2 * CHUNK
    spot = lax.broadcasted_iota(jnp.int32, (tall, LANES), 1)

    def gather(k, carry):
        at = pl.ds(pl.multiple_of(k * tall, tall), tall)
        total = jnp.zeros((tall, LANES), F32)
        for x in range(cx):
            for j, (lanes, lane_from) in enumerate(((low, 0), (high, LANES - 1))):
                tile = to_lane(field(x, at, lanes), 2 * x + j, lane_from)
                total = jnp.where(spot == 2 * x + j, tile, total)
        for side in range(2):
            for j, (lanes, lane_from) in enumerate(((low, 0), (high, LANES - 1))):
                place = base + 2 * side + j
                total = jnp.where(
                    spot == place, to_lane(q2[ends[side], at, lanes], place, lane_from), total
                )
        columns[at, :] = total
        return carry

    lax.fori_loop(0, side_cells // tall, gather, 0)
    rows = jnp.transpose(columns[...])
    for x in range(cx):
        values[4 * x + 2 : 4 * x + 4, :] = rows[2 * x : 2 * x + 2, :]
    for side in range(2):
        at, place = base + 2 * side, 4 * (cx + side)
        theirs = jnp.concatenate(
            [q2[ends[side], 0:1, :], q2[ends[side], last : last + 1, :], rows[at : at + 2, :]], axis=0
        )
        faces = slice(4 * side, 4 * side + 4)
        prior = (got_a, got_b)[side][2 * side_cells : 2 * side_cells + 4, :]
        values[place : place + 4, :] = theirs * (wall_gain[faces, :] * (prior - wall_now[faces, :]))
    all_maps, all_values = maps[...], values[...]

    def patch(k, carry):
        for m in range(GROUP // 8):
            block = []
            for j in range(8):
                picked = fold(jnp.where(all_maps == GROUP * k + 8 * m + j, all_values, 0.0))
                half = picked[:, :LANES]
                for first in range(LANES, side_cells, LANES):
                    half = half + picked[:, first : first + LANES]
                block.append(jnp.sum(half, axis=0, keepdims=True))
            total = jnp.sum(jnp.concatenate(block, axis=0), axis=1, keepdims=True)
            totals[pl.ds(pl.multiple_of(GROUP * k + 8 * m, 8), 8), :] = jnp.broadcast_to(
                total, (8, LANES)
            )
        return carry

    totals[totals.shape[0] - LANES :, :] = jnp.zeros((LANES, LANES), F32)
    lax.fori_loop(0, (totals.shape[0] - LANES) // GROUP, patch, 0)
    tall = -(-own // 8) * 8
    sub = lax.broadcasted_iota(jnp.int32, (tall, LANES), 0)
    diagonal = sub == lax.broadcasted_iota(jnp.int32, (tall, LANES), 1)

    def owner(d, carry):
        mine = jnp.where(diagonal, totals[pl.ds(d * own, tall), :], 0.0)
        sums[pl.ds(d, 1), :] = jnp.sum(mine, axis=0, keepdims=True)
        return carry

    lax.fori_loop(0, sums.shape[0], owner, 0, unroll=8)
    for copy in leave:
        copy.wait()


def join_last(side, w1, q2, c, inv, s, got, b, cur, prev, delta):
    cx, side_cells = w1.shape[0], w1.shape[1]
    x0, x1 = (end_layer(own_parity(), side, k, cx) for k in range(2))
    for row, count in chunks(side_cells):
        at = pl.ds(row, count)
        change = inv[x0, at, :] * got[at, :]
        prev[side, at, :] = (s[x0, at, :] - 1.0) * (w1[x0, at, :] + change)
        change = c[x0, at, :] * change
        delta[at, :] = change
        cur[x1, at, :] += change
    for row, count in chunks(side_cells):
        at, below = pl.ds(row, count), pl.ds(side_cells + row, count)
        v, total = beside(flat(delta, 0), row, count, side_cells)
        cur[x0, at, :] += (
            2.0 * (inv[x0, at, :] * got[at, :])
            + (total - 6.0 * v)
            + (got[below, :] + b[at, :] * q2[x0, at, :])
        )


def join_near_kernel(w1, q2, c, inv, s, got, b, cur_in, cur, prev, delta):
    join_last(0, w1, q2, c, inv, s, got, b, cur, prev, delta)


def share_kernel(own, dealt, cur_in, cur, mine):
    mine[...] = (jnp.sum(dealt[...], axis=0) / float(PATCH_CELLS))[:own]


def join_far_kernel(
    w1, q2, c, inv, s, got, b, mine, cur_in, ends_in, cur_hbm_in, prev_hbm_in,
    cur, prev, cur_hbm, prev_hbm, mine_hbm, delta, sems,
):
    cx = w1.shape[0]
    copies = []

    def send(src, dst):
        copies.append(pltpu.make_async_copy(src, dst, sems.at[len(copies)]))
        copies[-1].start()

    send(mine, mine_hbm)
    x0, x1 = (end_layer(own_parity(), 1, k, cx) for k in range(2))
    join_last(1, w1, q2, c, inv, s, got, b, cur, prev, delta)
    send(prev.at[1], prev_hbm.at[x0])
    send(cur.at[x1], cur_hbm.at[x1])
    send(cur.at[x0], cur_hbm.at[x0])
    for copy in copies:
        copy.wait()


def call(kernel, ins, outs, scratch=(), aliases=None, name=None, us=2.0):
    kinds = {"v": in_vmem, "s": in_smem, "h": in_hbm}
    return pl.pallas_call(
        kernel,
        out_shape=[
            (pltpu.VMEM if kind == "v" else pltpu.HBM)(shape, *(dtype or [F32]))
            for kind, shape, *dtype in outs
        ],
        in_specs=[kinds[kind] for kind, _ in ins],
        out_specs=[kinds[kind] for kind, *_ in outs],
        scratch_shapes=list(scratch),
        input_output_aliases=aliases or {},
        compiler_params=pltpu.CompilerParams(vmem_limit_bytes=12 * 2**20),
        cost_estimate=pl.CostEstimate(flops=0, transcendentals=0, bytes_accessed=int(us * 3.0e6)),
        name=name,
    )(*[value for _, value in ins])


def on_device(u_prev, u_cur, courant_sq, patch_map, absorb, checkpoint, target_curve, tail_energy):
    cx, side = u_cur.shape[0], u_cur.shape[1]
    count = lax.axis_size("gx")
    patches = absorb.shape[0]
    own = patches // count
    all_cells = float(cx * count * side * side)
    field, plane = (cx, side, side), (side, side)
    double, tall = (2 * side, side), (side + 8, side)
    within = [(i, i ^ 1) for i in range(count)]
    across = [(i, i + 1) for i in range(1, count - 1, 2)]
    across = across + [(j, i) for i, j in across]

    def swap(a, b):
        a = lax.ppermute(a, "gx", within)
        return a, lax.ppermute(b, "gx", across)

    def deal(rows):
        return lax.all_to_all(rows, "gx", 0, 0, tiled=True)

    dma = pltpu.SemaphoreType.DMA
    ab = ("s", absorb)
    v = lambda *arrays: [("v", a) for a in arrays]
    small = (checkpoint.reshape(1, 1), target_curve.reshape(1, -1), tail_energy.reshape(1, 1))
    raw = [
        ("h", pltpu.with_memory_space_constraint(a, pltpu.HBM))
        for a in (patch_map, u_cur, u_prev, courant_sq)
    ]
    c_a, u_b, c_b, own_maps = call(
        start_kernel,
        [raw[0], raw[1], raw[3]],
        [("v", (2 * side + 8, side)), ("v", plane), ("v", tall), ("v", (cx, 4, side), jnp.int32)],
        [dma((5,))],
        name="edges",
        us=1.0,
    )
    near_a = lax.ppermute(c_a, "gx", within)
    near = (near_a, lax.ppermute(u_b, "gx", across))
    got_c = (near_a, lax.ppermute(c_b, "gx", across))
    u, up, c, s, inv, u1, params = call(
        ahead_one_kernel,
        [ab] + v(*small, own_maps) + raw[1:],
        [("v", field)] * 6 + [("v", (8, LANES))],
        [
            VMEM((4 * cx, side), jnp.int32),
            VMEM((4 * cx, side), F32),
            VMEM((LANES, side), F32),
            VMEM((side, LANES), F32),
            VMEM((side, LANES), F32),
            dma((3, cx)),
        ],
        name="forward_1",
        us=6.0,
    )
    edge_1 = []
    for k in range(2):
        u1, plane_1 = call(
            functools.partial(join_one_kernel, k),
            v(c, inv, near[k], u1),
            [("v", field), ("v", plane)],
            aliases={3: 0},
            name="edges_1",
            us=0.1,
        )
        edge_1.append(plane_1)
    u1h_a, u1h_b = near = swap(*edge_1)
    u2, *own_b, b_a, b_b, maps, wall_gain, wall_prior = call(
        ahead_two_kernel,
        [ab] + v(own_maps, u, up, c, inv, u1, *got_c),
        [("v", field)]
        + [("v", plane)] * 4
        + [("v", (4 * cx + 8, side), jnp.int32), ("v", (8, side)), ("v", (8, side))],
        [VMEM((side, LANES), F32), VMEM((side, LANES), F32), VMEM((LANES, side), F32)],
        name="forward_2",
        us=3.5,
    )
    got_b = (b_a, b_b)
    edge_2 = []
    for k in range(2):
        u2, pay = call(
            functools.partial(join_two_kernel, k),
            v(c, inv, own_b[k], near[k], wall_prior, u1, u2),
            [("v", field), ("v", (2 * side + 8, side))],
            aliases={6: 0},
            name="edges_2",
            us=0.4,
        )
        edge_2.append(pay)
    second = swap(*edge_2)
    u3, u4, energy, wall_now = call(
        ahead_again_kernel,
        v(u1, u2, c, inv, u1h_a, u1h_b),
        [("v", field)] * 2 + [("v", (STEPS, 8, side)), ("v", (8, side))],
        [VMEM((side, LANES), F32)],
        name="forward_3_4",
        us=5.5,
    )
    edge_4, u3h, free = [], [], []
    for k in range(2):
        u3, u4, halo, pay, energy = call(
            functools.partial(join_second_kernel, k),
            v(c, inv, energy, edge_2[k], own_b[k], second[k], got_b[k], u3, u4, *free[:1]),
            [("v", field)] * 2
            + [("v", plane), ("v", double)]
            + [("v", (count, LANES) if k else (STEPS, 8, side))],
            [VMEM(plane, F32)],
            aliases={7: 0, 8: 1},
            name="edges_3_4",
            us=0.6,
        )
        edge_4.append(pay)
        u3h.append(halo)
        free = call(
            functools.partial(adjoint_free_kernel, k),
            v(u4, c, inv, *free),
            [("v", field)] * 3,
            aliases={3: 0, 4: 1, 5: 2} if k else None,
            name="adjoint_3",
            us=1.0,
        )
    third = swap(*edge_4)
    w4, w3, _ = free
    energy, w4, w3 = lax.optimization_barrier((energy, w4, w3))
    sums = deal(energy)
    weights, w4, w3, w2, q2 = call(
        functools.partial(adjoint_kernel, all_cells),
        v(params, sums, u2, u3, c, inv, w4, w3),
        [("v", (8 * STEPS, side))] + [("v", field)] * 4,
        [VMEM(field, F32)],
        aliases={6: 1, 7: 2},
        name="adjoint_2",
        us=3.0,
    )
    w3, w2, q2, *edge_2 = call(
        join_third_kernel,
        v(weights, u1, c, inv, *u3h, *edge_4, *third, *got_b, w3, w2, q2),
        [("v", field)] * 3 + [("v", double)] * 2,
        [VMEM(plane, F32), VMEM(plane, F32)],
        aliases={12: 0, 13: 1, 14: 2},
        name="edges_adjoint_3_2",
    )
    fourth = swap(*edge_2)
    w1, q1, prev = call(
        adjoint_end_kernel,
        v(weights, u1, w2, w3, q2, c, inv, s),
        [("v", field)] * 3,
        name="adjoint_1",
    )
    (cur,) = call(result_kernel, v(w1, q1, w2, s), [("v", field)], name="adjoint_0", us=1.8)
    cur, ends = call(
        join_near_kernel,
        v(w1, q2, c, inv, s, fourth[0], got_b[0], cur),
        [("v", field), ("v", (2, side, side))],
        [VMEM(plane, F32)],
        aliases={7: 0},
        name="near_edge_0",
        us=0.4,
    )
    partial, prev_out, cur_out = call(
        functools.partial(patch_kernel, own),
        v(maps, wall_gain, wall_now, second[0], second[1], up, u, u1, u2, u3, u4, w4, w3, w2, w1, q2)
        + v(prev, ends, cur),
        [("v", (count, LANES)), ("h", field), ("h", field)],
        [
            VMEM((4 * cx + 8, side), F32),
            VMEM((side, LANES), F32),
            VMEM((-(-patches // GROUP) * GROUP + LANES, LANES), F32),
            dma((cx,)),
        ],
        name="patch_sums",
        us=2.7,
    )
    cur, mine = call(
        functools.partial(share_kernel, own),
        v(deal(partial), cur),
        [("v", field), ("v", (own,))],
        aliases={1: 0},
        name="share",
        us=0.1,
    )
    _, _, cur, prev, mine = call(
        join_far_kernel,
        v(w1, q2, c, inv, s, fourth[1], got_b[1], mine, cur, ends)
        + [("h", cur_out), ("h", prev_out)],
        [("v", field), ("v", (2, side, side)), ("h", field), ("h", field), ("h", (own,))],
        [VMEM(plane, F32), dma((4,))],
        aliases={8: 0, 9: 1, 10: 2, 11: 3},
        name="far_edge_0",
        us=1.0,
    )
    return prev, cur, mine


def solution(mesh):
    bricks = P(("groups", "gx"), None, None)
    return jax.shard_map(
        on_device,
        mesh=mesh,
        in_specs=(bricks, bricks, bricks, bricks, P("groups"), P("groups"), P("groups"), P("groups")),
        out_specs=(bricks, bricks, P(("groups", "gx"))),
        check_vma=False,
    )
```
